32 devices in a mesh: blk: 16 (over z, y, x), fld: 2 (over core).
Axes of the slice: x: 2, y: 2, z: 4, core: 2. Of those that a mesh axis runs over, the one named last changes fastest.
Arguments:
- seed_fine: float32 [8, 128, 4096], P('fld', 'blk'), may hold values from -6 to 6
- seed_coarse: float32 [8, 32, 4096], P('fld', 'blk'), may hold values from -6 to 6
- saved_fine: float32 [4, 8, 128, 4096], P(None, 'fld', 'blk'), may hold values from 0.5 to 2
- saved_coarse: float32 [2, 8, 32, 4096], P(None, 'fld', 'blk'), may hold values from 0.5 to 2
- diffusion: float32 [8], P('fld'), may hold values from 0.02 to 0.15
- species_shares: float32 [8], P('fld'), may hold values from 0.1 to 1
- fine_nbr: int32 [128, 6], P('blk'), may hold values from -1 to 127, as said below
- coarse_nbr: int32 [32, 6], P('blk'), may hold values from -1 to 31, as said below
- children: int32 [32, 8], P('blk'), may hold values from -1 to 127, as said below
- fine_counts: int32 [128], P('blk'), may hold values from 1 to 4
- coarse_counts: int32 [32], P('blk'), may hold values from 1 to 4
Outputs:
- adj_fine: float32 [8, 128, 4096], P('fld', 'blk')
- adj_coarse: float32 [8, 32, 4096], P('fld', 'blk')
The draws below stay inside these ranges and needn't reach their ends.
Inputs may be any that keep to these rules, and one draw needn't show every extreme that they name: `fine_nbr`: slot of the block beside each face (first and last along cell dimensions 0, 1, 2), -1 at a wall. The relation is symmetric with faces 2a and 2a+1 paired. Across faces 0 to 3 the neighbour is held by the same index of blk, across face 4 by the same or the one below, across face 5 by the same or the one above. `coarse_nbr`: as for the fine level: symmetric, faces 2a and 2a+1 paired; across faces 0 to 3 the same index of blk, across face 4 the same or the one below, across face 5 the same or the one above. `children`: the fine block that refines each coarse octant, or -1. Every fine block refines exactly one octant. The octants held by index i of blk that are refined are refined by blocks of the indices i + d modulo 16 for d = 0 .. 7, exactly 1 of them by the blocks of each such index.
All inputs are finite; a program needn't handle non-finite values.
Results may differ from the reference program's by a relative error of at most 0.0003.
Values sent between devices are 32-bit elements; how exact they have to be, the bound alone decides.
No kernel may reach another device: no remote copies, remote signals or barrier semaphores. Data moves between devices by JAX's collectives and lax.ppermute only.
A program may use at most 128 MiB of HBM per device.

```python
import math
import jax
import jax.numpy as jnp

NV = 8
B = 16
LX = 2
LY = 2
FZ = 2
NSUB = 4
CYCLES = 2
BF = 8
BC = 2
NF = 128
NC = 32


def lattice_neighbours(key, span_x, span_y, span_z, devices):
    per_dev = span_x * span_y * span_z
    subkeys = jax.random.split(key, devices)
    orders = jax.vmap(lambda subkey: jax.random.permutation(subkey, per_dev))(subkeys).astype(jnp.int32)
    slot_of = (jnp.arange(devices, dtype=jnp.int32)[:, None] * per_dev + orders).reshape(-1)
    logical = jnp.arange(devices * per_dev, dtype=jnp.int32)
    device_no = logical // per_dev
    local_no = logical % per_dev
    pos_x = local_no // (span_y * span_z)
    pos_y = local_no // span_z % span_y
    pos_z = device_no * span_z + local_no % span_z
    full_depth = devices * span_z
    columns = []
    for axis_no in range(3):
        for direction in (-1, 1):
            shifted = [pos_x, pos_y, pos_z]
            shifted[axis_no] = shifted[axis_no] + direction
            upper_end = (span_x, span_y, full_depth)[axis_no]
            inside = (shifted[axis_no] >= 0) & (shifted[axis_no] < upper_end)
            target = shifted[2] // span_z * per_dev + (shifted[0] * span_y + shifted[1]) * span_z + shifted[2] % span_z
            target = jnp.clip(target, 0, devices * per_dev - 1)
            columns.append(jnp.where(inside, slot_of[target], -1))
    neighbour_table = jnp.stack(columns, axis=1).astype(jnp.int32)
    return jnp.zeros((devices * per_dev, 6), jnp.int32).at[slot_of].set(neighbour_table)


def draw_fine_nbr(key, part):
    return lattice_neighbours(jax.random.fold_in(key, 11), LX, LY, FZ, NF // BF)


def draw_coarse_nbr(key, part):
    return lattice_neighbours(jax.random.fold_in(key, 23), LX // 2, LY, FZ // 2, NC // BC)


def draw_children(key, part):
    devices = NF // BF
    links = min(BF, devices)
    per_link = BF // links
    octant_count = 8 * BC
    subkeys = jax.random.split(jax.random.fold_in(key, 37), 2)
    fine_orders = jax.vmap(lambda subkey: jax.random.permutation(subkey, BF))(jax.random.split(subkeys[0], devices)).astype(jnp.int32)
    coarse_orders = jax.vmap(lambda subkey: jax.random.permutation(subkey, octant_count))(jax.random.split(subkeys[1], devices)).astype(jnp.int32)
    holder = jnp.arange(devices, dtype=jnp.int32)[:, None, None]
    link_no = jnp.arange(links, dtype=jnp.int32)[None, :, None]
    member = jnp.arange(per_link, dtype=jnp.int32)[None, None, :]
    position = link_no * per_link + member
    source = (holder + link_no) % devices
    fine_ids = source * BF + fine_orders[source, position]
    octant_ids = holder * octant_count + coarse_orders[holder, position]
    fine_ids = jnp.broadcast_to(fine_ids, (devices, links, per_link)).reshape(-1)
    octant_ids = jnp.broadcast_to(octant_ids, (devices, links, per_link)).reshape(-1)
    flat_child = jnp.full((devices * octant_count,), -1, jnp.int32).at[octant_ids].set(fine_ids.astype(jnp.int32))
    return flat_child.reshape(NC, 8)


def touch_ends(array, key, smallest, high):
    shape = array.shape
    spot = [jax.random.randint(jax.random.fold_in(key, axis), (), 0, shape[axis]) for axis in range(len(shape))]
    array = array.at[tuple(spot)].set(smallest)
    longest = shape.index(max(shape))
    spot[longest] = (spot[longest] + 1) % shape[longest]
    return array.at[tuple(spot)].set(high)


def levels(stream_key, shape, pieces, low, top_value):
    def one(dim, parts):
        steps = jax.random.uniform(jax.random.fold_in(jax.random.fold_in(stream_key, 6), dim), (parts,), jnp.float32, low / len(pieces), top_value / len(pieces))
        return jnp.repeat(jnp.exp(steps), shape[dim] // parts).reshape((-1,) + (1,) * (len(shape) - dim - 1))

    factor_of = one(*pieces[0])
    for cut in pieces[1:]:
        factor_of = factor_of * one(*cut)
    return factor_of


def normal_values(stream_key, extent, scale, bound, shards=(), kind=jnp.bfloat16):
    entries = jax.random.normal(stream_key, extent, jnp.float32) * scale
    if len(shards) > 0:
        entries = levels(stream_key, extent, shards, -0.22, 0.18) * entries
    return jnp.clip(entries, min=-bound, max=bound).astype(kind)


def setup_inputs(seed: int = 0) -> dict:
    key_of = jax.random.split(jax.random.key(seed), 12)
    seed_fine = normal_values(key_of[0], (NV, NF, B**3), 1.0, 6.0, ((0, 2), (1, 16)), jnp.float32)
    seed_coarse = normal_values(key_of[1], (NV, NC, B**3), 1.0, 6.0, ((0, 2), (1, 16)), jnp.float32)
    saved_fine = jnp.clip(0.5 + 1.5 * jax.random.uniform(key_of[2], (2 * CYCLES, NV, NF, B**3), jnp.float32) ** levels(key_of[2], (2 * CYCLES, NV, NF, B**3), ((1, 2), (2, 16)), -0.2, 0.2), 0.5, 2.0)
    saved_coarse = jnp.clip(0.5 + 1.5 * jax.random.uniform(key_of[3], (CYCLES, NV, NC, B**3), jnp.float32) ** levels(key_of[3], (CYCLES, NV, NC, B**3), ((1, 2), (2, 16)), -0.2, 0.2), 0.5, 2.0)
    diffusion = jnp.clip(jnp.exp(math.log(0.15) - 2.014903 * jax.random.uniform(key_of[4], (NV,), jnp.float32) ** levels(key_of[4], (NV,), ((0, 2),), -0.2, 0.2)), 0.02, 0.15)
    species_shares = jnp.clip(jnp.exp(math.log(1.0) - 2.3025851 * jax.random.uniform(key_of[5], (NV,), jnp.float32) ** levels(key_of[5], (NV,), ((0, 2),), -0.2, 0.2)), 0.1, 1.0)
    fine_nbr = draw_fine_nbr(jax.random.fold_in(key_of[11], 71), 0)
    coarse_nbr = draw_coarse_nbr(jax.random.fold_in(key_of[11], 71), 0)
    children = draw_children(jax.random.fold_in(key_of[11], 71), 0)
    fine_counts = touch_ends(jax.random.randint(key_of[9], (NF,), 1, NSUB + 1), jax.random.fold_in(key_of[9], 1), 1, NSUB).astype(jnp.int32)
    coarse_counts = touch_ends(jax.random.randint(key_of[10], (NC,), 1, NSUB + 1), jax.random.fold_in(key_of[10], 1), 1, NSUB).astype(jnp.int32)
    return dict(seed_fine=seed_fine, seed_coarse=seed_coarse, saved_fine=saved_fine, saved_coarse=saved_coarse, diffusion=diffusion, species_shares=species_shares, fine_nbr=fine_nbr, coarse_nbr=coarse_nbr, children=children, fine_counts=fine_counts, coarse_counts=coarse_counts)


heat_gain = 0.5
energy = 2.0


def face_list(field):
    return [field[:, :, 0], field[:, :, -1], field[:, :, :, 0], field[:, :, :, -1], field[:, :, :, :, 0], field[:, :, :, :, -1]]


def with_ghosts(field, ghosts):
    running = -6.0 * field
    running = running + jnp.concatenate([ghosts[0][:, :, None], field[:, :, :-1]], axis=2)
    running = running + jnp.concatenate([field[:, :, 1:], ghosts[1][:, :, None]], axis=2)
    running = running + jnp.concatenate([ghosts[2][:, :, :, None], field[:, :, :, :-1]], axis=3)
    running = running + jnp.concatenate([field[:, :, :, 1:], ghosts[3][:, :, :, None]], axis=3)
    running = running + jnp.concatenate([ghosts[4][..., None], field[..., :-1]], axis=4)
    running = running + jnp.concatenate([field[..., 1:], ghosts[5][..., None]], axis=4)
    return running


def laplace(field, neighbours):
    faces = face_list(field)
    ghosts = []
    for face_no in range(6):
        target = neighbours[:, face_no]
        chosen = faces[face_no ^ 1][:, jnp.maximum(target, 0)]
        ghosts.append(jnp.where((target >= 0)[None, :, None, None], chosen, jnp.zeros_like(chosen)))
    return with_ghosts(field, ghosts)


def diffuse_adjoint(costate_values, neighbours, rates):
    first = rates * laplace(costate_values, neighbours)
    second = rates * laplace(first, neighbours)
    return costate_values + first + 0.5 * second


def exothermic_sources(thermal_costate, thermal_profile, tally_grid, blend_aggregate):
    substep = 1.0 / tally_grid.astype(jnp.float32)[:, None]
    history = []
    present_refinement = thermal_profile
    for counter in range(NSUB):
        history.append(present_refinement)
        active = (counter < tally_grid)[:, None]
        present_refinement = present_refinement + jnp.where(active, substep * heat_gain * blend_aggregate * jnp.exp(-energy / present_refinement), 0.0)
    remainder_passed = thermal_costate
    scaling_coefficient = jnp.zeros_like(thermal_costate)
    for counter in reversed(range(NSUB)):
        earlier = history[counter]
        active = (counter < tally_grid)[:, None]
        decay = jnp.exp(-energy / earlier)
        scaling_coefficient = scaling_coefficient + jnp.where(active, substep * heat_gain * decay * remainder_passed, 0.0)
        remainder_passed = jnp.where(active, remainder_passed * (1.0 + substep * heat_gain * blend_aggregate * energy * decay / (earlier * earlier)), remainder_passed)
    return remainder_passed, scaling_coefficient


def reaction_adjoint(costate_values, saved, tally_grid, species_shares):
    blend_aggregate = jnp.sum(species_shares[:, None, None] * saved, axis=0)
    remainder_passed, scaling_coefficient = exothermic_sources(costate_values[0], saved[0], tally_grid, blend_aggregate)
    costate_values = jnp.concatenate([remainder_passed[None], costate_values[1:]], axis=0)
    return costate_values + species_shares[:, None, None] * scaling_coefficient[None]


def restrict_adjoint(fine_adj, coarse_adj, children):
    fields = fine_adj.shape[0]
    count_c = coarse_adj.shape[1]
    half_edge = B // 2
    octants = coarse_adj.reshape(fields, count_c, 2, half_edge, 2, half_edge, 2, half_edge)
    octants = octants.transpose(0, 1, 2, 4, 6, 3, 5, 7).reshape(fields, count_c * 8, half_edge, half_edge, half_edge)
    flat_child = children.reshape(-1)
    refined = jnp.nonzero(flat_child >= 0, size=NF)[0].astype(jnp.int32)
    fine_ids = flat_child[refined].astype(jnp.int32)
    portion = octants[:, refined] * 0.125
    portion = jnp.repeat(jnp.repeat(jnp.repeat(portion, 2, axis=2), 2, axis=3), 2, axis=4)
    fine_adj = fine_adj.at[:, fine_ids].add(portion)
    keeping = (flat_child < 0).astype(coarse_adj.dtype).reshape(count_c, 2, 2, 2)
    shaped = coarse_adj.reshape(fields, count_c, 2, half_edge, 2, half_edge, 2, half_edge)
    coarse_adj = (shaped * keeping[None, :, :, None, :, None, :, None]).reshape(coarse_adj.shape)
    return fine_adj, coarse_adj


def reference(seed_fine, seed_coarse, saved_fine, saved_coarse, diffusion, species_shares, fine_nbr, coarse_nbr, children, fine_counts, coarse_counts):
    cell_count = B ** 3
    fine_adj = seed_fine.reshape(NV, NF, B, B, B)
    coarse_adj = seed_coarse.reshape(NV, NC, B, B, B)
    fine_rates = diffusion.reshape(NV, 1, 1, 1, 1)
    coarse_rates = 0.5 * fine_rates
    for sweep_no in reversed(range(CYCLES)):
        fine_adj, coarse_adj = restrict_adjoint(fine_adj, coarse_adj, children)
        for stepno in (2 * sweep_no + 1, 2 * sweep_no):
            flat_fine = reaction_adjoint(fine_adj.reshape(NV, NF, cell_count), saved_fine[stepno], fine_counts, species_shares)
            fine_adj = diffuse_adjoint(flat_fine.reshape(NV, NF, B, B, B), fine_nbr, fine_rates)
        flat_coarse = reaction_adjoint(coarse_adj.reshape(NV, NC, cell_count), saved_coarse[sweep_no], coarse_counts, species_shares)
        coarse_adj = diffuse_adjoint(flat_coarse.reshape(NV, NC, B, B, B), coarse_nbr, coarse_rates)
    return fine_adj.reshape(NV, NF, cell_count), coarse_adj.reshape(NV, NC, cell_count)
```

```python
import functools
import jax
import jax.numpy as jnp
from jax import lax
from jax.experimental import pallas as pl
from jax.experimental.pallas import tpu as pltpu
from jax.sharding import PartitionSpec as P

B = 16
H = B // 2
NSUB = 4
CYCLES = 2
LANES = 128
TILES = B**3 // LANES
HEAT = 0.5
ENERGY = 2.0
FAR = -(1 << 20)
VMEM = pl.BlockSpec(memory_space=pltpu.VMEM)
SMEM = pl.BlockSpec(memory_space=pltpu.SMEM)
F32 = jnp.float32


def core_swap(value):
    return lax.ppermute(value, "fld", [(0, 1), (1, 0)])


def pair_swap(value, first):
    n = lax.axis_size("blk")
    pairs = []
    for i in range(first, n + first, 2):
        a, b = i % n, (i + 1) % n
        pairs += [(a, b), (b, a)]
    return lax.ppermute(value, "blk", sorted(pairs))


def octant_sends(count):
    half = count // 2
    return [(1 + s if 1 + s < half else count - 1, half + s) for s in range(half)]


def octant_move(value, distances):
    n = lax.axis_size("blk")
    pairs = []
    for i in range(n):
        for core in range(2):
            pairs.append((2 * i + core, 2 * ((i + distances[core]) % n) + core))
    return lax.ppermute(value, ("blk", "fld"), pairs)


def lane_ids():
    return lax.broadcasted_iota(jnp.int32, (8, LANES), 1)


def row_ids():
    return lax.broadcasted_iota(jnp.int32, (8, LANES), 0)


def roll(x, steps):
    steps = steps % LANES
    return x if steps == 0 else pltpu.roll(x, steps, 1)


def odd_lanes():
    return lane_ids() % 2 == 1


def cols(i, jh, width=1):
    return pl.ds((2 * i + jh) * LANES, width * LANES)


class Links:
    def __init__(self, column, base, count, by_rows, remote_base=None):
        self.count = count
        self.by_rows = by_rows
        self.column = column
        self.base = base
        self.cache = {}

    def place(self, slab, face, base):
        raw = jnp.broadcast_to(self.column(slab, face), (8, LANES))
        return jnp.where(raw >= 0, raw - base, FAR)

    def prepare(self, name, slab, make):
        key = (name, None if self.by_rows else slab)
        if key not in self.cache:
            self.cache[key] = make(slab)
        return self.cache[key]

    def index(self, name, slab):
        base, count = self.base, self.count

        def one(face, shift=0):
            return lambda s: self.place(s, face, base + shift)

        lane = lane_ids()
        if name == "i0":
            return self.prepare(name, slab, one(0))
        if name == "i1":
            return self.prepare(name, slab, one(1))
        if name == "j":
            return self.prepare(
                name, slab, lambda s: jnp.where(lane < LANES // 2, one(2)(s), one(3)(s))
            )
        if name == "k":
            return self.prepare(name, slab, lambda s: jnp.where(odd_lanes(), one(4)(s), one(5)(s)))
        if name == "k_far":
            return self.prepare(
                name,
                slab,
                lambda s: jnp.where(odd_lanes(), one(4, -count)(s), one(5, count)(s)),
            )
        if name == "from_below":
            return self.prepare(name, slab, one(5, count))
        return self.prepare(name, slab, one(4, -count))

    def read(self, name, slab, tile):
        where = self.index(name, slab)
        if self.by_rows:
            there = (where >= 0) & (where < self.count)
            got = jnp.take_along_axis(
                tile(slab), jnp.clip(where, 0, self.count - 1), axis=0, mode="promise_in_bounds"
            )
            return jnp.where(there, got, 0.0)
        result = jnp.zeros((8, LANES), F32)
        for q in range(self.count):
            result = jnp.where(where == q, tile(q), result)
        return result


def in_plane(links, slab, c, tile, h_or_i):
    lane = lane_ids()
    low = [roll(c[0], B), roll(c[1], B)]
    high = [roll(c[0], -B), roll(c[1], -B)]
    edge = links.read(
        "j",
        slab,
        lambda q: jnp.where(
            lane < LANES // 2, roll(tile(q, h_or_i, 1), B), roll(tile(q, h_or_i, 0), -B)
        ),
    )
    first = jnp.where(lane < B, edge, low[0]) + jnp.where(lane >= LANES - B, high[1], high[0])
    second = jnp.where(lane < B, low[0], low[1]) + jnp.where(lane >= LANES - B, edge, high[1])
    return first, second


def laplace_slab(links, slab, tile, ghost, emit):
    lane = lane_ids()
    k = lane % B
    for h in range(2):
        packed = [ghost(h, 0), ghost(h, 1)]
        for q in range(H):
            i = h * H + q
            c = [tile(slab, i, 0), tile(slab, i, 1)]
            plane = in_plane(links, slab, c, tile, i)
            for jh in range(2):
                if i > 0:
                    before = tile(slab, i - 1, jh)
                else:
                    before = links.read("i0", slab, lambda s, jh=jh: tile(s, B - 1, jh))
                if i < B - 1:
                    after = tile(slab, i + 1, jh)
                else:
                    after = links.read("i1", slab, lambda s, jh=jh: tile(s, 0, jh))
                edge = roll(packed[jh], -(2 * q + 1))
                line = jnp.where(k == 0, edge, roll(c[jh], 1)) + jnp.where(
                    k == B - 1, edge, roll(c[jh], -1)
                )
                lap = (before + after) + (plane[jh] + line) - 6.0 * c[jh]
                emit(i, jh, c[jh], lap)


def laplace_far(links, slab, tile, inward, outward, emit):
    k = lane_ids() % B
    for h in range(2):
        c = [tile(slab, h, 0), tile(slab, h, 1)]
        plane = in_plane(links, slab, c, tile, h)
        for jh in range(2):
            if h == 1:
                head = roll(tile(slab, 0, jh), 2 - B)
                tail = links.read("i1", slab, lambda s, jh=jh: roll(tile(s, 0, jh), B - 2))
            else:
                head = links.read("i0", slab, lambda s, jh=jh: roll(tile(s, 1, jh), 2 - B))
                tail = roll(tile(slab, 1, jh), B - 2)
            before = jnp.where(k < 2, head, roll(c[jh], 2))
            after = jnp.where(k >= B - 2, tail, roll(c[jh], -2))
            lap = (before + after) + plane[jh] + inward(c[jh]) + outward(h, jh) - 6.0 * c[jh]
            emit(h, jh, lap)


def pack_into(store, q, value, shift):
    k = lane_ids() % B
    return jnp.where(k // 2 == q, roll(value, shift), store)


def zero_tile():
    return jnp.zeros((8, LANES), F32)


def diffuse(links, far_links, slabs, loop, tile, rate, up, down, far_up, far_down, work, finish):
    first_ref, edge_ref, below_ref, above_ref = work
    odd = odd_lanes()
    k = lane_ids() % B
    from_below, from_above = far_links

    def first_of(s):
        def ghost(h, jh):
            near = links.read(
                "k", s, lambda q: jnp.where(odd, up(q, h, jh), roll(down(q, h, jh), B))
            )
            far = links.read(
                "k_far", s, lambda q: jnp.where(odd, far_up(q, h, jh), roll(far_down(q, h, jh), B))
            )
            return near + far

        edges = [zero_tile(), zero_tile()]

        def emit(i, jh, c, lap):
            value = rate(s) * lap
            first_ref[s, :, cols(i, jh)] = value
            q = i % H
            edges[jh] = pack_into(zero_tile() if q == 0 else edges[jh], q, value, 2 * q + 1)
            if q == H - 1:
                edge_ref[s, i // H, jh] = edges[jh]

        laplace_slab(links, s, tile, ghost, emit)

        def emit_below(h, jh, lap):
            below_ref[s, h, jh] = rate(s) * lap

        def emit_above(h, jh, lap):
            above_ref[s, h, jh] = rate(s) * lap

        laplace_far(
            from_below,
            s,
            far_up,
            lambda c: roll(c, 1),
            lambda h, jh: from_below.read("from_below", s, lambda q: roll(down(q, h, jh), 1)),
            emit_below,
        )
        laplace_far(
            from_above,
            s,
            far_down,
            lambda c: roll(c, -1),
            lambda h, jh: from_above.read("from_above", s, lambda q: roll(up(q, h, jh), -1)),
            emit_above,
        )

    def second_of(s):
        def ghost(h, jh):
            near = links.read(
                "k",
                s,
                lambda q: jnp.where(
                    odd, roll(edge_ref[q, h, jh], 1 - B), roll(edge_ref[q, h, jh], B - 1)
                ),
            )
            far = links.read(
                "k_far",
                s,
                lambda q: jnp.where(odd, below_ref[q, h, jh], roll(above_ref[q, h, jh], B)),
            )
            return near + far

        def emit(i, jh, c, lap):
            finish(s, i, jh, tile(s, i, jh) + c + 0.5 * rate(s) * lap)

        laplace_slab(
            links, s, lambda q, i, jh: first_ref[q, :, cols(i, jh)], ghost, emit
        )

    if loop:
        def body(s, carry):
            first_of(s)
            second_of(s)
            return carry

        lax.fori_loop(0, slabs, body, 0)
    else:
        for s in range(slabs):
            first_of(s)
        for s in range(slabs):
            second_of(s)


def pick(core, a, b):
    return jnp.where(core == 0, a, b)


def spread_vector(core, own, other, row, fields):
    rows = row_ids()
    result = jnp.zeros((8, LANES), F32)
    for f in range(2 * fields):
        value = pick(core, own[row, f], other[row, f]) if f < fields else pick(
            core, other[row, f - fields], own[row, f - fields]
        )
        result = jnp.where(rows == f, value, result)
    return result


def mix_kernel(saved_f, saved_c, seed_f, par, pay, payc):
    steps, fields = saved_f.shape[0], saved_f.shape[1]
    cycles, blocks = saved_c.shape[0], saved_c.shape[2]
    for s in range(steps):
        total = par[1, 0] * saved_f[s, 0]
        for v in range(1, fields):
            total = total + par[1, v] * saved_f[s, v]
        pay[s] = total
        pay[steps + s] = saved_f[s, 0]
    pay[2 * steps] = seed_f[0]
    for c in range(cycles):
        total = par[1, 0] * saved_c[c, 0]
        for v in range(1, fields):
            total = total + par[1, v] * saved_c[c, v]
        payc[0, pl.ds(c * blocks, blocks), :] = total
        payc[1, pl.ds(c * blocks, blocks), :] = saved_c[c, 0]


def reaction_tables(mix, start, counts):
    step = HEAT / counts.astype(F32)
    state = start
    history = []
    for n in range(NSUB):
        inverse = 1.0 / state
        decay = jnp.exp(-ENERGY * inverse)
        active = n < counts
        history.append((active, inverse, decay))
        state = state + jnp.where(active, step * mix * decay, 0.0)
    passed = jnp.ones_like(start)
    weight = jnp.zeros_like(start)
    for active, inverse, decay in reversed(history):
        grown = jnp.where(active, step * decay, 0.0)
        weight = weight + grown * passed
        passed = passed * (1.0 + grown * mix * ENERGY * (inverse * inverse))
    return passed - 1.0, weight


def chem_kernel(pay, pay_o, payc, payc_o, fine_counts, coarse_counts, gain, weight, gain_c, weight_c):
    core = lax.axis_index("fld")
    steps = gain.shape[0]
    rows = row_ids()
    counts = jnp.ones((8, LANES), jnp.int32)
    for b in range(fine_counts.shape[0]):
        counts = jnp.where(rows == b, fine_counts[b], counts)
    blocks = coarse_counts.shape[0]
    entries = gain_c.shape[0]
    counts_c = jnp.ones((entries, LANES), jnp.int32)
    rows_c = lax.broadcasted_iota(jnp.int32, (entries, LANES), 0)
    for r in range(entries):
        counts_c = jnp.where(rows_c == r, coarse_counts[r % blocks], counts_c)

    def body(t, carry):
        at = pl.ds(pl.multiple_of(t * LANES, LANES), LANES)
        for s in range(steps):
            start = pick(core, pay[steps + s, :, at], pay_o[steps + s, :, at])
            a, w = reaction_tables(pay[s, :, at] + pay_o[s, :, at], start, counts)
            gain[s, :, at] = a
            weight[s, :, at] = w
        start = pick(core, payc[1, :, at], payc_o[1, :, at])
        a, w = reaction_tables(payc[0, :, at] + payc_o[0, :, at], start, counts_c)
        gain_c[:, at] = a
        weight_c[:, at] = w
        return carry

    lax.fori_loop(0, TILES, body, 0)


def octants_out(read, children, count_f, outs, cells):
    core = lax.axis_index("fld")
    me = lax.axis_index("blk")
    devices = lax.axis_size("blk")
    count_c = children.shape[0]
    fields = 8
    for p in range(count_c):
        for i in range(B):
            for jh in range(2):
                cells[p, jh, pl.ds(i, fields, stride=B), :] = read(p, i, jh)
    half = lane_ids() % B // H
    found = []
    for p in range(count_c):
        for o in range(8):
            child = children[p, o]
            distance = jnp.where(child >= 0, (child // count_f - me) % devices, -1)
            found.append((distance, child, p, o))
    sends = octant_sends(count_f)
    for s, out in enumerate(outs):
        if s < len(sends):
            want = jnp.where(core == 0, sends[s][0], sends[s][1])
        else:
            want = 0
        slot = jnp.int32(0)
        label = jnp.int32(-1)
        for distance, child, p, o in found:
            hit = distance == want
            slot = jnp.where(hit, p * 8 + o, slot)
            label = jnp.where(hit, child % count_f, label)
        if s < len(sends):
            label = jnp.where((core == 0) & (sends[s][0] == count_f - 1), -1, label)
        else:
            label = jnp.where(core == 0, label, -1)
        p, a, b, c = slot // 8, slot // 4 % 2, slot // 2 % 2, slot % 2
        kept = half == c
        for f in range(fields):
            from_row = pl.multiple_of(f * B + a * H, H)
            out[f] = jnp.where(kept, cells[p, b, pl.ds(from_row, H), :], 0.0)
        out[fields] = jnp.full((H, LANES), label.astype(F32))


def kept_octants(children, p):
    half = lane_ids() % B // H
    result = {}
    for a in range(2):
        for b in range(2):
            low = jnp.where(children[p, 4 * a + 2 * b] < 0, 1.0, 0.0)
            high = jnp.where(children[p, 4 * a + 2 * b + 1] < 0, 1.0, 0.0)
            result[a, b] = jnp.where(half == 0, low, high)
    return result


def seed_kernel(seed_c, seed_o, children, count_f, coarse, *rest):
    outs, cells = rest[:-1], rest[-1]
    core = lax.axis_index("fld")
    fields, count_c = seed_c.shape[0], seed_c.shape[1]
    for p in range(count_c):
        for v in range(fields):
            own = seed_c[v, pl.ds(p, 1), :]
            other = seed_o[v, pl.ds(p, 1), :]
            coarse[p, pl.ds(v, 1), :] = pick(core, own, other)
            coarse[p, pl.ds(fields + v, 1), :] = pick(core, other, own)
    octants_out(lambda p, i, jh: coarse[p, :, cols(i, jh)], children, count_f, outs, cells)
    for p in range(count_c):
        kept = kept_octants(children, p)
        for i in range(B):
            for jh in range(2):
                coarse[p, :, cols(i, jh)] = coarse[p, :, cols(i, jh)] * kept[i // H, jh]


def add_octants(messages, state, stage, fields):
    core = lax.axis_index("fld")
    slots = state.shape[0]
    rows = row_ids()
    lane = lane_ids()
    source = jnp.zeros((8, LANES), jnp.int32)
    order = jnp.full((8, LANES), 0, jnp.int32)
    serial = 0
    for d, message in enumerate(messages):
        label = message[2 * fields].astype(jnp.int32)
        source = jnp.where(label == rows, d, source)
        for s in range(slots):
            if s == fields:
                value = message[0]
            else:
                value = message[pl.ds(core * fields + s, 1)][0]
            stage[d // 8, s, pl.ds(d % 8, H, stride=8), :] = value
    lanes_of = [((H // 2 * jh + lane // B // 2) * B + lane % B // 2) for jh in range(2)]
    groups = (len(messages) + 7) // 8
    for s in range(slots):
        for i in range(H):
            got = None
            for g in range(groups):
                index = source - 8 * g
                part = jnp.take_along_axis(
                    stage[g, s, pl.ds(8 * i, 8), :],
                    jnp.clip(index, 0, 7),
                    axis=0,
                    mode="promise_in_bounds",
                )
                part = jnp.where((index >= 0) & (index < 8), part, 0.0)
                got = part if got is None else got + part
            got = 0.125 * (got + roll(got, -H))
            for jh in range(2):
                wide = jnp.take_along_axis(got, lanes_of[jh], axis=1, mode="promise_in_bounds")
                for ii in range(2):
                    at = cols(2 * i + ii, jh)
                    state[s, :, at] = state[s, :, at] + wide


def react_and_pack(state, fields, par, par_o, gain, weight, up, down):
    core = lax.axis_index("fld")
    share = [par[1, s] for s in range(fields)] + [pick(core, par[1, 0], par_o[1, 0])]
    extra = jnp.where(core == 0, 1.0, 0.0)
    for h in range(2):
        for jh in range(2):
            ups = [zero_tile() for _ in range(fields + 1)]
            downs = [zero_tile() for _ in range(fields + 1)]
            for q in range(H):
                at = cols(h * H + q, jh)
                driver = state[fields, :, at]
                heat = weight[:, at] * driver
                grown = gain[:, at] * driver
                for s in range(fields + 1):
                    value = state[s, :, at] + share[s] * heat
                    if s == 0:
                        value = value + extra * grown
                    if s == fields:
                        value = value + grown
                    state[s, :, at] = value
                    ups[s] = pack_into(ups[s], q, value, 2 * q + 2 - B)
                    downs[s] = pack_into(downs[s], q, value, 2 * q)
            for s in range(fields + 1):
                up(s, h, jh, ups[s])
                down(s, h, jh, downs[s])


def react_coarse_and_pack(state, shares, gain, weight, first_row, up, down):
    rows = row_ids()
    own = jnp.where(rows == 0, 1.0, 0.0)
    for p in range(state.shape[0]):
        for h in range(2):
            for jh in range(2):
                ups, downs = zero_tile(), zero_tile()
                for q in range(H):
                    at = cols(h * H + q, jh)
                    driver = jnp.broadcast_to(state[p, pl.ds(0, 1), at], (8, LANES))
                    heat = weight[pl.ds(first_row + p, 1), at] * driver
                    grown = gain[pl.ds(first_row + p, 1), at] * driver
                    value = state[p, :, at] + shares * heat + own * grown
                    state[p, :, at] = value
                    ups = pack_into(ups, q, value, 2 * q + 2 - B)
                    downs = pack_into(downs, q, value, 2 * q)
                up(p, h, jh, ups)
                down(p, h, jh, downs)


def step_kernel(plan, names, *refs):
    r = dict(zip(names, refs))
    core = lax.axis_index("fld")
    me = lax.axis_index("blk")
    even = me % 2 == 0
    fields = plan["fields"]
    slots = fields + 1
    count_f, count_c = plan["count_f"], plan["count_c"]
    par, par_o = r["par"], r["par_o"]
    coarse_slabs = count_c
    tables_at = 4 * (slots + coarse_slabs)

    def fine_at(s, h, jh):
        return 4 * s + 2 * h + jh

    def coarse_at(p, h, jh):
        return 4 * (slots + p) + 2 * h + jh

    far_b, far_a, own_up, own_down = (r.get(x) for x in ("far_b", "far_a", "own_up", "own_down"))

    if plan["diffuse_fine"]:

        @pl.when(even)
        def _():
            own_up[...] = r["sent_e"][...]
            own_down[...] = r["sent_o"][...]
            far_a[...] = r["got_e"][...]
            far_b[...] = r["got_o"][...]

        @pl.when(jnp.logical_not(even))
        def _():
            own_up[...] = r["sent_o"][...]
            own_down[...] = r["sent_e"][...]
            far_b[...] = r["got_e"][...]
            far_a[...] = r["got_o"][...]

        work = (r["first"], r["edge"], r["below"], r["above"])
        base = me * count_f
        base_c = me * count_c

        def table(ref, offset, rowwise):
            def column(slab, face):
                if rowwise:
                    return ref[tables_at, :, pl.ds(face, 1)].astype(jnp.int32)
                return ref[tables_at, pl.ds(slab, 1), pl.ds(offset + face, 1)].astype(jnp.int32)

            return column

        near = Links(table(own_up, 0, True), base, count_f, True)
        below = Links(table(far_b, 0, True), base - count_f, count_f, True)
        above = Links(table(far_a, 0, True), base + count_f, count_f, True)
        for links, names_used in (
            (near, ("i0", "i1", "j", "k", "k_far")),
            (below, ("i0", "i1", "j", "from_below")),
            (above, ("i0", "i1", "j", "from_above")),
        ):
            for name in names_used:
                links.index(name, 0)

        rate_of = [par[0, s] for s in range(fields)] + [pick(core, par[0, 0], par_o[0, 0])]

        def rate(s):
            value = rate_of[0]
            for n in range(1, slots):
                value = jnp.where(s == n, rate_of[n], value)
            return value

        done = r["fine_out"]

        def finish(s, i, jh, value):
            done[s, :, cols(i, jh)] = value

        diffuse(
            near,
            (below, above),
            done.shape[0],
            True,
            lambda s, i, jh: r["fine"][s, :, cols(i, jh)],
            rate,
            lambda s, h, jh: own_up[fine_at(s, h, jh)],
            lambda s, h, jh: own_down[fine_at(s, h, jh)],
            lambda s, h, jh: far_b[fine_at(s, h, jh)],
            lambda s, h, jh: far_a[fine_at(s, h, jh)],
            work,
            finish,
        )
        if plan["diffuse_coarse"]:
            near = Links(table(own_up, 8, False), base_c, count_c, False)
            below = Links(table(far_b, 8, False), base_c - count_c, count_c, False)
            above = Links(table(far_a, 8, False), base_c + count_c, count_c, False)
            rates = 0.5 * spread_vector(core, par, par_o, 0, fields)
            grown = r["coarse_out"] if plan["diffuse_coarse"] == "keep" else r["coarse_next"]

            def finish_c(p, i, jh, value):
                grown[p, :, cols(i, jh)] = value

            diffuse(
                near,
                (below, above),
                count_c,
                False,
                lambda p, i, jh: r["coarse"][p, :, cols(i, jh)],
                lambda p: rates,
                lambda p, h, jh: own_up[coarse_at(p, h, jh)],
                lambda p, h, jh: own_down[coarse_at(p, h, jh)],
                lambda p, h, jh: far_b[coarse_at(p, h, jh)],
                lambda p, h, jh: far_a[coarse_at(p, h, jh)],
                work,
                finish_c,
            )
            if plan["diffuse_coarse"] == "last":
                out = r["coarse_final"]
                for p in range(count_c):
                    for v in range(fields):
                        out[v, pl.ds(p, 1), :] = pick(
                            core,
                            grown[p, pl.ds(v, 1), :],
                            grown[p, pl.ds(fields + v, 1), :],
                        )
            else:
                octants_out(
                    lambda p, i, jh: grown[p, :, cols(i, jh)],
                    r["children"],
                    count_f,
                    [r[f"octant{s}"] for s in range(plan["messages"])],
                    r["cells"],
                )
                for p in range(count_c):
                    kept = kept_octants(r["children"], p)
                    for i in range(B):
                        for jh in range(2):
                            at = cols(i, jh)
                            grown[p, :, at] = grown[p, :, at] * kept[i // H, jh]
    else:
        done = r["fine_out"]
        for s in range(fields):
            done[s] = r["seed_f"][s]
        done[fields] = pick(core, r["pay"][r["pay"].shape[0] - 1], r["pay_o"][r["pay"].shape[0] - 1])
        grown = r["coarse_out"]
        grown[...] = r["coarse"][...]
        rows = row_ids()
        lane = lane_ids()
        faces = jnp.zeros((8, LANES), F32)
        for f in range(6):
            column = r["fine_nbr"][:, pl.ds(f, 1)].astype(F32)
            faces = jnp.where(lane == f, jnp.broadcast_to(column, (8, LANES)), faces)
            for p in range(count_c):
                column = r["coarse_nbr"][pl.ds(p, 1), pl.ds(f, 1)].astype(F32)
                faces = jnp.where(
                    (lane == 8 + f) & (rows == p), jnp.broadcast_to(column, (8, LANES)), faces
                )

    if plan["add"]:
        add_octants([r[f"arrived{s}"] for s in range(plan["arrivals"])], done, r["stage"], fields)
    if plan["react"]:
        up, down = r["up"], r["down"]

        def put(ref, place):
            def go(s, h, jh, value):
                ref[place(s, h, jh)] = value

            return go

        react_and_pack(
            done, fields, par, par_o, r["gain"].at[plan["step"]], r["weight"].at[plan["step"]],
            put(up, fine_at), put(down, fine_at),
        )
        if plan["react_coarse"] is not None:
            react_coarse_and_pack(
                grown,
                spread_vector(core, par, par_o, 1, fields),
                r["gain_c"],
                r["weight_c"],
                plan["react_coarse"] * count_c,
                put(up, coarse_at),
                put(down, coarse_at),
            )
        else:
            for n in range(4 * slots, tables_at):
                up[n] = zero_tile()
                down[n] = zero_tile()
        if plan["diffuse_fine"]:
            faces = own_up[tables_at]
        up[tables_at] = faces
        down[tables_at] = faces

        @pl.when(even)
        def _():
            r["send_e"][...] = up[...]
            r["send_o"][...] = down[...]

        @pl.when(jnp.logical_not(even))
        def _():
            r["send_e"][...] = down[...]
            r["send_o"][...] = up[...]


SCALARS = ("par", "par_o", "children", "fine_counts", "coarse_counts")


def call(kernel, inputs, outputs, scratch, cost=2_000_000):
    names = list(inputs) + list(outputs) + list(scratch)
    result = pl.pallas_call(
        functools.partial(kernel, names),
        out_shape=[jax.ShapeDtypeStruct(shape, F32) for shape in outputs.values()],
        in_specs=[SMEM if name in SCALARS else VMEM for name in inputs],
        out_specs=[VMEM] * len(outputs),
        scratch_shapes=[pltpu.VMEM(shape, F32) for shape in scratch.values()],
        compiler_params=pltpu.CompilerParams(vmem_limit_bytes=48 * 1024 * 1024),
        cost_estimate=pl.CostEstimate(flops=cost, bytes_accessed=cost, transcendentals=0),
    )(*inputs.values())
    return dict(zip(outputs, result))


def shards(
    seed_fine,
    seed_coarse,
    saved_fine,
    saved_coarse,
    diffusion,
    species_shares,
    fine_nbr,
    coarse_nbr,
    children,
    fine_counts,
    coarse_counts,
):
    fields, count_f, cells = seed_fine.shape
    count_c = seed_coarse.shape[1]
    steps = saved_fine.shape[0]
    cycles = saved_coarse.shape[0]
    slots = fields + 1
    sends = octant_sends(count_f)
    messages = len(sends) + 1
    par = jnp.stack([diffusion, species_shares])
    par_o = core_swap(par)
    seed_o = core_swap(seed_coarse)

    def wrapped(kernel):
        return lambda names, *refs: kernel(*refs)

    octant_shapes = {f"octant{s}": (2 * fields + 1, H, LANES) for s in range(messages)}
    cell_shape = (count_c, 2, 2 * fields * B, LANES)

    def seed_call(names, seed_c, seed_other, kids, *rest):
        seed_kernel(seed_c, seed_other, kids, count_f, *rest)

    opened = call(
        seed_call,
        dict(seed_c=seed_coarse, seed_o=seed_o, children=children),
        dict(coarse=(count_c, 2 * fields, cells), **octant_shapes),
        dict(cells=cell_shape),
    )

    def travel(made):
        landed = [octant_move(made[f"octant{s}"], d) for s, d in enumerate(sends)]
        landed.append(made[f"octant{len(sends)}"])
        return landed + [core_swap(value) for value in landed]

    arrived = travel(opened)

    paid = call(
        wrapped(mix_kernel),
        dict(saved_f=saved_fine, saved_c=saved_coarse, seed_f=seed_fine, par=par),
        dict(pay=(2 * steps + 1, count_f, cells), payc=(2, cycles * count_c, cells)),
        {},
    )
    pay, payc = paid["pay"], paid["payc"]
    pay_o, payc_o = core_swap(pay), core_swap(payc)
    tables = call(
        wrapped(chem_kernel),
        dict(
            pay=pay,
            pay_o=pay_o,
            payc=payc,
            payc_o=payc_o,
            fine_counts=fine_counts,
            coarse_counts=coarse_counts,
        ),
        dict(
            gain=(steps, count_f, cells),
            weight=(steps, count_f, cells),
            gain_c=(cycles * count_c, cells),
            weight_c=(cycles * count_c, cells),
        ),
        {},
    )

    rows = 4 * (slots + count_c) + 1
    strip = (rows, 8, LANES)
    most = max(slots, count_c)
    common = dict(par=par, par_o=par_o)
    edge_scratch = dict(
        far_b=strip,
        far_a=strip,
        own_up=strip,
        own_down=strip,
        first=(most, 8, cells),
        edge=(most, 2, 2, 8, LANES),
        below=(most, 2, 2, 8, LANES),
        above=(most, 2, 2, 8, LANES),
    )
    up_scratch = dict(up=strip, down=strip)
    stage_scratch = dict(stage=((2 * messages + 7) // 8, slots, 8 * H, LANES))
    fine_shape = (slots, count_f, cells)
    coarse_shape = (count_c, 2 * fields, cells)

    def plan_of(**changes):
        plan = dict(
            fields=fields,
            count_f=count_f,
            count_c=count_c,
            messages=messages,
            arrivals=2 * messages,
            diffuse_fine=True,
            diffuse_coarse=None,
            add=False,
            react=True,
            react_coarse=None,
            step=0,
        )
        plan.update(changes)
        return plan

    def run(plan, inputs, outputs, scratch):
        return call(functools.partial(step_kernel, plan), inputs, outputs, scratch)

    def halo(made):
        return dict(
            sent_e=made["send_e"],
            sent_o=made["send_o"],
            got_e=pair_swap(made["send_e"], 0),
            got_o=pair_swap(made["send_o"], 1),
        )

    def arrivals(values):
        return {f"arrived{s}": value for s, value in enumerate(values)}

    chem = {name: tables[name] for name in ("gain", "weight")}
    chem_c = {name: tables[name] for name in ("gain_c", "weight_c")}
    send_shapes = dict(send_e=strip, send_o=strip)

    made = run(
        plan_of(diffuse_fine=False, add=True, react_coarse=cycles - 1, step=steps - 1),
        dict(
            common,
            **chem,
            **chem_c,
            seed_f=seed_fine,
            pay=pay,
            pay_o=pay_o,
            coarse=opened["coarse"],
            fine_nbr=fine_nbr,
            coarse_nbr=coarse_nbr,
            **arrivals(arrived),
        ),
        dict(fine_out=fine_shape, coarse_out=coarse_shape, **send_shapes),
        dict(up_scratch, **stage_scratch),
    )
    coarse = made["coarse_out"]
    coarse_final = None
    for step in reversed(range(1, steps)):
        cycle, late = step // 2, step % 2 == 1
        inputs = dict(common, **chem, fine=made["fine_out"], **halo(made))
        outputs = dict(fine_out=fine_shape, **send_shapes)
        scratch = dict(edge_scratch, **up_scratch)
        if late and cycle > 0:
            inputs.update(chem_c, coarse=coarse, children=children)
            outputs.update(coarse_out=coarse_shape, **octant_shapes)
            scratch.update(cells=cell_shape)
            plan = plan_of(diffuse_coarse="keep", react_coarse=cycle - 1, step=step - 1)
        elif late:
            plan = plan_of(step=step - 1)
        else:
            inputs.update(arrivals(arrived))
            scratch.update(stage_scratch)
            plan = plan_of(add=True, step=step - 1)
            if cycle == 1:
                inputs.update(coarse=coarse)
                outputs.update(coarse_final=seed_coarse.shape)
                scratch.update(coarse_next=coarse_shape)
                plan.update(diffuse_coarse="last")
        made = run(plan, inputs, outputs, scratch)
        if "coarse_out" in made:
            coarse = made["coarse_out"]
            arrived = travel(made)
        if "coarse_final" in made:
            coarse_final = made["coarse_final"]
    made = run(
        plan_of(react=False),
        dict(common, fine=made["fine_out"], **halo(made)),
        dict(fine_out=seed_fine.shape),
        edge_scratch,
    )
    return made["fine_out"], coarse_final


def solution(mesh):
    return jax.shard_map(
        shards,
        mesh=mesh,
        in_specs=(
            P("fld", "blk", None),
            P("fld", "blk", None),
            P(None, "fld", "blk", None),
            P(None, "fld", "blk", None),
            P("fld"),
            P("fld"),
            P("blk", None),
            P("blk", None),
            P("blk", None),
            P("blk"),
            P("blk"),
        ),
        out_specs=(P("fld", "blk", None), P("fld", "blk", None)),
        check_vma=False,
    )
```

```python
import functools
import jax
import numpy as np
import jax.numpy as jnp
from jax import lax
from jax.experimental import pallas as pl
from jax.experimental.pallas import tpu as pltpu
from jax.sharding import PartitionSpec as P

B = 16
H = B // 2
NSUB = 4
G = 4
HG = B // G
PLANE = B * B
CYCLES = 2
LANES = 128
TILES = B**3 // LANES
PACK = LANES // G
HEAT = 0.5
ENERGY = 2.0
FAR = -(1 << 20)
VMEM = pl.BlockSpec(memory_space=pltpu.VMEM)
SMEM = pl.BlockSpec(memory_space=pltpu.SMEM)
F32 = jnp.float32
BF16 = jnp.bfloat16


def core_swap(value):
    return lax.ppermute(value, "fld", [(0, 1), (1, 0)])


def pair_swap(value, first):
    n = lax.axis_size("blk")
    pairs = []
    for i in range(first, n + first, 2):
        a, b = i % n, (i + 1) % n
        pairs += [(a, b), (b, a)]
    return lax.ppermute(value, "blk", sorted(pairs))


def octant_sends(count):
    half = count // 2
    return [(1 + s if 1 + s < half else count - 1, half + s) for s in range(half)]


def octant_move(value, distances):
    n = lax.axis_size("blk")
    pairs = []
    for i in range(n):
        for core in range(2):
            pairs.append((2 * i + core, 2 * ((i + distances[core]) % n) + core))
    return lax.ppermute(value, ("blk", "fld"), pairs)


def tables():
    cell = np.arange(PLANE)
    j, k = cell // B, cell % B
    near = np.abs(j[:, None] - j[None, :]) + np.abs(k[:, None] - k[None, :])
    plane = (near == 1).astype(np.float32)
    side = np.zeros((LANES, PLANE), np.float32)
    line = np.arange(B)
    side[line, (B - 1) * B + line] = 1
    side[LANES - B + line, line] = 1
    place = np.zeros((2 * LANES, G * PLANE), np.float32)
    pack = np.zeros((G, PLANE, 2 * LANES), np.float32)
    far = np.zeros((2 * LANES, LANES), np.float32)
    for g in range(G):
        at = g * PACK + line
        place[at, g * PLANE + line * B] = 1
        place[LANES + at, g * PLANE + line * B + B - 1] = 1
        for depth in range(2):
            pack[g, line * B + B - 1 - depth, at + depth * B] = 1
            pack[g, line * B + depth, LANES + at + depth * B] = 1
        far[at[:-1], at[1:]] = 1
        far[at[1:], at[:-1]] = 1
        far[at + B, at] = 1
        far[LANES + at[B - 1], at[0]] = 1
        far[LANES + at[0], at[B - 1]] = 1
    return dict(
        plane=jnp.asarray(plane, BF16),
        side=jnp.asarray(side, BF16),
        place=jnp.asarray(place, BF16),
        pack=jnp.asarray(pack, BF16),
        far=jnp.asarray(far, BF16),
    )


def lane_ids():
    return lax.broadcasted_iota(jnp.int32, (8, LANES), 1)


def row_ids():
    return lax.broadcasted_iota(jnp.int32, (8, LANES), 0)


def roll(x, steps):
    steps = steps % LANES
    return x if steps == 0 else pltpu.roll(x, steps, 1)


def cols(i, jh, width=1):
    return pl.ds((2 * i + jh) * LANES, width * LANES)


def half(jh):
    return pl.ds(jh * LANES, LANES)


def rows_of(i, count=1):
    return pl.ds(8 * i, 8 * count)


def split(x):
    high = x.astype(BF16)
    return high, (x - high.astype(F32)).astype(BF16)


def product(pairs):
    total = None
    for a, b in pairs:
        term = jnp.dot(a, b, preferred_element_type=F32)
        total = term if total is None else total + term
    return total


class Links:
    def __init__(self, column, base, count, by_rows, first_slab):
        self.count = count
        self.by_rows = by_rows
        self.column = column
        self.base = base
        self.first_slab = first_slab
        self.cache = {}

    def place(self, slab, face, shift=0):
        raw = jnp.broadcast_to(self.column(slab, face), (8, LANES))
        return jnp.where(raw >= 0, raw - (self.base + shift), FAR)

    def make(self, name, slab):
        lane = lane_ids()
        if name == "j":
            return jnp.where(lane < LANES // 2, self.place(slab, 3), self.place(slab, 2))
        if name == "j_packed":
            return jnp.where(lane % B == B - 1, self.place(slab, 2), self.place(slab, 3))
        face, step = name
        return self.place(slab, face, step * self.count)

    def index(self, name, slab):
        key = (name, None if self.by_rows else slab)
        if key not in self.cache:
            where = self.make(name, slab - self.first_slab)
            if self.by_rows:
                there = (where >= 0) & (where < self.count)
                self.cache[key] = (jnp.clip(where, 0, self.count - 1), there)
            else:
                self.cache[key] = [where == q for q in range(self.count)]
        return self.cache[key]

    def read(self, name, slab, tile):
        where = self.index(name, slab)
        if self.by_rows:
            got = jnp.take_along_axis(tile(slab), where[0], axis=0, mode="promise_in_bounds")
            return jnp.where(where[1], got, 0.0)
        result = jnp.zeros((8, LANES), F32)
        for q in range(self.count):
            result = jnp.where(where[q], tile(self.first_slab + q), result)
        return result


def put_split(ref, at, lead, value, high_at, low_at):
    high, low = split(value)
    ref[lead + (at, high_at)] = high
    ref[lead + (at, low_at)] = low


def build_planes(source, slabs, planes):
    for s in range(slabs):
        for i in range(0, B, 2):
            g, h = i // HG, i % HG
            for jh in range(2):
                put_split(
                    planes,
                    rows_of(s * HG + h, 2),
                    (g,),
                    source[s, jh, rows_of(i, 2), :],
                    half(jh),
                    half(2 + jh),
                )


def build_sides(source, slabs, near, planes):
    lane = lane_ids()
    for s in range(slabs):
        for i in range(0, B, 2):
            g, h = i // HG, i % HG
            edge = []
            for n in (i, i + 1):

                def tile(q, n=n):
                    return jnp.where(
                        lane < LANES // 2,
                        source[q, 0, rows_of(n), :],
                        source[q, 1, rows_of(n), :],
                    )

                edge.append(near(s).read("j", s, tile))
            put_split(
                planes,
                rows_of(s * HG + h, 2),
                (g,),
                jnp.concatenate(edge, axis=0),
                pl.ds(2 * PLANE, LANES),
                pl.ds(2 * PLANE + LANES, LANES),
            )


def pack_faces(planes, table, used):
    pairs = []
    for g in range(G):
        pairs.append((planes[g, pl.ds(0, used), pl.ds(0, PLANE)], table[g]))
        pairs.append((planes[g, pl.ds(0, used), pl.ds(PLANE, PLANE)], table[g]))
    return product(pairs)


def laplace(source, slabs, near, up, down, below, above, mats, work, emit):
    planes, sums, ends, placed = work["planes"], work["sums"], work["ends"], work["placed"]
    used = slabs * HG * 8
    for s in range(slabs):
        for h in range(0, HG, 2):
            for side in range(2):
                pieces = []
                for n in (h, h + 1):
                    if side == 0:
                        value = near(s).read((4, 0), s, lambda q, n=n: up(q, n))
                        value = value + near(s).read((4, -1), s, lambda q, n=n: below(q, n))
                    else:
                        value = near(s).read((5, 0), s, lambda q, n=n: down(q, n))
                        value = value + near(s).read((5, 1), s, lambda q, n=n: above(q, n))
                    pieces.append(value)
                put_split(
                    ends,
                    rows_of(s * HG + h, 2),
                    (),
                    jnp.concatenate(pieces, axis=0),
                    half(side),
                    half(2 + side),
                )
    every = pl.ds(0, used)
    plane, side = mats["plane"][...], mats["side"][...]
    for g in range(G):
        sums[g, every, :] = product(
            [
                (planes[g, every, pl.ds(0, PLANE)], plane),
                (planes[g, every, pl.ds(PLANE, PLANE)], plane),
                (planes[g, every, pl.ds(2 * PLANE, LANES)], side),
                (planes[g, every, pl.ds(2 * PLANE + LANES, LANES)], side),
            ]
        )
    for g in range(G):
        table = mats["place"][:, pl.ds(g * PLANE, PLANE)]
        placed[every, pl.ds(g * PLANE, PLANE)] = product(
            [
                (ends[every, pl.ds(0, 2 * LANES)], table),
                (ends[every, pl.ds(2 * LANES, 2 * LANES)], table),
            ]
        )
    for s in range(slabs):
        for i in range(B):
            g, h = i // HG, i % HG
            at = rows_of(s * HG + h)
            for jh in range(2):
                c = source[s, jh, rows_of(i), :]
                if i > 0:
                    before = source[s, jh, rows_of(i - 1), :]
                else:
                    before = near(s).read(
                        (0, 0), s, lambda q, jh=jh: source[q, jh, rows_of(B - 1), :]
                    )
                if i < B - 1:
                    after = source[s, jh, rows_of(i + 1), :]
                else:
                    after = near(s).read((1, 0), s, lambda q, jh=jh: source[q, jh, rows_of(0), :])
                lap = (before + after) - 6.0 * c
                lap = lap + (
                    sums[g, at, half(jh)] + placed[at, pl.ds(g * PLANE + jh * LANES, LANES)]
                )
                emit(s, i, jh, c, lap)


def laplace_far(slabs, sides, mats, work, emit):
    lhs, out = work["far_lhs"], work["far_out"]
    group = lane_ids() // PACK
    for n, (links, tile, _, _) in enumerate(sides):
        for s in range(slabs):
            for h in range(0, HG, 2):
                c = jnp.concatenate([tile(s, h), tile(s, h + 1)], axis=0)
                edge = jnp.concatenate(
                    [
                        links(s).read("j_packed", s, lambda q, m=m: tile(q, m))
                        for m in (h, h + 1)
                    ],
                    axis=0,
                )
                at = rows_of((n * slabs + s) * HG + h, 2)
                put_split(lhs, at, (), c, half(0), half(2))
                put_split(lhs, at, (), edge, half(1), half(3))
    every = pl.ds(0, 2 * slabs * HG * 8)
    table = mats["far"][...]
    out[every, :] = product(
        [
            (lhs[every, pl.ds(0, 2 * LANES)], table),
            (lhs[every, pl.ds(2 * LANES, 2 * LANES)], table),
        ]
    )
    for n, (links, tile, own, own_name) in enumerate(sides):
        for s in range(slabs):
            for h in range(HG):
                c = tile(s, h)
                if h > 0:
                    before = tile(s, h - 1)
                else:
                    wrap = links(s).read((0, 0), s, lambda q: tile(q, HG - 1))
                    before = roll(jnp.where(group == G - 1, wrap, tile(s, HG - 1)), PACK)
                if h < HG - 1:
                    after = tile(s, h + 1)
                else:
                    wrap = links(s).read((1, 0), s, lambda q: tile(q, 0))
                    after = roll(jnp.where(group == 0, wrap, tile(s, 0)), -PACK)
                inner = links(s).read(own_name, s, lambda q: own(q, h))
                lap = (before + after) + inner + out[rows_of((n * slabs + s) * HG + h), :] - 6.0 * c
                emit(n, s, h, lap)


def diffuse(source, slabs, near, from_below, from_above, rate, up, down, below, above, mats, work, finish):
    first, packed = work["first"], work["packed"]
    far_first = work["far_first"]
    build_planes(source, slabs, work["planes"])
    build_sides(source, slabs, near, work["planes"])

    def keep_first(s, i, jh, c, lap):
        first[s, jh, rows_of(i), :] = rate(s) * lap

    laplace(source, slabs, near, up, down, below, above, mats, work, keep_first)

    def keep_far(n, s, h, lap):
        far_first[n, s * HG + h] = rate(s) * lap

    laplace_far(
        slabs,
        ((from_below, below, down, (5, 1)), (from_above, above, up, (4, -1))),
        mats,
        work,
        keep_far,
    )
    build_planes(first, slabs, work["planes"])
    build_sides(first, slabs, near, work["planes"])
    packed[pl.ds(0, slabs * HG * 8), :] = pack_faces(work["planes"], mats["pack"], slabs * HG * 8)

    def last(s, i, jh, c, lap):
        finish(s, i, jh, source[s, jh, rows_of(i), :] + c + 0.5 * rate(s) * lap)

    laplace(
        first,
        slabs,
        near,
        lambda s, h: packed[rows_of(s * HG + h), half(0)],
        lambda s, h: packed[rows_of(s * HG + h), half(1)],
        lambda s, h: far_first[0, s * HG + h],
        lambda s, h: far_first[1, s * HG + h],
        mats,
        work,
        last,
    )


def pick(core, a, b):
    return jnp.where(core == 0, a, b)


def spread_vector(core, own, other, row, fields):
    rows = row_ids()
    result = jnp.zeros((8, LANES), F32)
    for f in range(2 * fields):
        value = pick(core, own[row, f], other[row, f]) if f < fields else pick(
            core, other[row, f - fields], own[row, f - fields]
        )
        result = jnp.where(rows == f, value, result)
    return result


def mix_kernel(saved_f, saved_c, seed_f, par, pay, payc):
    steps, fields = saved_f.shape[0], saved_f.shape[1]
    cycles, blocks = saved_c.shape[0], saved_c.shape[2]
    for s in range(steps):
        total = par[1, 0] * saved_f[s, 0]
        for v in range(1, fields):
            total = total + par[1, v] * saved_f[s, v]
        pay[s] = total
        pay[steps + s] = saved_f[s, 0]
    pay[2 * steps] = seed_f[0]
    for c in range(cycles):
        total = par[1, 0] * saved_c[c, 0]
        for v in range(1, fields):
            total = total + par[1, v] * saved_c[c, v]
        payc[0, pl.ds(c * blocks, blocks), :] = total
        payc[1, pl.ds(c * blocks, blocks), :] = saved_c[c, 0]


def reaction_tables(mix, start, counts):
    step = HEAT / counts.astype(F32)
    state = start
    history = []
    for n in range(NSUB):
        inverse = 1.0 / state
        decay = jnp.exp(-ENERGY * inverse)
        active = n < counts
        history.append((active, inverse, decay))
        state = state + jnp.where(active, step * mix * decay, 0.0)
    passed = jnp.ones_like(start)
    weight = jnp.zeros_like(start)
    for active, inverse, decay in reversed(history):
        grown = jnp.where(active, step * decay, 0.0)
        weight = weight + grown * passed
        passed = passed * (1.0 + grown * mix * ENERGY * (inverse * inverse))
    return passed - 1.0, weight


def chem_kernel(pay, pay_o, payc, payc_o, fine_counts, coarse_counts, gain, weight, gain_c, weight_c):
    core = lax.axis_index("fld")
    steps = gain.shape[0]
    rows = row_ids()
    counts = jnp.ones((8, LANES), jnp.int32)
    for b in range(fine_counts.shape[0]):
        counts = jnp.where(rows == b, fine_counts[b], counts)
    blocks = coarse_counts.shape[0]
    entries = gain_c.shape[0]
    counts_c = jnp.ones((entries, LANES), jnp.int32)
    rows_c = lax.broadcasted_iota(jnp.int32, (entries, LANES), 0)
    for r in range(entries):
        counts_c = jnp.where(rows_c == r, coarse_counts[r % blocks], counts_c)

    def body(t, carry):
        at = pl.ds(pl.multiple_of(t * LANES, LANES), LANES)
        for s in range(steps):
            start = pick(core, pay[steps + s, :, at], pay_o[steps + s, :, at])
            a, w = reaction_tables(pay[s, :, at] + pay_o[s, :, at], start, counts)
            gain[s, :, at] = a
            weight[s, :, at] = w
        start = pick(core, payc[1, :, at], payc_o[1, :, at])
        a, w = reaction_tables(payc[0, :, at] + payc_o[0, :, at], start, counts_c)
        gain_c[:, at] = a
        weight_c[:, at] = w
        return carry

    lax.fori_loop(0, TILES, body, 0)


def octants_out(state, first_slab, children, count_f, outs):
    core = lax.axis_index("fld")
    me = lax.axis_index("blk")
    devices = lax.axis_size("blk")
    count_c = children.shape[0]
    fields = 8
    upper = lane_ids() % B // H
    found = []
    for p in range(count_c):
        for o in range(8):
            child = children[p, o]
            distance = jnp.where(child >= 0, (child // count_f - me) % devices, -1)
            found.append((distance, child, p, o))
    sends = octant_sends(count_f)
    for s, out in enumerate(outs):
        if s < len(sends):
            want = jnp.where(core == 0, sends[s][0], sends[s][1])
        else:
            want = 0
        slot = jnp.int32(0)
        label = jnp.int32(-1)
        for distance, child, p, o in found:
            hit = distance == want
            slot = jnp.where(hit, p * 8 + o, slot)
            label = jnp.where(hit, child % count_f, label)
        if s < len(sends):
            label = jnp.where((core == 0) & (sends[s][0] == count_f - 1), -1, label)
        else:
            label = jnp.where(core == 0, label, -1)
        p, a, b, c = slot // 8, slot // 4 % 2, slot // 2 % 2, slot % 2
        kept = upper == c
        for f in range(fields):
            layers = state[first_slab + p, b, pl.ds(a * (H * 8) + f, H, stride=8), :]
            out[f] = jnp.where(kept, layers, 0.0)
        out[fields] = jnp.full((H, LANES), label.astype(F32))


def keep_coarse(state, first_slab, children):
    upper = lane_ids() % B // H
    for p in range(children.shape[0]):
        for a in range(2):
            for b in range(2):
                low = jnp.where(children[p, 4 * a + 2 * b] < 0, 1.0, 0.0)
                high = jnp.where(children[p, 4 * a + 2 * b + 1] < 0, 1.0, 0.0)
                kept = jnp.where(upper == 0, low, high)
                for i in range(a * H, a * H + H):
                    at = (first_slab + p, b, rows_of(i))
                    state[at] = state[at] * kept


def seed_kernel(seed_c, seed_o, children, count_f, coarse, *rest):
    outs, stage = rest[:-1], rest[-1]
    core = lax.axis_index("fld")
    fields, count_c = seed_c.shape[0], seed_c.shape[1]
    for p in range(count_c):
        for v in range(fields):
            own = seed_c[v, pl.ds(p, 1), :]
            other = seed_o[v, pl.ds(p, 1), :]
            stage[p, pl.ds(v, 1), :] = pick(core, own, other)
            stage[p, pl.ds(fields + v, 1), :] = pick(core, other, own)
        for i in range(B):
            for jh in range(2):
                coarse[p, jh, rows_of(i), :] = stage[p, :, cols(i, jh)]
    octants_out(coarse, 0, children, count_f, outs)
    keep_coarse(coarse, 0, children)


def add_octants(messages, state, stage, fields):
    core = lax.axis_index("fld")
    slots = fields + 1
    rows = row_ids()
    lane = lane_ids()
    source = jnp.zeros((8, LANES), jnp.int32)
    for d, message in enumerate(messages):
        label = message[2 * fields].astype(jnp.int32)
        source = jnp.where(label == rows, d, source)
        for s in range(slots):
            if s == fields:
                value = message[0]
            else:
                value = message[pl.ds(core * fields + s, 1)][0]
            stage[d // 8, s, pl.ds(d % 8, H, stride=8), :] = value
    lanes_of = [((H // 2 * jh + lane // B // 2) * B + lane % B // 2) for jh in range(2)]
    groups = (len(messages) + 7) // 8
    indices = []
    for g in range(groups):
        index = source - 8 * g
        indices.append((jnp.clip(index, 0, 7), (index >= 0) & (index < 8)))
    for s in range(slots):
        for i in range(H):
            got = None
            for g in range(groups):
                part = jnp.take_along_axis(
                    stage[g, s, rows_of(i), :], indices[g][0], axis=0, mode="promise_in_bounds"
                )
                part = jnp.where(indices[g][1], part, 0.0)
                got = part if got is None else got + part
            got = 0.125 * (got + roll(got, -H))
            for jh in range(2):
                wide = jnp.take_along_axis(got, lanes_of[jh], axis=1, mode="promise_in_bounds")
                for ii in range(2):
                    at = (s, jh, rows_of(2 * i + ii))
                    state[at] = state[at] + wide


def react_fine(state, fields, par, par_o, gain, weight):
    core = lax.axis_index("fld")
    share = [par[1, s] for s in range(fields)] + [pick(core, par[1, 0], par_o[1, 0])]
    extra = jnp.where(core == 0, 1.0, 0.0)
    for i in range(B):
        for jh in range(2):
            at = cols(i, jh)
            here = (jh, rows_of(i))
            driver = state[(fields,) + here]
            heat = weight[:, at] * driver
            grown = gain[:, at] * driver
            for s in range(fields + 1):
                value = state[(s,) + here] + share[s] * heat
                if s == 0:
                    value = value + extra * grown
                if s == fields:
                    value = value + grown
                state[(s,) + here] = value


def react_coarse(state, first_slab, count_c, shares, gain, weight, first_row):
    own = jnp.where(row_ids() == 0, 1.0, 0.0)
    for p in range(count_c):
        for i in range(B):
            for jh in range(2):
                at = cols(i, jh)
                here = (first_slab + p, jh, rows_of(i))
                value = state[here]
                driver = jnp.broadcast_to(value[0:1], (8, LANES))
                heat = weight[pl.ds(first_row + p, 1), at] * driver
                grown = gain[pl.ds(first_row + p, 1), at] * driver
                state[here] = value + shares * heat + own * grown


def step_kernel(plan, names, *refs):
    r = dict(zip(names, refs))
    core = lax.axis_index("fld")
    me = lax.axis_index("blk")
    even = me % 2 == 0
    fields = plan["fields"]
    slots = fields + 1
    count_f, count_c = plan["count_f"], plan["count_c"]
    par, par_o = r["par"], r["par_o"]
    mats = {name: r[name] for name in MATS}

    if plan["slabs"]:
        slabs, arrived = plan["slabs"], plan["slabs_in"]
        own_up, own_down, far_b, far_a = (r[x] for x in ("own_up", "own_down", "far_b", "far_a"))

        @pl.when(even)
        def _():
            own_up[...] = r["sent_e"][...]
            own_down[...] = r["sent_o"][...]
            far_a[...] = r["got_e"][...]
            far_b[...] = r["got_o"][...]

        @pl.when(jnp.logical_not(even))
        def _():
            own_up[...] = r["sent_o"][...]
            own_down[...] = r["sent_e"][...]
            far_b[...] = r["got_e"][...]
            far_a[...] = r["got_o"][...]

        faces = own_up[arrived * HG]
        rate_of = [par[0, s] for s in range(fields)] + [pick(core, par[0, 0], par_o[0, 0])]
        if slabs > slots:
            rate_of += [0.5 * spread_vector(core, par, par_o, 0, fields)] * count_c

        def links_of(ref, shift):
            def column(slab, face):
                return ref[arrived * HG, :, pl.ds(face, 1)].astype(jnp.int32)

            def column_c(slab, face):
                return ref[arrived * HG, pl.ds(slab, 1), pl.ds(8 + face, 1)].astype(jnp.int32)

            fine = Links(column, (me + shift) * count_f, count_f, True, 0)
            coarse = Links(column_c, (me + shift) * count_c, count_c, False, slots)
            return lambda s: fine if s < slots else coarse

        if slabs <= slots:
            source = r["state"]
        else:
            source = r["state"]
        out = r["state_out"]
        direct = plan["final"]

        def finish(s, i, jh, value):
            if s >= slots and plan["coarse_last"]:
                r["coarse_stage"][s - slots, :, cols(i, jh)] = value
            elif direct:
                out[s, :, cols(i, jh)] = value
            else:
                out[s, jh, rows_of(i), :] = value

        diffuse(
            source,
            slabs,
            links_of(own_up, 0),
            links_of(far_b, -1),
            links_of(far_a, 1),
            lambda s: rate_of[s],
            lambda s, h: own_up[s * HG + h],
            lambda s, h: own_down[s * HG + h],
            lambda s, h: far_b[s * HG + h],
            lambda s, h: far_a[s * HG + h],
            mats,
            r,
            finish,
        )
        if plan["coarse_last"]:
            final, stage = r["coarse_final"], r["coarse_stage"]
            for p in range(count_c):
                for v in range(fields):
                    final[v, pl.ds(p, 1), :] = pick(
                        core, stage[p, pl.ds(v, 1), :], stage[p, pl.ds(fields + v, 1), :]
                    )
        if plan["send_octants"]:
            octants_out(
                out,
                slots,
                r["children"],
                count_f,
                [r[f"octant{s}"] for s in range(plan["messages"])],
            )
            keep_coarse(out, slots, r["children"])
    else:
        out = r["state_out"]
        last = r["pay"].shape[0] - 1
        for i in range(B):
            for jh in range(2):
                at = cols(i, jh)
                for s in range(fields):
                    out[s, jh, rows_of(i), :] = r["seed_f"][s, :, at]
                out[fields, jh, rows_of(i), :] = pick(
                    core, r["pay"][last, :, at], r["pay_o"][last, :, at]
                )
        for p in range(count_c):
            out[slots + p] = r["coarse"][p]
        rows = row_ids()
        lane = lane_ids()
        faces = jnp.zeros((8, LANES), F32)
        for f in range(6):
            column = r["fine_nbr"][:, pl.ds(f, 1)].astype(F32)
            faces = jnp.where(lane == f, jnp.broadcast_to(column, (8, LANES)), faces)
            for p in range(count_c):
                column = r["coarse_nbr"][pl.ds(p, 1), pl.ds(f, 1)].astype(F32)
                faces = jnp.where(
                    (lane == 8 + f) & (rows == p), jnp.broadcast_to(column, (8, LANES)), faces
                )

    if plan["add"]:
        add_octants([r[f"arrived{s}"] for s in range(plan["arrivals"])], out, r["stage"], fields)
    if plan["react"]:
        step = plan["step"]
        react_fine(out, fields, par, par_o, r["gain"].at[step], r["weight"].at[step])
        if plan["react_coarse"] is not None:
            react_coarse(
                out,
                slots,
                count_c,
                spread_vector(core, par, par_o, 1, fields),
                r["gain_c"],
                r["weight_c"],
                plan["react_coarse"] * count_c,
            )
        going = plan["slabs_out"]
        build_planes(out, going, r["planes"])
        r["packed"][pl.ds(0, going * HG * 8), :] = pack_faces(
            r["planes"], mats["pack"], going * HG * 8
        )

        def send(up, down):
            for n in range(going * HG):
                up[n] = r["packed"][rows_of(n), half(0)]
                down[n] = r["packed"][rows_of(n), half(1)]
            up[going * HG] = faces
            down[going * HG] = faces

        pl.when(even)(lambda: send(r["send_e"], r["send_o"]))
        pl.when(jnp.logical_not(even))(lambda: send(r["send_o"], r["send_e"]))


SCALARS = ("par", "par_o", "children", "fine_counts", "coarse_counts")
MATS = ("plane", "side", "place", "pack", "far")
MIB = 1024 * 1024


def call(kernel, inputs, outputs, scratch, cost=2_000_000):
    names = list(inputs) + list(outputs) + list(scratch)
    scratch = {
        name: value if isinstance(value[-1], int) is False else value + (F32,)
        for name, value in scratch.items()
    }
    size = sum(4 * np.prod(v.shape) for v in inputs.values())
    size += sum(4 * np.prod(v) for v in outputs.values())
    size += sum(4 * np.prod(v[:-1]) for v in scratch.values())
    result = pl.pallas_call(
        functools.partial(kernel, names),
        out_shape=[jax.ShapeDtypeStruct(shape, F32) for shape in outputs.values()],
        in_specs=[SMEM if name in SCALARS else VMEM for name in inputs],
        out_specs=[VMEM] * len(outputs),
        scratch_shapes=[pltpu.VMEM(value[:-1], value[-1]) for value in scratch.values()],
        compiler_params=pltpu.CompilerParams(vmem_limit_bytes=int(size) + 12 * MIB),
        cost_estimate=pl.CostEstimate(flops=cost, bytes_accessed=cost, transcendentals=0),
    )(*inputs.values())
    return dict(zip(outputs, result))


def shards(
    seed_fine,
    seed_coarse,
    saved_fine,
    saved_coarse,
    diffusion,
    species_shares,
    fine_nbr,
    coarse_nbr,
    children,
    fine_counts,
    coarse_counts,
):
    fields, count_f, cells = seed_fine.shape
    count_c = seed_coarse.shape[1]
    steps = saved_fine.shape[0]
    cycles = saved_coarse.shape[0]
    slots = fields + 1
    every = slots + count_c
    sends = octant_sends(count_f)
    messages = len(sends) + 1
    par = jnp.stack([diffusion, species_shares])
    par_o = core_swap(par)
    seed_o = core_swap(seed_coarse)
    mats = tables()

    def wrapped(kernel):
        return lambda names, *refs: kernel(*refs)

    octant_shapes = {f"octant{s}": (2 * fields + 1, H, LANES) for s in range(messages)}

    def seed_call(names, seed_c, seed_other, kids, *rest):
        seed_kernel(seed_c, seed_other, kids, count_f, *rest)

    opened = call(
        seed_call,
        dict(seed_c=seed_coarse, seed_o=seed_o, children=children),
        dict(coarse=(count_c, 2, 8 * B, LANES), **octant_shapes),
        dict(seed_stage=(count_c, 2 * fields, cells)),
    )

    def travel(made):
        landed = [octant_move(made[f"octant{s}"], d) for s, d in enumerate(sends)]
        landed.append(made[f"octant{len(sends)}"])
        return landed + [core_swap(value) for value in landed]

    arrived = travel(opened)

    paid = call(
        wrapped(mix_kernel),
        dict(saved_f=saved_fine, saved_c=saved_coarse, seed_f=seed_fine, par=par),
        dict(pay=(2 * steps + 1, count_f, cells), payc=(2, cycles * count_c, cells)),
        {},
    )
    pay, payc = paid["pay"], paid["payc"]
    pay_o, payc_o = core_swap(pay), core_swap(payc)
    made_tables = call(
        wrapped(chem_kernel),
        dict(
            pay=pay,
            pay_o=pay_o,
            payc=payc,
            payc_o=payc_o,
            fine_counts=fine_counts,
            coarse_counts=coarse_counts,
        ),
        dict(
            gain=(steps, count_f, cells),
            weight=(steps, count_f, cells),
            gain_c=(cycles * count_c, cells),
            weight_c=(cycles * count_c, cells),
        ),
        {},
    )
    chem = {name: made_tables[name] for name in ("gain", "weight")}
    chem_c = {name: made_tables[name] for name in ("gain_c", "weight_c")}

    def strip(slabs):
        return (slabs * HG + 1, 8, LANES)

    def state_shape(slabs):
        return (slabs, 2, 8 * B, LANES)

    def work(slabs_in, slabs):
        rows = slabs * HG * 8
        return dict(
            far_b=strip(slabs_in),
            far_a=strip(slabs_in),
            own_up=strip(slabs_in),
            own_down=strip(slabs_in),
            first=state_shape(slabs),
            far_first=(2, slabs * HG, 8, LANES),
            sums=(G, rows, PLANE),
            ends=(rows, 4 * LANES, BF16),
            placed=(rows, G * PLANE),
            far_lhs=(2 * rows, 4 * LANES, BF16),
            far_out=(2 * rows, LANES),
        )

    def pack_work(slabs):
        rows = slabs * HG * 8
        return dict(
            planes=(G, rows, 2 * PLANE + 2 * LANES, BF16),
            packed=(rows, 2 * LANES),
        )

    stage_work = dict(stage=((2 * messages + 7) // 8, slots, 8 * H, LANES))
    common = dict(par=par, par_o=par_o, **mats)

    def plan_of(**changes):
        plan = dict(
            fields=fields,
            count_f=count_f,
            count_c=count_c,
            messages=messages,
            arrivals=2 * messages,
            slabs_in=0,
            slabs=0,
            slabs_out=slots,
            final=False,
            coarse_last=False,
            send_octants=False,
            add=False,
            react=True,
            react_coarse=None,
            step=0,
        )
        plan.update(changes)
        return plan

    def run(plan, inputs, outputs, scratch):
        return call(functools.partial(step_kernel, plan), inputs, outputs, scratch)

    def halo(made):
        return dict(
            state=made["state_out"],
            sent_e=made["send_e"],
            sent_o=made["send_o"],
            got_e=pair_swap(made["send_e"], 0),
            got_o=pair_swap(made["send_o"], 1),
        )

    def sending(slabs):
        return dict(state_out=state_shape(slabs), send_e=strip(slabs), send_o=strip(slabs))

    def arrivals(values):
        return {f"arrived{s}": value for s, value in enumerate(values)}

    made = run(
        plan_of(add=True, react_coarse=cycles - 1, step=steps - 1, slabs_out=every),
        dict(
            common,
            **chem,
            **chem_c,
            seed_f=seed_fine,
            pay=pay,
            pay_o=pay_o,
            coarse=opened["coarse"],
            fine_nbr=fine_nbr,
            coarse_nbr=coarse_nbr,
            **arrivals(arrived),
        ),
        sending(every),
        dict(pack_work(every), **stage_work),
    )
    held = every
    coarse_final = None
    for step in reversed(range(1, steps)):
        cycle, late = step // 2, step % 2 == 1
        inputs = dict(common, **chem, **halo(made))
        scratch = dict(work(held, held), **pack_work(held))
        plan = plan_of(slabs_in=held, slabs=held, step=step - 1)
        outputs = {}
        if late and cycle > 0:
            inputs.update(chem_c, children=children)
            outputs.update(octant_shapes)
            plan.update(send_octants=True, react_coarse=cycle - 1, slabs_out=held)
        elif not late:
            inputs.update(arrivals(arrived))
            scratch.update(stage_work)
            plan.update(add=True, slabs_out=held)
            if cycle == 1:
                outputs.update(coarse_final=seed_coarse.shape)
                scratch.update(coarse_stage=(count_c, 2 * fields, cells))
                plan.update(coarse_last=True, slabs_out=slots)
        else:
            plan.update(slabs_out=held)
        held = plan["slabs_out"]
        outputs.update(sending(held))
        made = run(plan, inputs, outputs, scratch)
        if plan["send_octants"]:
            arrived = travel(made)
        if plan["coarse_last"]:
            coarse_final = made["coarse_final"]
    made = run(
        plan_of(react=False, final=True, slabs_in=held, slabs=fields),
        dict(common, **halo(made)),
        dict(state_out=seed_fine.shape),
        dict(work(held, fields), **pack_work(fields)),
    )
    return made["state_out"], coarse_final


def solution(mesh):
    return jax.shard_map(
        shards,
        mesh=mesh,
        in_specs=(
            P("fld", "blk", None),
            P("fld", "blk", None),
            P(None, "fld", "blk", None),
            P(None, "fld", "blk", None),
            P("fld"),
            P("fld"),
            P("blk", None),
            P("blk", None),
            P("blk", None),
            P("blk"),
            P("blk"),
        ),
        out_specs=(P("fld", "blk", None), P("fld", "blk", None)),
        check_vma=False,
    )
```

```python
import functools
import jax
import numpy as np
import jax.numpy as jnp
from jax import lax
from jax.experimental import pallas as pl
from jax.experimental.pallas import tpu as pltpu
from jax.sharding import PartitionSpec as P

B = 16
H = B // 2
NSUB = 4
G = 4
HG = B // G
PLANE = B * B
CYCLES = 2
LANES = 128
TILES = B**3 // LANES
PACK = LANES // G
HEAT = 0.5
ENERGY = 2.0
FAR = -(1 << 20)
VMEM = pl.BlockSpec(memory_space=pltpu.VMEM)
SMEM = pl.BlockSpec(memory_space=pltpu.SMEM)
HBM = pl.BlockSpec(memory_space=pltpu.HBM)
F32 = jnp.float32
BF16 = jnp.bfloat16


def core_swap(value):
    return lax.ppermute(value, "fld", [(0, 1), (1, 0)])


def pair_swap(value, first, ring):
    n = lax.axis_size("blk")
    pairs = []
    for i in range(n):
        other = i + 1 if (i - first) % 2 == 0 else i - 1
        for core in range(2):
            if ring or 0 <= other < n:
                pairs.append((2 * i + core, 2 * (other % n) + core))
            else:
                pairs.append((2 * i + core, 2 * i + 1 - core))
    return lax.ppermute(value, ("blk", "fld"), pairs)


def first_sends(count):
    middle = count // 2
    return list(zip(list(range(2, middle)) + [1, -1], range(middle, count)))


def later_sends(count):
    middle = count // 2 + 1
    return list(zip(range(2, middle), range(middle, count)))


def octant_move(value, distances):
    n = lax.axis_size("blk")
    pairs = []
    for i in range(n):
        for core in range(2):
            pairs.append((2 * i + core, 2 * ((i + distances[core]) % n) + core))
    return lax.ppermute(value, ("blk", "fld"), pairs)


def tables():
    cell = np.arange(PLANE)
    j, k = cell // B, cell % B
    near = np.abs(j[:, None] - j[None, :]) + np.abs(k[:, None] - k[None, :])
    plane = (near == 1).astype(np.float32)
    side = np.zeros((LANES, PLANE), np.float32)
    line = np.arange(B)
    side[line, (B - 1) * B + line] = 1
    side[LANES - B + line, line] = 1
    place = np.zeros((2 * LANES, G * PLANE), np.float32)
    pack = np.zeros((G, PLANE, 2 * LANES), np.float32)
    far = np.zeros((2 * LANES, LANES), np.float32)
    for g in range(G):
        at = g * PACK + line
        place[at, g * PLANE + line * B] = 1
        place[LANES + at, g * PLANE + line * B + B - 1] = 1
        for depth in range(2):
            pack[g, line * B + B - 1 - depth, at + depth * B] = 1
            pack[g, line * B + depth, LANES + at + depth * B] = 1
        far[at[:-1], at[1:]] = 1
        far[at[1:], at[:-1]] = 1
        far[at + B, at] = 1
        far[LANES + at[B - 1], at[0]] = 1
        far[LANES + at[0], at[B - 1]] = 1
    return dict(
        plane=jnp.asarray(plane, BF16),
        side=jnp.asarray(side, BF16),
        place=jnp.asarray(place, BF16),
        pack=jnp.asarray(pack, BF16),
        far=jnp.asarray(far, BF16),
    )


def lane_ids():
    return lax.broadcasted_iota(jnp.int32, (8, LANES), 1)


def row_ids():
    return lax.broadcasted_iota(jnp.int32, (8, LANES), 0)


def roll(x, steps):
    steps = steps % LANES
    return x if steps == 0 else pltpu.roll(x, steps, 1)


def cols(i, jh, width=1):
    return pl.ds((2 * i + jh) * LANES, width * LANES)


def half(jh):
    return pl.ds(jh * LANES, LANES)


def rows_of(i, count=1):
    return pl.ds(8 * i, 8 * count)


def split(x):
    high = x.astype(BF16)
    return high, (x - high.astype(F32)).astype(BF16)


def product(pairs):
    total = None
    for a, b in pairs:
        term = jnp.dot(a, b, preferred_element_type=F32)
        total = term if total is None else total + term
    return total


class Links:
    def __init__(self, column, base, count, by_rows, first_slab):
        self.count = count
        self.by_rows = by_rows
        self.column = column
        self.base = base
        self.first_slab = first_slab
        self.cache = {}

    def place(self, slab, face, shift=0):
        raw = jnp.broadcast_to(self.column(slab, face), (8, LANES))
        return jnp.where(raw >= 0, raw - (self.base + shift), FAR)

    def make(self, name, slab):
        lane = lane_ids()
        if name == "j":
            return jnp.where(lane < LANES // 2, self.place(slab, 3), self.place(slab, 2))
        if name == "j_packed":
            return jnp.where(lane % B == B - 1, self.place(slab, 2), self.place(slab, 3))
        face, step = name
        return self.place(slab, face, step * self.count)

    def index(self, name, slab):
        key = (name, None if self.by_rows else slab)
        if key not in self.cache:
            where = self.make(name, slab - self.first_slab)
            if self.by_rows:
                there = (where >= 0) & (where < self.count)
                self.cache[key] = (jnp.clip(where, 0, self.count - 1), there)
            else:
                self.cache[key] = [where == q for q in range(self.count)]
        return self.cache[key]

    def read(self, name, slab, tile):
        where = self.index(name, slab)
        if self.by_rows:
            got = jnp.take_along_axis(tile(slab), where[0], axis=0, mode="promise_in_bounds")
            return jnp.where(where[1], got, 0.0)
        result = jnp.zeros((8, LANES), F32)
        for q in range(self.count):
            result = jnp.where(where[q], tile(self.first_slab + q), result)
        return result


def put_split(ref, at, lead, value, high_at, low_at):
    high, low = split(value)
    ref[lead + (at, high_at)] = high
    ref[lead + (at, low_at)] = low


def build_planes(source, slabs, planes):
    for s in range(slabs):
        for i in range(0, B, 2):
            g, h = i // HG, i % HG
            for jh in range(2):
                put_split(
                    planes,
                    rows_of(s * HG + h, 2),
                    (g,),
                    source[s, jh, rows_of(i, 2), :],
                    half(jh),
                    half(2 + jh),
                )


def build_sides(source, slabs, near, planes):
    lane = lane_ids()
    for s in range(slabs):
        for i in range(0, B, 2):
            g, h = i // HG, i % HG
            edge = []
            for n in (i, i + 1):

                def tile(q, n=n):
                    return jnp.where(
                        lane < LANES // 2,
                        source[q, 0, rows_of(n), :],
                        source[q, 1, rows_of(n), :],
                    )

                edge.append(near(s).read("j", s, tile))
            put_split(
                planes,
                rows_of(s * HG + h, 2),
                (g,),
                jnp.concatenate(edge, axis=0),
                pl.ds(2 * PLANE, LANES),
                pl.ds(2 * PLANE + LANES, LANES),
            )


def pack_faces(planes, table, used):
    pairs = []
    for g in range(G):
        pairs.append((planes[g, pl.ds(0, used), pl.ds(0, PLANE)], table[g]))
        pairs.append((planes[g, pl.ds(0, used), pl.ds(PLANE, PLANE)], table[g]))
    return product(pairs)


def laplace(source, slabs, near, up, down, below, above, mats, work, emit):
    planes, sums, ends, placed = work["planes"], work["sums"], work["ends"], work["placed"]
    used = slabs * HG * 8
    for s in range(slabs):
        for h in range(0, HG, 2):
            for side in range(2):
                pieces = []
                for n in (h, h + 1):
                    if side == 0:
                        value = near(s).read((4, 0), s, lambda q, n=n: up(q, n))
                        value = value + near(s).read((4, -1), s, lambda q, n=n: below(q, n))
                    else:
                        value = near(s).read((5, 0), s, lambda q, n=n: down(q, n))
                        value = value + near(s).read((5, 1), s, lambda q, n=n: above(q, n))
                    pieces.append(value)
                put_split(
                    ends,
                    rows_of(s * HG + h, 2),
                    (),
                    jnp.concatenate(pieces, axis=0),
                    half(side),
                    half(2 + side),
                )
    every = pl.ds(0, used)
    plane, side = mats["plane"][...], mats["side"][...]
    for g in range(G):
        sums[g, every, :] = product(
            [
                (planes[g, every, pl.ds(0, PLANE)], plane),
                (planes[g, every, pl.ds(PLANE, PLANE)], plane),
                (planes[g, every, pl.ds(2 * PLANE, LANES)], side),
                (planes[g, every, pl.ds(2 * PLANE + LANES, LANES)], side),
            ]
        )
    for g in range(G):
        table = mats["place"][:, pl.ds(g * PLANE, PLANE)]
        placed[every, pl.ds(g * PLANE, PLANE)] = product(
            [
                (ends[every, pl.ds(0, 2 * LANES)], table),
                (ends[every, pl.ds(2 * LANES, 2 * LANES)], table),
            ]
        )
    for s in range(slabs):
        for i in range(B):
            g, h = i // HG, i % HG
            at = rows_of(s * HG + h)
            for jh in range(2):
                c = source[s, jh, rows_of(i), :]
                if i > 0:
                    before = source[s, jh, rows_of(i - 1), :]
                else:
                    before = near(s).read(
                        (0, 0), s, lambda q, jh=jh: source[q, jh, rows_of(B - 1), :]
                    )
                if i < B - 1:
                    after = source[s, jh, rows_of(i + 1), :]
                else:
                    after = near(s).read((1, 0), s, lambda q, jh=jh: source[q, jh, rows_of(0), :])
                lap = (before + after) - 6.0 * c
                lap = lap + (
                    sums[g, at, half(jh)] + placed[at, pl.ds(g * PLANE + jh * LANES, LANES)]
                )
                emit(s, i, jh, c, lap)


def laplace_far(slabs, sides, mats, work, emit):
    lhs, out = work["far_lhs"], work["far_out"]
    group = lane_ids() // PACK
    for n, (links, tile, _, _) in enumerate(sides):
        for s in range(slabs):
            for h in range(0, HG, 2):
                c = jnp.concatenate([tile(s, h), tile(s, h + 1)], axis=0)
                edge = jnp.concatenate(
                    [
                        links(s).read("j_packed", s, lambda q, m=m: tile(q, m))
                        for m in (h, h + 1)
                    ],
                    axis=0,
                )
                at = rows_of((n * slabs + s) * HG + h, 2)
                put_split(lhs, at, (), c, half(0), half(2))
                put_split(lhs, at, (), edge, half(1), half(3))
    every = pl.ds(0, 2 * slabs * HG * 8)
    table = mats["far"][...]
    out[every, :] = product(
        [
            (lhs[every, pl.ds(0, 2 * LANES)], table),
            (lhs[every, pl.ds(2 * LANES, 2 * LANES)], table),
        ]
    )
    for n, (links, tile, own, own_name) in enumerate(sides):
        for s in range(slabs):
            for h in range(HG):
                c = tile(s, h)
                if h > 0:
                    before = tile(s, h - 1)
                else:
                    wrap = links(s).read((0, 0), s, lambda q: tile(q, HG - 1))
                    before = roll(jnp.where(group == G - 1, wrap, tile(s, HG - 1)), PACK)
                if h < HG - 1:
                    after = tile(s, h + 1)
                else:
                    wrap = links(s).read((1, 0), s, lambda q: tile(q, 0))
                    after = roll(jnp.where(group == 0, wrap, tile(s, 0)), -PACK)
                inner = links(s).read(own_name, s, lambda q: own(q, h))
                lap = (before + after) + inner + out[rows_of((n * slabs + s) * HG + h), :] - 6.0 * c
                emit(n, s, h, lap)


def diffuse(source, slabs, near, from_below, from_above, rate, up, down, below, above, mats, work, finish):
    first, packed = work["first"], work["packed"]
    far_first = work["far_first"]
    build_planes(source, slabs, work["planes"])
    build_sides(source, slabs, near, work["planes"])

    def keep_first(s, i, jh, c, lap):
        first[s, jh, rows_of(i), :] = rate(s) * lap

    laplace(source, slabs, near, up, down, below, above, mats, work, keep_first)

    def keep_far(n, s, h, lap):
        far_first[n, s * HG + h] = rate(s) * lap

    laplace_far(
        slabs,
        ((from_below, below, down, (5, 1)), (from_above, above, up, (4, -1))),
        mats,
        work,
        keep_far,
    )
    build_planes(first, slabs, work["planes"])
    build_sides(first, slabs, near, work["planes"])
    packed[pl.ds(0, slabs * HG * 8), :] = pack_faces(work["planes"], mats["pack"], slabs * HG * 8)

    def last(s, i, jh, c, lap):
        finish(s, i, jh, source[s, jh, rows_of(i), :] + c + 0.5 * rate(s) * lap)

    laplace(
        first,
        slabs,
        near,
        lambda s, h: packed[rows_of(s * HG + h), half(0)],
        lambda s, h: packed[rows_of(s * HG + h), half(1)],
        lambda s, h: far_first[0, s * HG + h],
        lambda s, h: far_first[1, s * HG + h],
        mats,
        work,
        last,
    )


def pick(core, a, b):
    return jnp.where(core == 0, a, b)


def spread_vector(core, own, other, row, fields):
    rows = row_ids()
    result = jnp.zeros((8, LANES), F32)
    for f in range(2 * fields):
        value = pick(core, own[row][f], other[row][f]) if f < fields else pick(
            core, other[row][f - fields], own[row][f - fields]
        )
        result = jnp.where(rows == f, value, result)
    return result


def mix_kernel(
    saved_f, saved_c, seed_f, seed_c, shares, pay, payc, fine, coarse, seeds,
    fine_sem, coarse_sem, seed_sem, seeds_sem,
):
    steps, fields = saved_f.shape[0], saved_f.shape[1]
    cycles, blocks = saved_c.shape[0], saved_c.shape[2]
    copies = [
        pltpu.make_async_copy(saved_f.at[s], fine.at[s], fine_sem.at[s]) for s in range(steps)
    ]
    copy_c = pltpu.make_async_copy(saved_c, coarse, coarse_sem)
    copy_s = pltpu.make_async_copy(seed_f.at[0], pay.at[2 * steps], seed_sem)
    copy_seeds = pltpu.make_async_copy(seed_c, seeds, seeds_sem)
    copy_c.start()
    copy_seeds.start()
    for copy in copies:
        copy.start()
    copy_s.start()
    copy_c.wait()
    for c in range(cycles):
        total = shares[0] * coarse[c, 0]
        for v in range(1, fields):
            total = total + shares[v] * coarse[c, v]
        payc[0, pl.ds(c * blocks, blocks), :] = total
        payc[1, pl.ds(c * blocks, blocks), :] = coarse[c, 0]
    copy_seeds.wait()
    for v in range(fields):
        payc[2 + v, pl.ds(0, blocks), :] = seeds[v]
        payc[2 + v, pl.ds(blocks, blocks), :] = seeds[v]
    for s in range(steps):
        copies[s].wait()
        total = shares[0] * fine[s, 0]
        for v in range(1, fields):
            total = total + shares[v] * fine[s, v]
        pay[s] = total
        pay[steps + s] = fine[s, 0]
    copy_s.wait()


def reaction_tables(mix, start, counts):
    step = HEAT / counts.astype(F32)
    state = start
    history = []
    for n in range(NSUB):
        inverse = 1.0 / state
        decay = jnp.exp(-ENERGY * inverse)
        active = n < counts
        history.append((active, inverse, decay))
        state = state + jnp.where(active, step * mix * decay, 0.0)
    passed = jnp.ones_like(start)
    weight = jnp.zeros_like(start)
    for active, inverse, decay in reversed(history):
        grown = jnp.where(active, step * decay, 0.0)
        weight = weight + grown * passed
        passed = passed * (1.0 + grown * mix * ENERGY * (inverse * inverse))
    return passed - 1.0, weight


def chem_kernel(pay, pay_o, fine_counts, gain, weight):
    core = lax.axis_index("fld")
    steps = gain.shape[0]
    rows = row_ids()
    counts = jnp.ones((8, LANES), jnp.int32)
    for b in range(fine_counts.shape[0]):
        counts = jnp.where(rows == b, fine_counts[b], counts)

    def body(t, carry):
        at = pl.ds(pl.multiple_of(t * LANES, LANES), LANES)
        for s in range(steps):
            start = pick(core, pay[steps + s, :, at], pay_o[steps + s, :, at])
            a, w = reaction_tables(pay[s, :, at] + pay_o[s, :, at], start, counts)
            gain[s, :, at] = a
            weight[s, :, at] = w
        return carry

    lax.fori_loop(0, TILES, body, 0)


def chem_coarse(payc, payc_o, coarse_counts, gain, weight):
    core = lax.axis_index("fld")
    blocks = coarse_counts.shape[0]
    entries = gain.shape[0]
    shape = (entries, 4 * LANES)
    counts = jnp.ones(shape, jnp.int32)
    rows = lax.broadcasted_iota(jnp.int32, shape, 0)
    for r in range(entries):
        counts = jnp.where(rows == r, coarse_counts[r % blocks], counts)

    def body(t, carry):
        at = pl.ds(pl.multiple_of(t * 4 * LANES, 4 * LANES), 4 * LANES)
        start = pick(core, payc[1, :, at], payc_o[1, :, at])
        gain[:, at], weight[:, at] = reaction_tables(
            payc[0, :, at] + payc_o[0, :, at], start, counts
        )
        return carry

    lax.fori_loop(0, TILES // 4, body, 0)


def octant_finder(children, count_f):
    me = lax.axis_index("blk")
    devices = lax.axis_size("blk")
    found = []
    for p in range(children.shape[0]):
        for o in range(8):
            child = children[p, o]
            distance = jnp.where(child >= 0, (child // count_f - me) % devices, FAR)
            found.append((distance, child, p * 8 + o))

    def find(want):
        slot = jnp.int32(0)
        label = jnp.int32(-1)
        for distance, child, place in found:
            hit = distance == want
            slot = jnp.where(hit, place, slot)
            label = jnp.where(hit, child % count_f, label)
        return slot, label

    return find


def write_octant(state, first_slab, found, wanted_fields, out, at):
    slot, label = found
    p, a, b, c = slot // 8, slot // 4 % 2, slot // 2 % 2, slot % 2
    kept = lane_ids() % B // H == c
    for n, f in enumerate(wanted_fields):
        layers = state[first_slab + p, b, pl.ds(a * (H * 8) + f, H, stride=8), :]
        out[at + n] = jnp.where(kept, layers, 0.0)
    out[at + len(wanted_fields)] = jnp.full((H, LANES), label.astype(F32))


def slot_fields(core, fields):
    return [core * fields + v for v in range(fields)] + [0]


def keep_coarse(state, first_slab, children):
    upper = lane_ids() % B // H
    for p in range(children.shape[0]):
        for a in range(2):
            for b in range(2):
                low = jnp.where(children[p, 4 * a + 2 * b] < 0, 1.0, 0.0)
                high = jnp.where(children[p, 4 * a + 2 * b + 1] < 0, 1.0, 0.0)
                kept = jnp.where(upper == 0, low, high)
                for i in range(a * H, a * H + H):
                    at = (first_slab + p, b, rows_of(i))
                    state[at] = state[at] * kept


def start_kernel(
    sends, count_f, fields, payc, payc_o, children, coarse_counts, dif, shr, dif_o, shr_o,
    fine_nbr, coarse_nbr, table, coarse, gain_c, weight_c, local, *rest
):
    core = lax.axis_index("fld")
    count_c = children.shape[0]
    outs, (planes, packed, stage) = rest[:-3], rest[-3:]
    up, down = outs[-2:]
    for p in range(count_c):
        for v in range(fields):
            mine = payc[2 + v, pl.ds(p, 1), :]
            theirs = payc_o[2 + v, pl.ds(p, 1), :]
            stage[p, pl.ds(v, 1), :] = pick(core, mine, theirs)
            stage[p, pl.ds(fields + v, 1), :] = pick(core, theirs, mine)
        for i in range(B):
            for jh in range(2):
                coarse[p, jh, rows_of(i), :] = stage[p, :, cols(i, jh)]
    find = octant_finder(children, count_f)
    for out, distances in zip(outs, sends):
        write_octant(coarse, 0, find(pick(core, *distances)), list(range(2 * fields)), out, 0)
    write_octant(coarse, 0, find(0), slot_fields(core, fields), local, 0)
    chem_coarse(payc, payc_o, coarse_counts, gain_c, weight_c)
    keep_coarse(coarse, 0, children)
    react_coarse(
        coarse,
        0,
        count_c,
        spread_vector(core, (dif, shr), (dif_o, shr_o), 1, fields),
        gain_c,
        weight_c,
        gain_c.shape[0] - count_c,
    )
    build_planes(coarse, count_c, planes)
    packed[...] = pack_faces(planes, table, count_c * HG * 8)
    rows = row_ids()
    lane = lane_ids()
    faces = jnp.zeros((8, LANES), F32)
    for f in range(6):
        column = fine_nbr[:, pl.ds(f, 1)].astype(F32)
        faces = jnp.where(lane == f, jnp.broadcast_to(column, (8, LANES)), faces)
        for p in range(count_c):
            column = coarse_nbr[pl.ds(p, 1), pl.ds(f, 1)].astype(F32)
            faces = jnp.where(
                (lane == 8 + f) & (rows == p), jnp.broadcast_to(column, (8, LANES)), faces
            )
    base = 2 * fields + 1
    for n in range(count_c * HG):
        up[base + n] = packed[rows_of(n), half(0)]
        down[base + n] = packed[rows_of(n), half(1)]
    up[base + count_c * HG] = faces
    down[base + count_c * HG] = faces


def add_octants(entries, state, stage, fields):
    slots = fields + 1
    rows = row_ids()
    lane = lane_ids()
    source = jnp.zeros((8, LANES), jnp.int32)
    for d, tile in enumerate(entries):
        source = jnp.where(tile(None).astype(jnp.int32) == rows, d, source)
        for s in range(slots):
            stage[d // 8, s, pl.ds(d % 8, H, stride=8), :] = tile(s)
    lanes_of = [((H // 2 * jh + lane // B // 2) * B + lane % B // 2) for jh in range(2)]
    groups = (len(entries) + 7) // 8
    indices = []
    for g in range(groups):
        index = source - 8 * g
        indices.append((jnp.clip(index, 0, 7), (index >= 0) & (index < 8)))
    for s in range(slots):
        for i in range(H):
            got = None
            for g in range(groups):
                part = jnp.take_along_axis(
                    stage[g, s, rows_of(i), :], indices[g][0], axis=0, mode="promise_in_bounds"
                )
                part = jnp.where(indices[g][1], part, 0.0)
                got = part if got is None else got + part
            got = 0.125 * (got + roll(got, -H))
            for jh in range(2):
                wide = jnp.take_along_axis(got, lanes_of[jh], axis=1, mode="promise_in_bounds")
                for ii in range(2):
                    at = (s, jh, rows_of(2 * i + ii))
                    state[at] = state[at] + wide


def all_fields(core, fields, ref):
    def tile(s):
        if s is None:
            return ref[2 * fields]
        return ref[0] if s == fields else ref[pl.ds(core * fields + s, 1)][0]

    return tile


def own_slots(fields, ref, at=0):
    return lambda s: ref[at + (fields + 1 if s is None else s)]


def react_fine(state, fields, par, par_o, gain, weight):
    core = lax.axis_index("fld")
    share = [par[1][s] for s in range(fields)] + [pick(core, par[1][0], par_o[1][0])]
    extra = jnp.where(core == 0, 1.0, 0.0)
    for i in range(B):
        for jh in range(2):
            at = cols(i, jh)
            here = (jh, rows_of(i))
            driver = state[(fields,) + here]
            heat = weight[:, at] * driver
            grown = gain[:, at] * driver
            for s in range(fields + 1):
                value = state[(s,) + here] + share[s] * heat
                if s == 0:
                    value = value + extra * grown
                if s == fields:
                    value = value + grown
                state[(s,) + here] = value


def react_coarse(state, first_slab, count_c, shares, gain, weight, first_row):
    own = jnp.where(row_ids() == 0, 1.0, 0.0)
    for p in range(count_c):
        for i in range(B):
            for jh in range(2):
                at = cols(i, jh)
                here = (first_slab + p, jh, rows_of(i))
                value = state[here]
                driver = jnp.broadcast_to(value[0:1], (8, LANES))
                heat = weight[pl.ds(first_row + p, 1), at] * driver
                grown = gain[pl.ds(first_row + p, 1), at] * driver
                state[here] = value + shares * heat + own * grown


def links_maker(plan, faces, shift, fine_slabs):
    me = lax.axis_index("blk") + shift
    count_f, count_c = plan["count_f"], plan["count_c"]

    def column(slab, face):
        return faces[:, face : face + 1].astype(jnp.int32)

    def column_c(slab, face):
        return faces[slab : slab + 1, 8 + face : 9 + face].astype(jnp.int32)

    fine = Links(column, me * count_f, count_f, True, 0)
    coarse = Links(column_c, me * count_c, count_c, False, fine_slabs)
    return lambda s: fine if s < fine_slabs else coarse


def strips_out(plan, r, out, faces, up_octant):
    going = plan["slabs_out"]
    even = lax.axis_index("blk") % 2 == 0
    build_planes(out, going, r["planes"])
    r["packed"][pl.ds(0, going * HG * 8), :] = pack_faces(
        r["planes"], r["pack"], going * HG * 8
    )

    def send(up, down):
        for n in range(going * HG):
            up[n] = r["packed"][rows_of(n), half(0)]
            down[n] = r["packed"][rows_of(n), half(1)]
        at = going * HG
        up[at] = faces
        down[at] = faces
        if up_octant is not None:
            up_octant(up, at + 1)
            for n in range(plan["fields"] + 2):
                down[at + 1 + n] = zero_tile()

    pl.when(even)(lambda: send(r["send_e"], r["send_o"]))
    pl.when(jnp.logical_not(even))(lambda: send(r["send_o"], r["send_e"]))


def zero_tile():
    return jnp.zeros((8, LANES), F32)


def open_kernel(plan, names, *refs):
    r = dict(zip(names, refs))
    core = lax.axis_index("fld")
    fields = plan["fields"]
    slots = fields + 1
    count_f, count_c = plan["count_f"], plan["count_c"]
    par, par_o = (r["dif"], r["shr"]), (r["dif_o"], r["shr_o"])
    out = r["state_out"]
    base = 2 * fields + 1
    strip = count_c * HG

    def far(ref, ref_o, n):
        return pick(core, ref[base + n], ref_o[base + n])

    last = len(plan["sends"]) - 1
    below = [far(r[f"landed{last - 1}"], r[f"shared{last - 1}"], n) for n in range(strip + 1)]
    above = [far(r[f"landed{last}"], r[f"shared{last}"], n) for n in range(strip + 1)]
    own_up, own_down = r["own_up"], r["own_down"]
    faces = own_up[base + strip]
    rates = 0.5 * spread_vector(core, par, par_o, 0, fields)

    def finish(p, i, jh, value):
        out[slots + p, jh, rows_of(i), :] = value

    diffuse(
        r["coarse"],
        count_c,
        links_maker(plan, faces, 0, 0),
        links_maker(plan, below[strip], -1, 0),
        links_maker(plan, above[strip], 1, 0),
        lambda s: rates,
        lambda s, h: own_up[base + s * HG + h],
        lambda s, h: own_down[base + s * HG + h],
        lambda s, h: below[s * HG + h],
        lambda s, h: above[s * HG + h],
        r,
        r,
        finish,
    )
    find = octant_finder(r["children"], count_f)
    for n, distances in enumerate(plan["later"]):
        write_octant(
            out, slots, find(pick(core, *distances)), list(range(2 * fields)), r[f"octant{n}"], 0
        )
    mine = slot_fields(core, fields)
    write_octant(out, slots, find(0), mine, r["local_out"], 0)
    near_octant = r["near_octant"]
    write_octant(out, slots, find(1), mine, near_octant, 0)
    keep_coarse(out, slots, r["children"])
    react_coarse(
        out, slots, count_c, spread_vector(core, par, par_o, 1, fields), r["gain_c"], r["weight_c"], 0
    )
    for i in range(B):
        for jh in range(2):
            at = cols(i, jh)
            for s in range(fields):
                out[s, jh, rows_of(i), :] = r["seed_f"][s, :, at]
            out[fields, jh, rows_of(i), :] = pick(core, r["seed"][0, :, at], r["seed_other"][0, :, at])
    entries = [own_slots(fields, r["local"])]
    for n in range(last):
        entries.append(all_fields(core, fields, r[f"landed{n}"]))
        entries.append(all_fields(core, fields, r[f"shared{n}"]))
    one, two = (all_fields(core, fields, r[f"{word}{last}"]) for word in ("landed", "shared"))
    entries.append(lambda s: pick(core, two(s), one(s)))
    add_octants(entries, out, r["stage"], fields)
    react_fine(out, fields, par, par_o, r["gain"].at[plan["step"]], r["weight"].at[plan["step"]])

    def up_octant(up, at):
        for n in range(slots + 1):
            up[at + n] = near_octant[n]

    strips_out(plan, r, out, faces, up_octant)


def step_kernel(plan, names, *refs):
    r = dict(zip(names, refs))
    core = lax.axis_index("fld")
    even = lax.axis_index("blk") % 2 == 0
    fields = plan["fields"]
    slots = fields + 1
    count_c = plan["count_c"]
    par, par_o = (r["dif"], r["shr"]), (r["dif_o"], r["shr_o"])
    slabs, arrived = plan["slabs"], plan["slabs_in"]
    own_up, own_down, far_b, far_a = (r[x] for x in ("own_up", "own_down", "far_b", "far_a"))
    used = arrived * HG + 1

    def sort_strips(up, down, below, above):
        for n in range(used):
            own_up[n] = up[n]
            own_down[n] = down[n]
            far_b[n] = below[n]
            far_a[n] = above[n]

    pl.when(even)(lambda: sort_strips(r["sent_e"], r["sent_o"], r["got_o"], r["got_e"]))
    pl.when(jnp.logical_not(even))(
        lambda: sort_strips(r["sent_o"], r["sent_e"], r["got_e"], r["got_o"])
    )
    faces = own_up[arrived * HG]
    rate_of = [par[0][s] for s in range(fields)] + [pick(core, par[0][0], par_o[0][0])]
    if slabs > slots:
        rate_of += [0.5 * spread_vector(core, par, par_o, 0, fields)] * count_c
    source, out = r["state"], r["state_out"]

    def finish(s, i, jh, value):
        if s >= slots:
            r["coarse_stage"][s - slots, :, cols(i, jh)] = value
        elif plan["final"]:
            out[s, :, cols(i, jh)] = value
        else:
            out[s, jh, rows_of(i), :] = value

    diffuse(
        source,
        slabs,
        links_maker(plan, faces, 0, slots),
        links_maker(plan, far_b[arrived * HG], -1, slots),
        links_maker(plan, far_a[arrived * HG], 1, slots),
        lambda s: rate_of[s],
        lambda s, h: own_up[s * HG + h],
        lambda s, h: own_down[s * HG + h],
        lambda s, h: far_b[s * HG + h],
        lambda s, h: far_a[s * HG + h],
        r,
        r,
        finish,
    )
    if slabs > slots:
        final, stage = r["coarse_final"], r["coarse_stage"]
        for p in range(count_c):
            for v in range(fields):
                final[v, pl.ds(p, 1), :] = pick(
                    core, stage[p, pl.ds(v, 1), :], stage[p, pl.ds(fields + v, 1), :]
                )
    if plan["add"]:
        near = r["near_octant"]

        def take(ref):
            for n in range(slots + 1):
                near[n] = ref[plan["near_at"] + n]

        pl.when(even)(lambda: take(r["near_o"]))
        pl.when(jnp.logical_not(even))(lambda: take(r["near_e"]))
        entries = [own_slots(fields, r["local"]), own_slots(fields, near)]
        for n in range(len(plan["later"])):
            entries.append(all_fields(core, fields, r[f"landed{n}"]))
            entries.append(all_fields(core, fields, r[f"shared{n}"]))
        add_octants(entries, out, r["stage"], fields)
    if not plan["final"]:
        step = plan["step"]
        react_fine(out, fields, par, par_o, r["gain"].at[step], r["weight"].at[step])
        strips_out(plan, r, out, faces, None)


SCALARS = ("dif", "shr", "dif_o", "shr_o", "children", "fine_counts", "coarse_counts")
MATS = ("plane", "side", "place", "pack", "far")
MIB = 1024 * 1024


def call(kernel, inputs, outputs, scratch, hbm=(), sems=(), limit=None, cost=1000):
    names = list(inputs) + list(outputs) + list(scratch)
    scratch = {
        name: value if value[-1] is BF16 else value + (F32,) for name, value in scratch.items()
    }
    size = sum(4 * np.prod(v.shape) for name, v in inputs.items() if name not in hbm)
    size += sum(4 * np.prod(v) for v in outputs.values())
    size += sum(4 * np.prod(v[:-1]) for v in scratch.values())

    def spec(name):
        if name in hbm:
            return HBM
        return SMEM if name in SCALARS else VMEM

    result = pl.pallas_call(
        functools.partial(kernel, names),
        out_shape=[jax.ShapeDtypeStruct(shape, F32) for shape in outputs.values()],
        in_specs=[spec(name) for name in inputs],
        out_specs=[VMEM] * len(outputs),
        scratch_shapes=[pltpu.VMEM(value[:-1], value[-1]) for value in scratch.values()]
        + [pltpu.SemaphoreType.DMA(shape) for shape in sems],
        compiler_params=pltpu.CompilerParams(vmem_limit_bytes=limit or int(size) + 12 * MIB),
        cost_estimate=pl.CostEstimate(flops=cost, bytes_accessed=cost, transcendentals=0),
    )(*inputs.values())
    return dict(zip(outputs, result))


def shards(
    seed_fine,
    seed_coarse,
    saved_fine,
    saved_coarse,
    diffusion,
    species_shares,
    fine_nbr,
    coarse_nbr,
    children,
    fine_counts,
    coarse_counts,
):
    fields, count_f, cells = seed_fine.shape
    count_c = seed_coarse.shape[1]
    steps = saved_fine.shape[0]
    cycles = saved_coarse.shape[0]
    slots = fields + 1
    every = slots + count_c
    sends, later = first_sends(count_f), later_sends(count_f)
    mats = tables()
    octant_shape = (2 * fields + 1, H, LANES)
    slots_shape = (slots + 1, H, LANES)
    loaded_shape = (2 * fields + 1 + count_c * HG + 1, 8, LANES)

    def plain(kernel, *fixed):
        return lambda names, *refs: kernel(*fixed, *refs)

    def strip(slabs, more=0):
        return (slabs * HG + 1 + more, 8, LANES)

    def state_shape(slabs):
        return (slabs, 2, 8 * B, LANES)

    def work(slabs):
        rows = slabs * HG * 8
        return dict(
            first=state_shape(slabs),
            far_first=(2, slabs * HG, 8, LANES),
            sums=(G, rows, PLANE),
            ends=(rows, 4 * LANES, BF16),
            placed=(rows, G * PLANE),
            far_lhs=(2 * rows, 4 * LANES, BF16),
            far_out=(2 * rows, LANES),
        )

    def strip_work(slabs):
        return {name: strip(slabs) for name in ("far_b", "far_a", "own_up", "own_down")}

    def pack_work(slabs):
        rows = slabs * HG * 8
        return dict(
            planes=(G, rows, 2 * PLANE + 2 * LANES, BF16),
            packed=(rows, 2 * LANES),
        )

    def after(value, *before):
        return lax.optimization_barrier((value, before))[0]

    stage_work = dict(stage=(1, slots, 8 * H, LANES))
    dif_o, shr_o = core_swap(diffusion), core_swap(species_shares)
    par = dict(dif=diffusion, shr=species_shares, dif_o=dif_o, shr_o=shr_o)

    paid = call(
        plain(mix_kernel),
        dict(
            saved_f=saved_fine,
            saved_c=saved_coarse,
            seed_f=seed_fine,
            seed_c=seed_coarse,
            shr=species_shares,
        ),
        dict(
            pay=(2 * steps + 1, count_f, cells), payc=(2 + fields, cycles * count_c, cells)
        ),
        dict(fine=saved_fine.shape, coarse=saved_coarse.shape, seeds=seed_coarse.shape),
        hbm=("saved_f", "saved_c", "seed_f", "seed_c"),
        sems=((steps,), (), (), ()),
        limit=60 * MIB,
    )
    pay, payc = paid["pay"], paid["payc"]
    payc_o, pay_o = core_swap(payc), core_swap(pay)

    loaded = [f"octant{n}" for n in range(len(sends) - 2)] + ["up", "down"]
    started = call(
        plain(start_kernel, sends, count_f, fields),
        dict(
            payc=payc,
            payc_o=payc_o,
            children=children,
            coarse_counts=coarse_counts,
            **par,
            fine_nbr=fine_nbr,
            coarse_nbr=coarse_nbr,
            pack=mats["pack"],
        ),
        dict(
            coarse=state_shape(count_c),
            gain_c=(cycles * count_c, cells),
            weight_c=(cycles * count_c, cells),
            local=slots_shape,
            **{name: loaded_shape if name in ("up", "down") else octant_shape for name in loaded},
        ),
        dict(pack_work(count_c), coarse_stage=(count_c, 2 * fields, cells)),
    )
    landed = [octant_move(started[name], d) for name, d in zip(loaded, sends)]
    chem = call(
        plain(chem_kernel),
        dict(pay=pay, pay_o=pay_o, fine_counts=fine_counts),
        dict(gain=(steps, count_f, cells), weight=(steps, count_f, cells)),
        {},
    )
    landed, chem = lax.optimization_barrier((landed, chem))
    shared = [core_swap(value) for value in landed]

    def named(word, values):
        return {f"{word}{n}": value for n, value in enumerate(values)}

    plan = dict(
        fields=fields,
        count_f=count_f,
        count_c=count_c,
        sends=sends,
        later=later,
        slabs_in=every,
        slabs=every,
        slabs_out=slots,
        final=False,
        add=False,
        near_at=every * HG + 1,
    )

    def run(kernel, changes, inputs, outputs, scratch):
        return call(
            functools.partial(kernel, dict(plan, **changes)),
            dict(par, **mats, **inputs),
            outputs,
            scratch,
        )

    def halo(made, ring=False):
        got_o = pair_swap(made["send_o"], 1, ring)
        got_e = pair_swap(made["send_e"], 0, ring)
        return dict(sent_o=made["send_o"], got_o=got_o, sent_e=made["send_e"], got_e=got_e)

    def sending(slabs, more=0):
        return dict(
            state_out=state_shape(slabs), send_e=strip(slabs, more), send_o=strip(slabs, more)
        )

    made = run(
        open_kernel,
        dict(slabs_out=every, step=steps - 1),
        dict(
            chem,
            gain_c=started["gain_c"],
            weight_c=started["weight_c"],
            children=children,
            coarse=started["coarse"],
            own_up=started["up"],
            own_down=started["down"],
            seed_f=seed_fine,
            seed=pay[2 * steps :],
            seed_other=pay_o[2 * steps :],
            local=started["local"],
            **named("landed", landed),
            **named("shared", shared),
        ),
        dict(
            sending(every, slots + 1),
            local_out=slots_shape,
            **named("octant", [octant_shape] * len(later)),
        ),
        dict(work(count_c), **pack_work(every), **stage_work, near_octant=slots_shape),
    )
    first_halo = halo(made, True)
    local = made["local_out"]
    landed = [octant_move(made[f"octant{n}"], d) for n, d in enumerate(later)]
    landed, first_halo = lax.optimization_barrier((landed, first_halo))
    shared = [core_swap(value) for value in landed]
    made = run(
        step_kernel,
        dict(step=steps - 2),
        dict(chem, state=made["state_out"], **first_halo),
        dict(sending(slots), coarse_final=seed_coarse.shape),
        dict(
            work(every),
            **strip_work(every),
            **pack_work(every),
            coarse_stage=(count_c, 2 * fields, cells),
        ),
    )
    coarse_final = made["coarse_final"]
    for step in reversed(range(steps - 2)):
        inputs = dict(chem, state=made["state_out"], **halo(made))
        scratch = dict(work(slots), **strip_work(slots), **pack_work(slots))
        changes = dict(step=step, slabs_in=slots, slabs=slots)
        if step == steps - 3:
            inputs.update(named("landed", landed), **named("shared", shared), local=local)
            inputs.update(near_e=first_halo["got_e"], near_o=first_halo["got_o"])
            scratch.update(stage_work, near_octant=slots_shape)
            changes.update(add=True)
        made = run(step_kernel, changes, inputs, sending(slots), scratch)
    made = run(
        step_kernel,
        dict(final=True, slabs_in=slots, slabs=fields),
        dict(state=made["state_out"], **halo(made)),
        dict(state_out=seed_fine.shape),
        dict(work(fields), **strip_work(slots), **pack_work(fields)),
    )
    return made["state_out"], coarse_final


def solution(mesh):
    return jax.shard_map(
        shards,
        mesh=mesh,
        in_specs=(
            P("fld", "blk", None),
            P("fld", "blk", None),
            P(None, "fld", "blk", None),
            P(None, "fld", "blk", None),
            P("fld"),
            P("fld"),
            P("blk", None),
            P("blk", None),
            P("blk", None),
            P("blk"),
            P("blk"),
        ),
        out_specs=(P("fld", "blk", None), P("fld", "blk", None)),
        check_vma=False,
    )
```

```python
import functools
from types import SimpleNamespace
import jax
import numpy as np
import jax.numpy as jnp
from jax import lax
from jax.experimental import pallas as pl
from jax.experimental.pallas import tpu as pltpu
from jax.sharding import PartitionSpec as P

B = 16
H = B // 2
NSUB = 4
G = 4
HG = B // G
PLANE = B * B
CYCLES = 2
LANES = 128
TILES = B**3 // LANES
PACK = LANES // G
HEAT = 0.5
ENERGY = 2.0
FAR = -(1 << 20)
VMEM = pl.BlockSpec(memory_space=pltpu.VMEM)
SMEM = pl.BlockSpec(memory_space=pltpu.SMEM)
HBM = pl.BlockSpec(memory_space=pltpu.HBM)
F32 = jnp.float32
BF16 = jnp.bfloat16


def core_swap(value):
    return lax.ppermute(value, "fld", [(0, 1), (1, 0)])


def pair_swap(value, first, ring):
    n = lax.axis_size("blk")
    pairs = []
    for i in range(n):
        other = i + 1 if (i - first) % 2 == 0 else i - 1
        for core in range(2):
            if ring or 0 <= other < n:
                pairs.append((2 * i + core, 2 * (other % n) + core))
            else:
                pairs.append((2 * i + core, 2 * i + 1 - core))
    return lax.ppermute(value, ("blk", "fld"), pairs)


def first_sends(count):
    middle = count // 2
    return list(zip(list(range(2, middle)) + [1, -1], range(middle, count)))


def later_sends(count):
    middle = count // 2 + 1
    return list(zip(range(2, middle), range(middle, count)))


def octant_move(value, distances):
    n = lax.axis_size("blk")
    pairs = []
    for i in range(n):
        for core in range(2):
            pairs.append((2 * i + core, 2 * ((i + distances[core]) % n) + core))
    return lax.ppermute(value, ("blk", "fld"), pairs)


def tables():
    cell = np.arange(PLANE)
    j, k = cell // B, cell % B
    near = np.abs(j[:, None] - j[None, :]) + np.abs(k[:, None] - k[None, :])
    plane = (near == 1).astype(np.float32)
    side = np.zeros((LANES, PLANE), np.float32)
    line = np.arange(B)
    side[line, (B - 1) * B + line] = 1
    side[LANES - B + line, line] = 1
    pack = np.zeros((G, PLANE, 2 * LANES), np.float32)
    far = np.zeros((2 * LANES, LANES), np.float32)
    for g in range(G):
        at = g * PACK + line
        for depth in range(2):
            pack[g, line * B + B - 1 - depth, at + depth * B] = 1
            pack[g, line * B + depth, LANES + at + depth * B] = 1
        far[at[:-1], at[1:]] = 1
        far[at[1:], at[:-1]] = 1
        far[at + B, at] = 1
        far[LANES + at[B - 1], at[0]] = 1
        far[LANES + at[0], at[B - 1]] = 1
    place = np.concatenate([pack[g].T for g in range(G)], axis=1)
    return SimpleNamespace(
        plane=jnp.asarray(plane, BF16),
        side=jnp.asarray(side, BF16),
        place=jnp.asarray(place, BF16),
        pack=jnp.asarray(pack, BF16),
        far=jnp.asarray(far, BF16),
    )


def lane_ids():
    return lax.broadcasted_iota(jnp.int32, (8, LANES), 1)


def row_ids():
    return lax.broadcasted_iota(jnp.int32, (8, LANES), 0)


def roll(x, steps):
    steps = steps % LANES
    return x if steps == 0 else pltpu.roll(x, steps, 1)


def cols(i, jh, width=1):
    return pl.ds((2 * i + jh) * LANES, width * LANES)


def half(jh):
    return pl.ds(jh * LANES, LANES)


def rows_of(i, count=1):
    return pl.ds(8 * i, 8 * count)


def split(x):
    high = x.astype(BF16)
    return high, (x - high.astype(F32)).astype(BF16)


def product(pairs):
    total = None
    for a, b in pairs:
        term = jnp.dot(a, b, preferred_element_type=F32)
        total = term if total is None else total + term
    return total


class Links:
    def __init__(self, column, base, count, by_rows, first_slab):
        self.count = count
        self.by_rows = by_rows
        self.column = column
        self.base = base
        self.first_slab = first_slab
        self.cache = {}

    def place(self, slab, face, shift=0):
        raw = jnp.broadcast_to(self.column(slab, face), (8, LANES))
        return jnp.where(raw >= 0, raw - (self.base + shift), FAR)

    def make(self, name, slab):
        lane = lane_ids()
        if name == "j":
            return jnp.where(lane < LANES // 2, self.place(slab, 3), self.place(slab, 2))
        if name == "j_packed":
            return jnp.where(lane % B == B - 1, self.place(slab, 2), self.place(slab, 3))
        face, step = name
        return self.place(slab, face, step * self.count)

    def index(self, name, slab):
        key = (name, None if self.by_rows else slab)
        if key not in self.cache:
            where = self.make(name, slab - self.first_slab)
            if self.by_rows:
                there = (where >= 0) & (where < self.count)
                self.cache[key] = (jnp.clip(where, 0, self.count - 1), there)
            else:
                self.cache[key] = [where == q for q in range(self.count)]
        return self.cache[key]

    def read(self, name, slab, tile):
        where = self.index(name, slab)
        if self.by_rows:
            got = jnp.take_along_axis(tile(slab), where[0], axis=0, mode="promise_in_bounds")
            return jnp.where(where[1], got, 0.0)
        result = jnp.zeros((8, LANES), F32)
        for q in range(self.count):
            result = jnp.where(where[q], tile(self.first_slab + q), result)
        return result


def put_split(ref, at, lead, value, high_at, low_at):
    high, low = split(value)
    ref[lead + (at, high_at)] = high
    ref[lead + (at, low_at)] = low


def build_planes(source, slabs, planes):
    for s in range(slabs):
        for i in range(0, B, 2):
            g, h = i // HG, i % HG
            for jh in range(2):
                put_split(
                    planes,
                    rows_of(s * HG + h, 2),
                    (g,),
                    source[s, jh, rows_of(i, 2), :],
                    half(jh),
                    half(2 + jh),
                )


def build_sides(source, slabs, near, planes):
    lane = lane_ids()
    for s in range(slabs):
        for i in range(0, B, 2):
            g, h = i // HG, i % HG
            edge = []
            for n in (i, i + 1):

                def tile(q, n=n):
                    return jnp.where(
                        lane < LANES // 2,
                        source[q, 0, rows_of(n), :],
                        source[q, 1, rows_of(n), :],
                    )

                edge.append(near(s).read("j", s, tile))
            put_split(
                planes,
                rows_of(s * HG + h, 2),
                (g,),
                jnp.concatenate(edge, axis=0),
                pl.ds(2 * PLANE, LANES),
                pl.ds(2 * PLANE + LANES, LANES),
            )


def pack_faces(planes, table, used):
    pairs = []
    for g in range(G):
        pairs.append((planes[g, pl.ds(0, used), pl.ds(0, PLANE)], table[g]))
        pairs.append((planes[g, pl.ds(0, used), pl.ds(PLANE, PLANE)], table[g]))
    return product(pairs)


def outer_lanes():
    return lane_ids() // B % 2 == 0


def place_ends(ends, placed, used, mats):
    every = pl.ds(0, used)
    for g in range(G):
        table = mats.place[:, pl.ds(g * PLANE, PLANE)]
        placed[every, pl.ds(g * PLANE, PLANE)] = product(
            [
                (ends[every, pl.ds(0, 2 * LANES)], table),
                (ends[every, pl.ds(2 * LANES, 2 * LANES)], table),
            ]
        )


def placed_tile(placed, s, i, jh):
    return placed[rows_of(s * HG + i % HG), pl.ds(i // HG * PLANE + jh * LANES, LANES)]


def laplace(source, slabs, near, up, down, below, above, mats, work, emit):
    planes, sums, ends, placed = work.planes, work.sums, work.ends, work.placed
    used = slabs * HG * 8
    outer = outer_lanes()
    for s in range(slabs):
        for h in range(0, HG, 2):
            for side in range(2):
                pieces = []
                for n in (h, h + 1):
                    if side == 0:
                        value = near(s).read((5, 0), s, lambda q, n=n: down(q, n))
                        if above is not None:
                            value = value + near(s).read((5, 1), s, lambda q, n=n: above(q, n))
                    else:
                        value = near(s).read((4, 0), s, lambda q, n=n: up(q, n))
                        if below is not None:
                            value = value + near(s).read((4, -1), s, lambda q, n=n: below(q, n))
                    pieces.append(jnp.where(outer, value, 0.0))
                put_split(
                    ends,
                    rows_of(s * HG + h, 2),
                    (),
                    jnp.concatenate(pieces, axis=0),
                    half(side),
                    half(2 + side),
                )
    every = pl.ds(0, used)
    plane, side = mats.plane[...], mats.side[...]
    for g in range(G):
        sums[g, every, :] = product(
            [
                (planes[g, every, pl.ds(0, PLANE)], plane),
                (planes[g, every, pl.ds(PLANE, PLANE)], plane),
                (planes[g, every, pl.ds(2 * PLANE, LANES)], side),
                (planes[g, every, pl.ds(2 * PLANE + LANES, LANES)], side),
            ]
        )
    place_ends(ends, placed, used, mats)
    for s in range(slabs):
        for i in range(B):
            g, h = i // HG, i % HG
            at = rows_of(s * HG + h)
            for jh in range(2):
                c = source[s, jh, rows_of(i), :]
                if i > 0:
                    before = source[s, jh, rows_of(i - 1), :]
                else:
                    before = near(s).read(
                        (0, 0), s, lambda q, jh=jh: source[q, jh, rows_of(B - 1), :]
                    )
                if i < B - 1:
                    after = source[s, jh, rows_of(i + 1), :]
                else:
                    after = near(s).read((1, 0), s, lambda q, jh=jh: source[q, jh, rows_of(0), :])
                lap = (before + after) - 6.0 * c
                lap = lap + (
                    sums[g, at, half(jh)] + placed[at, pl.ds(g * PLANE + jh * LANES, LANES)]
                )
                emit(s, i, jh, c, lap)


def laplace_far(slabs, sides, mats, work, emit):
    lhs, out = work.far_lhs, work.far_out
    group = lane_ids() // PACK
    for n, (links, tile, _, _) in enumerate(sides):
        for s in range(slabs):
            for h in range(0, HG, 2):
                c = jnp.concatenate([tile(s, h), tile(s, h + 1)], axis=0)
                edge = jnp.concatenate(
                    [
                        links(s).read("j_packed", s, lambda q, m=m: tile(q, m))
                        for m in (h, h + 1)
                    ],
                    axis=0,
                )
                at = rows_of((n * slabs + s) * HG + h, 2)
                put_split(lhs, at, (), c, half(0), half(2))
                put_split(lhs, at, (), edge, half(1), half(3))
    every = pl.ds(0, 2 * slabs * HG * 8)
    table = mats.far[...]
    out[every, :] = product(
        [
            (lhs[every, pl.ds(0, 2 * LANES)], table),
            (lhs[every, pl.ds(2 * LANES, 2 * LANES)], table),
        ]
    )
    for n, (links, tile, own, own_name) in enumerate(sides):
        for s in range(slabs):
            for h in range(HG):
                c = tile(s, h)
                if h > 0:
                    before = tile(s, h - 1)
                else:
                    wrap = links(s).read((0, 0), s, lambda q: tile(q, HG - 1))
                    before = roll(jnp.where(group == G - 1, wrap, tile(s, HG - 1)), PACK)
                if h < HG - 1:
                    after = tile(s, h + 1)
                else:
                    wrap = links(s).read((1, 0), s, lambda q: tile(q, 0))
                    after = roll(jnp.where(group == 0, wrap, tile(s, 0)), -PACK)
                lap = (before + after) + out[rows_of((n * slabs + s) * HG + h), :] - 6.0 * c
                if own is not None:
                    lap = lap + links(s).read(own_name, s, lambda q: own(q, h))
                emit(n, s, h, lap)


def diffuse(source, slabs, near, from_below, from_above, rate, up, down, below, above, mats, work, finish):
    first, packed = work.first, work.packed
    alone = below is None
    far_first = None if alone else work.far_first
    build_planes(source, slabs, work.planes)
    build_sides(source, slabs, near, work.planes)

    def keep_first(s, i, jh, c, lap):
        first[s, jh, rows_of(i), :] = rate(s) * lap

    laplace(source, slabs, near, up, down, below, above, mats, work, keep_first)

    def keep_far(n, s, h, lap):
        far_first[n, s * HG + h] = rate(s) * lap

    if not alone:
        laplace_far(
            slabs,
            ((from_below, below, down, (5, 1)), (from_above, above, up, (4, -1))),
            mats,
            work,
            keep_far,
        )
    build_planes(first, slabs, work.planes)
    build_sides(first, slabs, near, work.planes)
    packed[pl.ds(0, slabs * HG * 8), :] = pack_faces(work.planes, mats.pack, slabs * HG * 8)

    def last(s, i, jh, c, lap):
        finish(s, i, jh, source[s, jh, rows_of(i), :] + c + 0.5 * rate(s) * lap)

    laplace(
        first,
        slabs,
        near,
        lambda s, h: packed[rows_of(s * HG + h), half(0)],
        lambda s, h: packed[rows_of(s * HG + h), half(1)],
        None if alone else lambda s, h: far_first[0, s * HG + h],
        None if alone else lambda s, h: far_first[1, s * HG + h],
        mats,
        work,
        last,
    )


def numbered(word, n):
    return word + str(n)


def pick(core, a, b):
    return jnp.where(core == 0, a, b)


def spread_vector(core, own, other, row, fields):
    rows = row_ids()
    result = jnp.zeros((8, LANES), F32)
    for f in range(2 * fields):
        value = pick(core, own[row][f], other[row][f]) if f < fields else pick(
            core, other[row][f - fields], own[row][f - fields]
        )
        result = jnp.where(rows == f, value, result)
    return result


def mix_kernel(
    saved_f, saved_c, seed_f, seed_c, shares, pay, payc, fine, coarse, seeds,
    fine_sem, coarse_sem, seed_sem, seeds_sem,
):
    steps, fields = saved_f.shape[0], saved_f.shape[1]
    cycles, blocks = saved_c.shape[0], saved_c.shape[2]
    copies = [
        pltpu.make_async_copy(saved_f.at[s], fine.at[s], fine_sem.at[s]) for s in range(steps)
    ]
    copy_c = pltpu.make_async_copy(saved_c, coarse, coarse_sem)
    copy_s = pltpu.make_async_copy(seed_f.at[0], pay.at[2 * steps], seed_sem)
    copy_seeds = pltpu.make_async_copy(seed_c, seeds, seeds_sem)
    copy_c.start()
    copy_seeds.start()
    for copy in copies:
        copy.start()
    copy_s.start()
    copy_c.wait()
    for c in range(cycles):
        total = shares[0] * coarse[c, 0]
        for v in range(1, fields):
            total = total + shares[v] * coarse[c, v]
        payc[0, pl.ds(c * blocks, blocks), :] = total
        payc[1, pl.ds(c * blocks, blocks), :] = coarse[c, 0]
    copy_seeds.wait()
    for v in range(fields):
        payc[2 + v, pl.ds(0, blocks), :] = seeds[v]
        payc[2 + v, pl.ds(blocks, blocks), :] = seeds[v]
    for s in range(steps):
        copies[s].wait()
        total = shares[0] * fine[s, 0]
        for v in range(1, fields):
            total = total + shares[v] * fine[s, v]
        pay[s] = total
        pay[steps + s] = fine[s, 0]
    copy_s.wait()


def reaction_tables(mix, start, counts):
    step = HEAT / counts.astype(F32)
    state = start
    history = []
    for n in range(NSUB):
        inverse = 1.0 / state
        decay = jnp.exp(-ENERGY * inverse)
        active = n < counts
        history.append((active, inverse, decay))
        state = state + jnp.where(active, step * mix * decay, 0.0)
    passed = jnp.ones_like(start)
    weight = jnp.zeros_like(start)
    for active, inverse, decay in reversed(history):
        grown = jnp.where(active, step * decay, 0.0)
        weight = weight + grown * passed
        passed = passed * (1.0 + grown * mix * ENERGY * (inverse * inverse))
    return passed - 1.0, weight


def chem_kernel(pay, pay_o, fine_counts, pack, gain, weight, edges, planes):
    core = lax.axis_index("fld")
    steps = gain.shape[0]
    rows = row_ids()
    counts = jnp.ones((8, LANES), jnp.int32)
    for b in range(fine_counts.shape[0]):
        counts = jnp.where(rows == b, fine_counts[b], counts)

    def body(t, carry):
        at = pl.ds(pl.multiple_of(t * LANES, LANES), LANES)
        for s in range(steps):
            start = pick(core, pay[steps + s, :, at], pay_o[steps + s, :, at])
            a, w = reaction_tables(pay[s, :, at] + pay_o[s, :, at], start, counts)
            gain[s, :, at] = a
            weight[s, :, at] = w
        return carry

    lax.fori_loop(0, TILES, body, 0)
    for n, table in enumerate((gain, weight)):
        for s in range(steps - 1):
            for i in range(0, B, 2):
                for jh in range(2):
                    put_split(
                        planes,
                        rows_of((n * (steps - 1) + s) * HG + i % HG, 2),
                        (i // HG,),
                        jnp.concatenate([table[s, :, cols(i, jh)], table[s, :, cols(i + 1, jh)]], axis=0),
                        half(jh),
                        half(2 + jh),
                    )
    edges[...] = pack_faces(planes, pack, edges.shape[0])


def chem_coarse(payc, payc_o, coarse_counts, gain, weight):
    core = lax.axis_index("fld")
    blocks = coarse_counts.shape[0]
    entries = gain.shape[0]
    shape = (entries, 4 * LANES)
    counts = jnp.ones(shape, jnp.int32)
    rows = lax.broadcasted_iota(jnp.int32, shape, 0)
    for r in range(entries):
        counts = jnp.where(rows == r, coarse_counts[r % blocks], counts)

    def body(t, carry):
        at = pl.ds(pl.multiple_of(t * 4 * LANES, 4 * LANES), 4 * LANES)
        start = pick(core, payc[1, :, at], payc_o[1, :, at])
        gain[:, at], weight[:, at] = reaction_tables(
            payc[0, :, at] + payc_o[0, :, at], start, counts
        )
        return carry

    lax.fori_loop(0, TILES // 4, body, 0)


def octant_finder(children, count_f):
    me = lax.axis_index("blk")
    devices = lax.axis_size("blk")
    found = []
    for p in range(children.shape[0]):
        for o in range(8):
            child = children[p, o]
            distance = jnp.where(child >= 0, (child // count_f - me) % devices, FAR)
            found.append((distance, child, p * 8 + o))

    def find(want):
        slot = jnp.int32(0)
        label = jnp.int32(-1)
        for distance, child, place in found:
            hit = distance == want
            slot = jnp.where(hit, place, slot)
            label = jnp.where(hit, child % count_f, label)
        return slot, label

    return find


def write_octant(state, first_slab, found, wanted_fields, out, at):
    slot, label = found
    p, a, b, c = slot // 8, slot // 4 % 2, slot // 2 % 2, slot % 2
    kept = lane_ids() % B // H == c
    for n, f in enumerate(wanted_fields):
        layers = state[first_slab + p, b, pl.ds(a * (H * 8) + f, H, stride=8), :]
        out[at + n] = jnp.where(kept, layers, 0.0)
    out[at + len(wanted_fields)] = jnp.full((H, LANES), label.astype(F32))


def slot_fields(core, fields):
    return [core * fields + v for v in range(fields)] + [0]


def keep_coarse(state, first_slab, children):
    upper = lane_ids() % B // H
    for p in range(children.shape[0]):
        for a in range(2):
            for b in range(2):
                low = jnp.where(children[p, 4 * a + 2 * b] < 0, 1.0, 0.0)
                high = jnp.where(children[p, 4 * a + 2 * b + 1] < 0, 1.0, 0.0)
                kept = jnp.where(upper == 0, low, high)
                for i in range(a * H, a * H + H):
                    at = (first_slab + p, b, rows_of(i))
                    state[at] = state[at] * kept


def fill_pack(table):
    cell = lax.broadcasted_iota(jnp.int32, (PLANE, 2 * LANES), 0)
    place = lax.broadcasted_iota(jnp.int32, (PLANE, 2 * LANES), 1)
    depth = place // B % 2
    layer = jnp.where(place < LANES, B - 1 - depth, depth)
    match = jnp.where(cell == place % B * B + layer, 1.0, 0.0)
    group = place % LANES // PACK
    for g in range(G):
        table[g] = jnp.where(group == g, match, 0.0).astype(BF16)


def start_kernel(
    sends, count_f, fields, payc, payc_o, children, coarse_counts, dif, shr, dif_o, shr_o,
    fine_nbr, coarse_nbr, coarse, gain_c, weight_c, local, *rest
):
    core = lax.axis_index("fld")
    count_c = children.shape[0]
    outs, (planes, packed, table, stage) = rest[:-4], rest[-4:]
    fill_pack(table)
    up, down = outs[-2:]
    for p in range(count_c):
        for v in range(fields):
            mine = payc[2 + v, pl.ds(p, 1), :]
            theirs = payc_o[2 + v, pl.ds(p, 1), :]
            stage[p, pl.ds(v, 1), :] = pick(core, mine, theirs)
            stage[p, pl.ds(fields + v, 1), :] = pick(core, theirs, mine)
        for i in range(B):
            for jh in range(2):
                coarse[p, jh, rows_of(i), :] = stage[p, :, cols(i, jh)]
    find = octant_finder(children, count_f)
    for out, distances in zip(outs, sends):
        write_octant(coarse, 0, find(pick(core, *distances)), list(range(2 * fields)), out, 0)
    write_octant(coarse, 0, find(0), slot_fields(core, fields), local, 0)
    chem_coarse(payc, payc_o, coarse_counts, gain_c, weight_c)
    keep_coarse(coarse, 0, children)
    react_coarse(
        coarse,
        0,
        count_c,
        spread_vector(core, (dif, shr), (dif_o, shr_o), 1, fields),
        gain_c,
        weight_c,
        gain_c.shape[0] - count_c,
    )
    build_planes(coarse, count_c, planes)
    packed[...] = pack_faces(planes, table, count_c * HG * 8)
    rows = row_ids()
    lane = lane_ids()
    faces = jnp.zeros((8, LANES), F32)
    for f in range(6):
        column = fine_nbr[:, pl.ds(f, 1)].astype(F32)
        faces = jnp.where(lane == f, jnp.broadcast_to(column, (8, LANES)), faces)
        for p in range(count_c):
            column = coarse_nbr[pl.ds(p, 1), pl.ds(f, 1)].astype(F32)
            faces = jnp.where(
                (lane == 8 + f) & (rows == p), jnp.broadcast_to(column, (8, LANES)), faces
            )
    base = 2 * fields + 1
    for n in range(count_c * HG):
        up[base + n] = packed[rows_of(n), half(0)]
        down[base + n] = packed[rows_of(n), half(1)]
    up[base + count_c * HG] = faces
    down[base + count_c * HG] = faces


def add_octants(entries, state, stage, fields):
    slots = fields + 1
    rows = row_ids()
    lane = lane_ids()
    source = jnp.zeros((8, LANES), jnp.int32)
    for d, tile in enumerate(entries):
        source = jnp.where(tile(None).astype(jnp.int32) == rows, d, source)
        for s in range(slots):
            stage[d // 8, s, pl.ds(d % 8, H, stride=8), :] = tile(s)
    lanes_of = [((H // 2 * jh + lane // B // 2) * B + lane % B // 2) for jh in range(2)]
    groups = (len(entries) + 7) // 8
    indices = []
    for g in range(groups):
        index = source - 8 * g
        indices.append((jnp.clip(index, 0, 7), (index >= 0) & (index < 8)))
    for s in range(slots):
        for i in range(H):
            got = None
            for g in range(groups):
                part = jnp.take_along_axis(
                    stage[g, s, rows_of(i), :], indices[g][0], axis=0, mode="promise_in_bounds"
                )
                part = jnp.where(indices[g][1], part, 0.0)
                got = part if got is None else got + part
            got = 0.125 * (got + roll(got, -H))
            for jh in range(2):
                wide = jnp.take_along_axis(got, lanes_of[jh], axis=1, mode="promise_in_bounds")
                for ii in range(2):
                    at = (s, jh, rows_of(2 * i + ii))
                    state[at] = state[at] + wide


def all_fields(core, fields, ref):
    def tile(s):
        if s is None:
            return ref[2 * fields]
        return ref[0] if s == fields else ref[pl.ds(core * fields + s, 1)][0]

    return tile


def own_slots(fields, ref, at=0):
    return lambda s: ref[at + (fields + 1 if s is None else s)]


def react_fine(state, fields, par, par_o, gain, weight):
    core = lax.axis_index("fld")
    share = [par[1][s] for s in range(fields)] + [pick(core, par[1][0], par_o[1][0])]
    extra = jnp.where(core == 0, 1.0, 0.0)
    for i in range(B):
        for jh in range(2):
            at = cols(i, jh)
            here = (jh, rows_of(i))
            driver = state[(fields,) + here]
            heat = weight[:, at] * driver
            grown = gain[:, at] * driver
            for s in range(fields + 1):
                value = state[(s,) + here] + share[s] * heat
                if s == 0:
                    value = value + extra * grown
                if s == fields:
                    value = value + grown
                state[(s,) + here] = value


def react_coarse(state, first_slab, count_c, shares, gain, weight, first_row):
    own = jnp.where(row_ids() == 0, 1.0, 0.0)
    for p in range(count_c):
        for i in range(B):
            for jh in range(2):
                at = cols(i, jh)
                here = (first_slab + p, jh, rows_of(i))
                value = state[here]
                driver = jnp.broadcast_to(value[0:1], (8, LANES))
                heat = weight[pl.ds(first_row + p, 1), at] * driver
                grown = gain[pl.ds(first_row + p, 1), at] * driver
                state[here] = value + shares * heat + own * grown


def links_maker(plan, faces, shift, fine_slabs):
    me = lax.axis_index("blk") + shift
    count_f, count_c = plan.count_f, plan.count_c

    def column(slab, face):
        return faces[:, face : face + 1].astype(jnp.int32)

    def column_c(slab, face):
        return faces[slab : slab + 1, 8 + face : 9 + face].astype(jnp.int32)

    fine = Links(column, me * count_f, count_f, True, 0)
    coarse = Links(column_c, me * count_c, count_c, False, fine_slabs)
    return lambda s: fine if s < fine_slabs else coarse


def strips_out(plan, r, out, faces, up_octant):
    going = plan.slabs_out
    even = lax.axis_index("blk") % 2 == 0
    build_planes(out, going, r.planes)
    r.packed[pl.ds(0, going * HG * 8), :] = pack_faces(
        r.planes, r.pack, going * HG * 8
    )

    def send(up, down):
        for n in range(going * HG):
            up[n] = r.packed[rows_of(n), half(0)]
            down[n] = r.packed[rows_of(n), half(1)]
        at = going * HG
        up[at] = faces
        down[at] = faces
        if up_octant is not None:
            up_octant(up, at + 1)
            for n in range(plan.fields + 2):
                down[at + 1 + n] = zero_tile()

    pl.when(even)(lambda: send(r.send_e, r.send_o))
    pl.when(jnp.logical_not(even))(lambda: send(r.send_o, r.send_e))


def zero_tile():
    return jnp.zeros((8, LANES), F32)


def open_kernel(plan, names, *refs):
    r = SimpleNamespace(**dict(zip(names, refs)))
    core = lax.axis_index("fld")
    fields = plan.fields
    slots = fields + 1
    count_f, count_c = plan.count_f, plan.count_c
    par, par_o = (r.dif, r.shr), (r.dif_o, r.shr_o)
    out = r.state_out
    base = 2 * fields + 1
    strip = count_c * HG

    def far(ref, ref_o, n):
        return pick(core, ref[base + n], ref_o[base + n])

    last = len(plan.sends) - 1
    below = [far(getattr(r, numbered("landed", last - 1)), getattr(r, numbered("shared", last - 1)), n) for n in range(strip + 1)]
    above = [far(getattr(r, numbered("landed", last)), getattr(r, numbered("shared", last)), n) for n in range(strip + 1)]
    own_up, own_down = r.own_up, r.own_down
    faces = own_up[base + strip]
    rates = 0.5 * spread_vector(core, par, par_o, 0, fields)

    def finish(p, i, jh, value):
        out[slots + p, jh, rows_of(i), :] = value

    diffuse(
        r.coarse,
        count_c,
        links_maker(plan, faces, 0, 0),
        links_maker(plan, below[strip], -1, 0),
        links_maker(plan, above[strip], 1, 0),
        lambda s: rates,
        lambda s, h: own_up[base + s * HG + h],
        lambda s, h: own_down[base + s * HG + h],
        lambda s, h: below[s * HG + h],
        lambda s, h: above[s * HG + h],
        r,
        r,
        finish,
    )
    find = octant_finder(r.children, count_f)
    for n, distances in enumerate(plan.later):
        write_octant(
            out, slots, find(pick(core, *distances)), list(range(2 * fields)), getattr(r, numbered("octant", n)), 0
        )
    mine = slot_fields(core, fields)
    write_octant(out, slots, find(0), mine, r.local_out, 0)
    near_octant = r.near_octant
    write_octant(out, slots, find(1), mine, near_octant, 0)
    keep_coarse(out, slots, r.children)
    react_coarse(
        out, slots, count_c, spread_vector(core, par, par_o, 1, fields), r.gain_c, r.weight_c, 0
    )
    for i in range(B):
        for jh in range(2):
            at = cols(i, jh)
            for s in range(fields):
                out[s, jh, rows_of(i), :] = r.seed_f[s, :, at]
            out[fields, jh, rows_of(i), :] = pick(core, r.seed[0, :, at], r.seed_other[0, :, at])
    entries = [own_slots(fields, r.local)]
    for n in range(last):
        entries.append(all_fields(core, fields, getattr(r, numbered("landed", n))))
        entries.append(all_fields(core, fields, getattr(r, numbered("shared", n))))
    one, two = (all_fields(core, fields, getattr(r, numbered(word, last))) for word in ("landed", "shared"))
    entries.append(lambda s: pick(core, two(s), one(s)))
    add_octants(entries, out, r.stage, fields)
    react_fine(out, fields, par, par_o, r.gain.at[plan.step], r.weight.at[plan.step])

    def up_octant(up, at):
        for n in range(slots + 1):
            up[at + n] = near_octant[n]

    strips_out(plan, r, out, faces, up_octant)


def rates_of(plan, r):
    core = lax.axis_index("fld")
    par, par_o = (r.dif, r.shr), (r.dif_o, r.shr_o)
    fields = plan.fields
    rates = [par[0][s] for s in range(fields)] + [pick(core, par[0][0], par_o[0][0])]
    return rates + [0.5 * spread_vector(core, par, par_o, 0, fields)] * plan.count_c


def by_parity(action, r):
    even = lax.axis_index("blk") % 2 == 0
    pl.when(even)(lambda: action(r.sent_e, r.sent_o, r.got_o, r.got_e))
    pl.when(jnp.logical_not(even))(lambda: action(r.sent_o, r.sent_e, r.got_e, r.got_o))


def bulk_kernel(plan, names, *refs):
    r = SimpleNamespace(**dict(zip(names, refs)))
    core = lax.axis_index("fld")
    fields = plan.fields
    slots = fields + 1
    count_c = plan.count_c
    par, par_o = (r.dif, r.shr), (r.dif_o, r.shr_o)
    slabs, arrived = plan.slabs, plan.slabs_in
    own_up, own_down = r.own_up, r.own_down

    def sort_strips(up, down, below, above):
        for n in range(arrived * HG + 1):
            own_up[n] = up[n]
            own_down[n] = down[n]

    even = lax.axis_index("blk") % 2 == 0
    pl.when(even)(lambda: sort_strips(r.sent_e, r.sent_o, None, None))
    pl.when(jnp.logical_not(even))(lambda: sort_strips(r.sent_o, r.sent_e, None, None))
    faces = own_up[arrived * HG]
    source, out = r.state, r.state_out
    if plan.late:
        late = plan.late * HG * 8
        high, low = split(r.late[pl.ds(0, late), :])
        r.ends[pl.ds(0, late), pl.ds(0, 2 * LANES)] = high
        r.ends[pl.ds(0, late), pl.ds(2 * LANES, 2 * LANES)] = low
        place_ends(r.ends, r.placed, late, r)
        source = r.whole
        for i in range(B):
            for jh in range(2):
                for s in range(slabs):
                    source[s, jh, rows_of(i), :] = r.state[s, jh, rows_of(i), :] + placed_tile(
                        r.placed, s, i, jh
                    )
                for p in range(plan.late - slots):
                    r.coarse_stage[p, :, cols(i, jh)] = r.coarse[p, jh, rows_of(i), :] + placed_tile(
                        r.placed, slots + p, i, jh
                    )
        for p in range(plan.late - slots):
            for v in range(fields):
                r.coarse_final[v, pl.ds(p, 1), :] = pick(
                    core,
                    r.coarse_stage[p, pl.ds(v, 1), :],
                    r.coarse_stage[p, pl.ds(fields + v, 1), :],
                )

    def finish(s, i, jh, value):
        if s >= slots:
            r.coarse_out[s - slots, jh, rows_of(i), :] = value
        else:
            out[s, jh, rows_of(i), :] = value

    rates = rates_of(plan, r)
    diffuse(
        source,
        slabs,
        links_maker(plan, faces, 0, slots),
        None,
        None,
        lambda s: rates[s],
        lambda s, h: own_up[s * HG + h],
        lambda s, h: own_down[s * HG + h],
        None,
        None,
        r,
        r,
        finish,
    )
    if plan.add:
        near = r.near_octant

        def take(ref):
            for n in range(slots + 1):
                near[n] = ref[plan.near_at + n]

        pl.when(even)(lambda: take(r.near_o))
        pl.when(jnp.logical_not(even))(lambda: take(r.near_e))
        entries = [own_slots(fields, r.local), own_slots(fields, near)]
        for n in range(len(plan.later)):
            entries.append(all_fields(core, fields, getattr(r, numbered("landed", n))))
            entries.append(all_fields(core, fields, getattr(r, numbered("shared", n))))
        add_octants(entries, out, r.stage, fields)
    if not plan.final:
        step = plan.step
        react_fine(out, fields, par, par_o, r.gain.at[step], r.weight.at[step])
        build_planes(out, slots, r.planes)
        r.faces_out[...] = pack_faces(r.planes, r.pack, slots * HG * 8)


def edge_kernel(plan, names, *refs):
    r = SimpleNamespace(**dict(zip(names, refs)))
    core = lax.axis_index("fld")
    fields = plan.fields
    slots = fields + 1
    par, par_o = (r.dif, r.shr), (r.dif_o, r.shr_o)
    slabs, arrived = plan.slabs, plan.slabs_in
    own_up, own_down, far_b, far_a = r.own_up, r.own_down, r.far_b, r.far_a

    def sort_strips(up, down, below, above):
        for n in range(arrived * HG + 1):
            own_up[n] = up[n]
            own_down[n] = down[n]
            far_b[n] = below[n]
            far_a[n] = above[n]

    by_parity(sort_strips, r)
    faces = own_up[arrived * HG]
    rates = rates_of(plan, r)
    near = links_maker(plan, faces, 0, slots)
    from_below = links_maker(plan, far_b[arrived * HG], -1, slots)
    from_above = links_maker(plan, far_a[arrived * HG], 1, slots)
    outer = outer_lanes()
    delta, far_first, lateral, late = r.delta, r.far_first, r.lateral, r.late

    def at_tile(ref):
        return lambda s, h: ref[s * HG + h]

    for s in range(slabs):
        for h in range(HG):
            for n, (name, ref) in enumerate((((5, 1), far_a), ((4, -1), far_b))):
                ghost = near(s).read(name, s, lambda q, ref=ref: ref[q * HG + h])
                delta[n, s * HG + h] = jnp.where(outer, rates[s] * ghost, 0.0)

    def keep_far(n, s, h, lap):
        far_first[n, s * HG + h] = rates[s] * lap

    def keep_lateral(n, s, h, lap):
        lateral[n, s * HG + h] = lap

    laplace_far(
        slabs,
        (
            (from_below, at_tile(far_b), at_tile(own_down), (5, 1)),
            (from_above, at_tile(far_a), at_tile(own_up), (4, -1)),
        ),
        r,
        r,
        keep_far,
    )
    laplace_far(
        slabs,
        ((near, at_tile(delta.at[0]), None, None), (near, at_tile(delta.at[1]), None, None)),
        r,
        SimpleNamespace(far_lhs=r.far_lhs2, far_out=r.far_out2),
        keep_lateral,
    )
    share = [par[1][s] for s in range(fields)] + [pick(core, par[1][0], par_o[1][0])]
    extra = jnp.where(core == 0, 1.0, 0.0)
    for n, (name, other) in enumerate((((5, 1), 1), ((4, -1), 0))):
        for h in range(HG):
            added = []
            for s in range(slabs):
                at = s * HG + h
                ghost = near(s).read(name, s, lambda q: far_first[other, q * HG + h])
                value = delta[n, at]
                more = 0.5 * rates[s]
                inner = more * roll(value, B)
                value = value + more * (lateral[n, at] + ghost)
                added.append(jnp.where(outer, value, inner))
            if not plan.final:
                gain = r.edges[rows_of(plan.step * HG + h), half(n)]
                weight = r.edges[rows_of((plan.steps + plan.step) * HG + h), half(n)]
                driver = added[fields]
                heat, grown = weight * driver, gain * driver
                for s in range(slots):
                    added[s] = added[s] + share[s] * heat
                added[0] = added[0] + extra * grown
                added[fields] = added[fields] + grown
            for s in range(slabs):
                late[rows_of(s * HG + h), half(n)] = added[s]
    if plan.final:
        high, low = split(late[...])
        r.ends[:, pl.ds(0, 2 * LANES)] = high
        r.ends[:, pl.ds(2 * LANES, 2 * LANES)] = low
        place_ends(r.ends, r.placed, slabs * HG * 8, r)
        for s in range(slabs):
            for i in range(B):
                for jh in range(2):
                    r.state_out[s, :, cols(i, jh)] = r.state[s, jh, rows_of(i), :] + placed_tile(
                        r.placed, s, i, jh
                    )
        return

    def send(up, down):
        for n in range(slots * HG):
            up[n] = r.faces_in[rows_of(n), half(0)] + late[rows_of(n), half(0)]
            down[n] = r.faces_in[rows_of(n), half(1)] + late[rows_of(n), half(1)]
        up[slots * HG] = faces
        down[slots * HG] = faces

    even = lax.axis_index("blk") % 2 == 0
    pl.when(even)(lambda: send(r.send_e, r.send_o))
    pl.when(jnp.logical_not(even))(lambda: send(r.send_o, r.send_e))


SCALARS = ("dif", "shr", "dif_o", "shr_o", "children", "fine_counts", "coarse_counts")
MATS = ("plane", "side", "place", "pack", "far")
MIB = 1024 * 1024
LIMIT = 60


def call(kernel, inputs, outputs, scratch, hbm=(), sems=(), limit=None, cost=1000):
    names = list(inputs) + list(outputs) + list(scratch)
    scratch = {
        name: value if value[-1] is BF16 else value + (F32,) for name, value in scratch.items()
    }
    size = sum(4 * np.prod(v.shape) for name, v in inputs.items() if name not in hbm)
    size += sum(4 * np.prod(v) for v in outputs.values())
    size += sum(4 * np.prod(v[:-1]) for v in scratch.values())

    def spec(name):
        if name in hbm:
            return HBM
        return SMEM if name in SCALARS else VMEM

    result = pl.pallas_call(
        functools.partial(kernel, names),
        out_shape=[jax.ShapeDtypeStruct(shape, F32) for shape in outputs.values()],
        in_specs=[spec(name) for name in inputs],
        out_specs=[VMEM] * len(outputs),
        scratch_shapes=[pltpu.VMEM(value[:-1], value[-1]) for value in scratch.values()]
        + [pltpu.SemaphoreType.DMA(shape) for shape in sems],
        compiler_params=pltpu.CompilerParams(vmem_limit_bytes=limit or int(size) + 12 * MIB),
        cost_estimate=pl.CostEstimate(flops=cost, bytes_accessed=cost, transcendentals=0),
    )(*inputs.values())
    return SimpleNamespace(**dict(zip(outputs, result)))


def shards(
    seed_fine,
    seed_coarse,
    saved_fine,
    saved_coarse,
    diffusion,
    species_shares,
    fine_nbr,
    coarse_nbr,
    children,
    fine_counts,
    coarse_counts,
):
    fields, count_f, cells = seed_fine.shape
    count_c = seed_coarse.shape[1]
    steps = saved_fine.shape[0]
    cycles = saved_coarse.shape[0]
    slots = fields + 1
    every = slots + count_c
    sends, later = first_sends(count_f), later_sends(count_f)
    mats = tables()
    octant_shape = (2 * fields + 1, H, LANES)
    slots_shape = (slots + 1, H, LANES)
    loaded_shape = (2 * fields + 1 + count_c * HG + 1, 8, LANES)

    def plain(kernel, *fixed):
        return lambda names, *refs: kernel(*fixed, *refs)

    def strip(slabs, more=0):
        return (slabs * HG + 1 + more, 8, LANES)

    def state_shape(slabs):
        return (slabs, 2, 8 * B, LANES)

    def work(slabs):
        rows = slabs * HG * 8
        return dict(
            first=state_shape(slabs),
            far_first=(2, slabs * HG, 8, LANES),
            sums=(G, rows, PLANE),
            ends=(rows, 4 * LANES, BF16),
            placed=(rows, G * PLANE),
            far_lhs=(2 * rows, 4 * LANES, BF16),
            far_out=(2 * rows, LANES),
        )

    def strip_work(slabs):
        return {name: strip(slabs) for name in ("far_b", "far_a", "own_up", "own_down")}

    def pack_work(slabs):
        rows = slabs * HG * 8
        return dict(
            planes=(G, rows, 2 * PLANE + 2 * LANES, BF16),
            packed=(rows, 2 * LANES),
        )

    def after(value, *before):
        return lax.optimization_barrier((value, before))[0]

    stage_work = dict(stage=(1, slots, 8 * H, LANES))
    dif_o, shr_o = core_swap(diffusion), core_swap(species_shares)
    paid = call(
        plain(mix_kernel),
        dict(
            saved_f=saved_fine,
            saved_c=saved_coarse,
            seed_f=seed_fine,
            seed_c=seed_coarse,
            shr=species_shares,
        ),
        dict(
            pay=(2 * steps + 1, count_f, cells), payc=(2 + fields, cycles * count_c, cells)
        ),
        dict(fine=saved_fine.shape, coarse=saved_coarse.shape, seeds=seed_coarse.shape),
        hbm=("saved_f", "saved_c", "seed_f", "seed_c"),
        sems=((steps,), (), (), ()),
        limit=LIMIT * MIB,
    )
    payc = paid.payc
    payc_o = core_swap(payc)
    pay, payc_o, dif_o, shr_o = lax.optimization_barrier((paid.pay, payc_o, dif_o, shr_o))
    par = dict(dif=diffusion, shr=species_shares, dif_o=dif_o, shr_o=shr_o)
    pay_o = core_swap(pay)

    loaded = [numbered("octant", n) for n in range(len(sends) - 2)] + ["up", "down"]
    started = call(
        plain(start_kernel, sends, count_f, fields),
        dict(
            payc=payc,
            payc_o=payc_o,
            children=children,
            coarse_counts=coarse_counts,
            **par,
            fine_nbr=fine_nbr,
            coarse_nbr=coarse_nbr,
        ),
        dict(
            coarse=state_shape(count_c),
            gain_c=(cycles * count_c, cells),
            weight_c=(cycles * count_c, cells),
            local=slots_shape,
            **{name: loaded_shape if name in ("up", "down") else octant_shape for name in loaded},
        ),
        dict(
            pack_work(count_c),
            table=(G, PLANE, 2 * LANES, BF16),
            coarse_stage=(count_c, 2 * fields, cells),
        ),
    )
    landed = [octant_move(getattr(started, name), d) for name, d in zip(loaded, sends)]
    chem = call(
        plain(chem_kernel),
        dict(pay=pay, pay_o=pay_o, fine_counts=fine_counts, pack=mats.pack),
        dict(
            gain=(steps, count_f, cells),
            weight=(steps, count_f, cells),
            edges=(2 * (steps - 1) * HG * 8, 2 * LANES),
        ),
        dict(planes=pack_work(2 * (steps - 1))["planes"]),
    )
    landed, (chem.gain, chem.weight, chem.edges) = lax.optimization_barrier(
        (landed, (chem.gain, chem.weight, chem.edges))
    )
    shared = [core_swap(value) for value in landed]

    def named(word, values):
        return {numbered(word, n): value for n, value in enumerate(values)}

    plan = dict(
        fields=fields,
        count_f=count_f,
        count_c=count_c,
        sends=sends,
        later=later,
        slabs_in=every,
        slabs=every,
        slabs_out=slots,
        final=False,
        add=False,
        near_at=every * HG + 1,
        late=0,
        steps=steps,
    )

    def run(kernel, changes, inputs, outputs, scratch):
        return call(
            functools.partial(kernel, SimpleNamespace(**{**plan, **changes})),
            dict(par, **vars(mats), **inputs),
            outputs,
            scratch,
        )

    def halo(made, ring=False):
        got_o = pair_swap(made.send_o, 1, ring)
        got_e = pair_swap(made.send_e, 0, ring)
        return dict(sent_o=made.send_o, got_o=got_o, sent_e=made.send_e, got_e=got_e)

    def sending(slabs, more=0):
        return dict(
            state_out=state_shape(slabs), send_e=strip(slabs, more), send_o=strip(slabs, more)
        )

    made = run(
        open_kernel,
        dict(slabs_out=every, step=steps - 1),
        dict(
            vars(chem),
            gain_c=started.gain_c,
            weight_c=started.weight_c,
            children=children,
            coarse=started.coarse,
            own_up=started.up,
            own_down=started.down,
            seed_f=seed_fine,
            seed=pay[2 * steps :],
            seed_other=pay_o[2 * steps :],
            local=started.local,
            **named("landed", landed),
            **named("shared", shared),
        ),
        dict(
            sending(every, slots + 1),
            local_out=slots_shape,
            **named("octant", [octant_shape] * len(later)),
        ),
        dict(work(count_c), **pack_work(every), **stage_work, near_octant=slots_shape),
    )
    first_halo = halo(made, True)
    landed = [octant_move(getattr(made, numbered("octant", n)), d) for n, d in enumerate(later)]
    landed, arrived_halo = lax.optimization_barrier((landed, first_halo))
    shared = [core_swap(value) for value in landed]

    def edge_work(slabs):
        rows = slabs * HG * 8
        packed = (2, slabs * HG, 8, LANES)
        return dict(
            delta=packed,
            far_first=packed,
            lateral=packed,
            far_lhs=(2 * rows, 4 * LANES, BF16),
            far_out=(2 * rows, LANES),
            far_lhs2=(2 * rows, 4 * LANES, BF16),
            far_out2=(2 * rows, LANES),
        )

    def place_work(slabs):
        rows = slabs * HG * 8
        return dict(ends=(rows, 4 * LANES, BF16), placed=(rows, G * PLANE))

    def own_strips(slabs):
        return dict(own_up=strip(slabs), own_down=strip(slabs))

    state, flown, held = made.state_out, arrived_halo, every
    local = made.local_out
    sent = dict(sent_e=made.send_e, sent_o=made.send_o)
    late, coarse, coarse_final = None, None, None
    for step in reversed(range(-1, steps - 1)):
        final = step < 0
        slabs = fields if final else held
        changes = dict(step=step, steps=steps - 1, slabs_in=held, slabs=slabs, final=final)
        inputs = dict(state=state, **sent)
        outputs = dict(state_out=state_shape(min(slabs, slots)))
        scratch = dict(work(slabs), **own_strips(held), **pack_work(slabs))
        if not final:
            inputs.update(gain=chem.gain, weight=chem.weight)
            outputs.update(faces_out=(slots * HG * 8, 2 * LANES))
        if held > slots:
            outputs.update(coarse_out=state_shape(count_c))
        if late is not None:
            before = every if coarse is not None else slabs
            inputs.update(late=late)
            scratch.update(whole=state_shape(slabs), **place_work(max(before, slabs)))
            changes.update(late=before)
            if coarse is not None:
                inputs.update(coarse=coarse)
                outputs.update(coarse_final=seed_coarse.shape)
                scratch.update(coarse_stage=(count_c, 2 * fields, cells))
        if step == steps - 3:
            inputs.update(named("landed", landed), **named("shared", shared), local=local)
            inputs.update(near_e=arrived_halo["got_e"], near_o=arrived_halo["got_o"])
            scratch.update(stage_work, near_octant=slots_shape)
            changes.update(add=True)
        bulk = run(bulk_kernel, changes, inputs, outputs, scratch)
        if coarse is not None:
            coarse_final = bulk.coarse_final
        coarse = bulk.coarse_out if held > slots else None
        inputs = dict(flown)
        scratch = dict(edge_work(slabs), **strip_work(held))
        if final:
            inputs.update(state=bulk.state_out)
            outputs = dict(state_out=seed_fine.shape)
            scratch.update(late=(slabs * HG * 8, 2 * LANES), **place_work(slabs))
        else:
            inputs.update(edges=chem.edges, faces_in=bulk.faces_out)
            outputs = dict(
                late=(slabs * HG * 8, 2 * LANES), send_e=strip(slots), send_o=strip(slots)
            )
        made = run(edge_kernel, changes, inputs, outputs, scratch)
        if final:
            break
        state, late, held = bulk.state_out, made.late, slots
        flown = halo(made)
        sent = dict(sent_e=made.send_e, sent_o=made.send_o)
    return made.state_out, coarse_final


def solution(mesh):
    return jax.shard_map(
        shards,
        mesh=mesh,
        in_specs=(
            P("fld", "blk", None),
            P("fld", "blk", None),
            P(None, "fld", "blk", None),
            P(None, "fld", "blk", None),
            P("fld"),
            P("fld"),
            P("blk", None),
            P("blk", None),
            P("blk", None),
            P("blk"),
            P("blk"),
        ),
        out_specs=(P("fld", "blk", None), P("fld", "blk", None)),
        check_vma=False,
    )
```

```python
import functools
from types import SimpleNamespace
import jax
import numpy as np
import jax.numpy as jnp
from jax import lax
from jax.experimental import pallas as pl
from jax.experimental.pallas import tpu as pltpu
from jax.sharding import PartitionSpec as P

B = 16
H = B // 2
NSUB = 4
G = 4
HG = B // G
PLANE = B * B
CYCLES = 2
LANES = 128
TILES = B**3 // LANES
PACK = LANES // G
CHEM = 4
HEAT = 0.5
ENERGY = 2.0
FAR = -(1 << 20)
VMEM = pl.BlockSpec(memory_space=pltpu.VMEM)
SMEM = pl.BlockSpec(memory_space=pltpu.SMEM)
HBM = pl.BlockSpec(memory_space=pltpu.HBM)
F32 = jnp.float32
BF16 = jnp.bfloat16


def core_swap(value):
    return lax.ppermute(value, "fld", [(0, 1), (1, 0)])


def pair_swap(value, first, ring):
    n = lax.axis_size("blk")
    pairs = []
    for i in range(n):
        other = i + 1 if (i - first) % 2 == 0 else i - 1
        for core in range(2):
            if ring or 0 <= other < n:
                pairs.append((2 * i + core, 2 * (other % n) + core))
            else:
                pairs.append((2 * i + core, 2 * i + 1 - core))
    return lax.ppermute(value, ("blk", "fld"), pairs)


def first_sends(count):
    middle = count // 2
    return list(zip(list(range(2, middle)) + [1, -1], range(middle, count)))


def later_sends(count):
    middle = count // 2 + 1
    return list(zip(range(2, middle), range(middle, count)))


def octant_move(value, distances):
    n = lax.axis_size("blk")
    pairs = []
    for i in range(n):
        for core in range(2):
            pairs.append((2 * i + core, 2 * ((i + distances[core]) % n) + core))
    return lax.ppermute(value, ("blk", "fld"), pairs)


def tables():
    cell = np.arange(PLANE)
    j, k = cell // B, cell % B
    near = np.abs(j[:, None] - j[None, :]) + np.abs(k[:, None] - k[None, :])
    plane = (near == 1).astype(np.float32)
    side = np.zeros((LANES, PLANE), np.float32)
    line = np.arange(B)
    side[line, (B - 1) * B + line] = 1
    side[LANES - B + line, line] = 1
    pack = np.zeros((G, PLANE, 2 * LANES), np.float32)
    far = np.zeros((2 * LANES, LANES), np.float32)
    for g in range(G):
        at = g * PACK + line
        for depth in range(2):
            pack[g, line * B + B - 1 - depth, at + depth * B] = 1
            pack[g, line * B + depth, LANES + at + depth * B] = 1
        far[at[:-1], at[1:]] = 1
        far[at[1:], at[:-1]] = 1
        far[at + B, at] = 1
        far[LANES + at[B - 1], at[0]] = 1
        far[LANES + at[0], at[B - 1]] = 1
    place = np.concatenate([pack[g].T for g in range(G)], axis=1)
    return SimpleNamespace(
        plane=jnp.asarray(plane, BF16),
        side=jnp.asarray(side, BF16),
        place=jnp.asarray(place, BF16),
        pack=jnp.asarray(pack, BF16),
        far=jnp.asarray(far, BF16),
    )


def lane_ids():
    return lax.broadcasted_iota(jnp.int32, (8, LANES), 1)


def row_ids():
    return lax.broadcasted_iota(jnp.int32, (8, LANES), 0)


def roll(x, steps):
    steps = steps % LANES
    return x if steps == 0 else pltpu.roll(x, steps, 1)


def cols(i, jh, width=1):
    return pl.ds((2 * i + jh) * LANES, width * LANES)


def half(jh):
    return pl.ds(jh * LANES, LANES)


def rows_of(i, count=1):
    return pl.ds(8 * i, 8 * count)


def split(x):
    high = x.astype(BF16)
    return high, (x - high.astype(F32)).astype(BF16)


def product(pairs):
    total = None
    for a, b in pairs:
        term = jnp.dot(a, b, preferred_element_type=F32)
        total = term if total is None else total + term
    return total


class Links:
    def __init__(self, column, base, count, by_rows, first_slab):
        self.count = count
        self.by_rows = by_rows
        self.column = column
        self.base = base
        self.first_slab = first_slab
        self.cache = {}

    def place(self, slab, face, shift=0):
        raw = jnp.broadcast_to(self.column(slab, face), (8, LANES))
        return jnp.where(raw >= 0, raw - (self.base + shift), FAR)

    def make(self, name, slab):
        lane = lane_ids()
        if name == "j":
            return jnp.where(lane < LANES // 2, self.place(slab, 3), self.place(slab, 2))
        if name == "j_packed":
            return jnp.where(lane % B == B - 1, self.place(slab, 2), self.place(slab, 3))
        face, step = name
        return self.place(slab, face, step * self.count)

    def index(self, name, slab):
        key = (name, None if self.by_rows else slab)
        if key not in self.cache:
            where = self.make(name, slab - self.first_slab)
            if self.by_rows:
                there = (where >= 0) & (where < self.count)
                self.cache[key] = (jnp.clip(where, 0, self.count - 1), there)
            else:
                self.cache[key] = [where == q for q in range(self.count)]
        return self.cache[key]

    def read(self, name, slab, tile):
        where = self.index(name, slab)
        if self.by_rows:
            got = jnp.take_along_axis(tile(slab), where[0], axis=0, mode="promise_in_bounds")
            return jnp.where(where[1], got, 0.0)
        result = jnp.zeros((8, LANES), F32)
        for q in range(self.count):
            result = jnp.where(where[q], tile(self.first_slab + q), result)
        return result


def put_split(ref, at, lead, value, high_at, low_at):
    high, low = split(value)
    ref[lead + (at, high_at)] = high
    ref[lead + (at, low_at)] = low


def build_planes(source, slabs, planes):
    for s in range(slabs):
        for i in range(0, B, 2):
            g, h = i // HG, i % HG
            for jh in range(2):
                put_split(
                    planes,
                    rows_of(s * HG + h, 2),
                    (g,),
                    source[s, jh, rows_of(i, 2), :],
                    half(jh),
                    half(2 + jh),
                )


def build_sides(source, slabs, near, planes):
    lane = lane_ids()
    for s in range(slabs):
        for i in range(0, B, 2):
            g, h = i // HG, i % HG
            edge = []
            for n in (i, i + 1):

                def tile(q, n=n):
                    return jnp.where(
                        lane < LANES // 2,
                        source[q, 0, rows_of(n), :],
                        source[q, 1, rows_of(n), :],
                    )

                edge.append(near(s).read("j", s, tile))
            put_split(
                planes,
                rows_of(s * HG + h, 2),
                (g,),
                jnp.concatenate(edge, axis=0),
                pl.ds(2 * PLANE, LANES),
                pl.ds(2 * PLANE + LANES, LANES),
            )


def pack_faces(planes, table, used):
    pairs = []
    for g in range(G):
        pairs.append((planes[g, pl.ds(0, used), pl.ds(0, PLANE)], table[g]))
        pairs.append((planes[g, pl.ds(0, used), pl.ds(PLANE, PLANE)], table[g]))
    return product(pairs)


def outer_lanes():
    return lane_ids() // B % 2 == 0


def place_ends(ends, placed, used, mats):
    every = pl.ds(0, used)
    for g in range(G):
        table = mats.place[:, pl.ds(g * PLANE, PLANE)]
        placed[every, pl.ds(g * PLANE, PLANE)] = product(
            [
                (ends[every, pl.ds(0, 2 * LANES)], table),
                (ends[every, pl.ds(2 * LANES, 2 * LANES)], table),
            ]
        )


def placed_tile(placed, s, i, jh):
    return placed[rows_of(s * HG + i % HG), pl.ds(i // HG * PLANE + jh * LANES, LANES)]


def laplace(source, slabs, near, up, down, below, above, mats, work, emit):
    planes, sums, ends, placed = work.planes, work.sums, work.ends, work.placed
    used = slabs * HG * 8
    outer = outer_lanes()
    for s in range(slabs):
        for h in range(0, HG, 2):
            for side in range(2):
                pieces = []
                for n in (h, h + 1):
                    if side == 0:
                        value = near(s).read((5, 0), s, lambda q, n=n: down(q, n))
                        if above is not None:
                            value = value + near(s).read((5, 1), s, lambda q, n=n: above(q, n))
                    else:
                        value = near(s).read((4, 0), s, lambda q, n=n: up(q, n))
                        if below is not None:
                            value = value + near(s).read((4, -1), s, lambda q, n=n: below(q, n))
                    pieces.append(jnp.where(outer, value, 0.0))
                put_split(
                    ends,
                    rows_of(s * HG + h, 2),
                    (),
                    jnp.concatenate(pieces, axis=0),
                    half(side),
                    half(2 + side),
                )
    every = pl.ds(0, used)
    plane, side = mats.plane[...], mats.side[...]
    for g in range(G):
        sums[g, every, :] = product(
            [
                (planes[g, every, pl.ds(0, PLANE)], plane),
                (planes[g, every, pl.ds(PLANE, PLANE)], plane),
                (planes[g, every, pl.ds(2 * PLANE, LANES)], side),
                (planes[g, every, pl.ds(2 * PLANE + LANES, LANES)], side),
            ]
        )
    place_ends(ends, placed, used, mats)
    for s in range(slabs):
        for i in range(B):
            g, h = i // HG, i % HG
            at = rows_of(s * HG + h)
            for jh in range(2):
                c = source[s, jh, rows_of(i), :]
                if i > 0:
                    before = source[s, jh, rows_of(i - 1), :]
                else:
                    before = near(s).read(
                        (0, 0), s, lambda q, jh=jh: source[q, jh, rows_of(B - 1), :]
                    )
                if i < B - 1:
                    after = source[s, jh, rows_of(i + 1), :]
                else:
                    after = near(s).read((1, 0), s, lambda q, jh=jh: source[q, jh, rows_of(0), :])
                lap = (before + after) - 6.0 * c
                lap = lap + (
                    sums[g, at, half(jh)] + placed[at, pl.ds(g * PLANE + jh * LANES, LANES)]
                )
                emit(s, i, jh, c, lap)


def laplace_far(slabs, sides, mats, work, emit):
    lhs, out = work.far_lhs, work.far_out
    group = lane_ids() // PACK
    for n, (links, tile, _, _) in enumerate(sides):
        for s in range(slabs):
            for h in range(0, HG, 2):
                c = jnp.concatenate([tile(s, h), tile(s, h + 1)], axis=0)
                edge = jnp.concatenate(
                    [
                        links(s).read("j_packed", s, lambda q, m=m: tile(q, m))
                        for m in (h, h + 1)
                    ],
                    axis=0,
                )
                at = rows_of((n * slabs + s) * HG + h, 2)
                put_split(lhs, at, (), c, half(0), half(2))
                put_split(lhs, at, (), edge, half(1), half(3))
    every = pl.ds(0, 2 * slabs * HG * 8)
    table = mats.far[...]
    out[every, :] = product(
        [
            (lhs[every, pl.ds(0, 2 * LANES)], table),
            (lhs[every, pl.ds(2 * LANES, 2 * LANES)], table),
        ]
    )
    for n, (links, tile, own, own_name) in enumerate(sides):
        for s in range(slabs):
            for h in range(HG):
                c = tile(s, h)
                if h > 0:
                    before = tile(s, h - 1)
                else:
                    wrap = links(s).read((0, 0), s, lambda q: tile(q, HG - 1))
                    before = roll(jnp.where(group == G - 1, wrap, tile(s, HG - 1)), PACK)
                if h < HG - 1:
                    after = tile(s, h + 1)
                else:
                    wrap = links(s).read((1, 0), s, lambda q: tile(q, 0))
                    after = roll(jnp.where(group == 0, wrap, tile(s, 0)), -PACK)
                lap = (before + after) + out[rows_of((n * slabs + s) * HG + h), :] - 6.0 * c
                if own is not None:
                    lap = lap + links(s).read(own_name, s, lambda q: own(q, h))
                emit(n, s, h, lap)


def diffuse(source, slabs, near, from_below, from_above, rate, up, down, below, above, mats, work, finish):
    first, packed = work.first, work.packed
    alone = below is None
    far_first = None if alone else work.far_first
    build_planes(source, slabs, work.planes)
    build_sides(source, slabs, near, work.planes)

    def keep_first(s, i, jh, c, lap):
        first[s, jh, rows_of(i), :] = rate(s) * lap

    laplace(source, slabs, near, up, down, below, above, mats, work, keep_first)

    def keep_far(n, s, h, lap):
        far_first[n, s * HG + h] = rate(s) * lap

    if not alone:
        laplace_far(
            slabs,
            ((from_below, below, down, (5, 1)), (from_above, above, up, (4, -1))),
            mats,
            work,
            keep_far,
        )
    build_planes(first, slabs, work.planes)
    build_sides(first, slabs, near, work.planes)
    packed[pl.ds(0, slabs * HG * 8), :] = pack_faces(work.planes, mats.pack, slabs * HG * 8)

    def last(s, i, jh, c, lap):
        finish(s, i, jh, source[s, jh, rows_of(i), :] + c + 0.5 * rate(s) * lap)

    laplace(
        first,
        slabs,
        near,
        lambda s, h: packed[rows_of(s * HG + h), half(0)],
        lambda s, h: packed[rows_of(s * HG + h), half(1)],
        None if alone else lambda s, h: far_first[0, s * HG + h],
        None if alone else lambda s, h: far_first[1, s * HG + h],
        mats,
        work,
        last,
    )


def numbered(word, n):
    return word + str(n)


def pick(core, a, b):
    return jnp.where(core == 0, a, b)


def spread_vector(core, own, other, row, fields):
    rows = row_ids()
    result = jnp.zeros((8, LANES), F32)
    for f in range(2 * fields):
        value = pick(core, own[row][f], other[row][f]) if f < fields else pick(
            core, other[row][f - fields], own[row][f - fields]
        )
        result = jnp.where(rows == f, value, result)
    return result


def mix_fine(saved_f, shares, pay, fine, sems):
    steps, fields = saved_f.shape[0], saved_f.shape[1]
    copies = [pltpu.make_async_copy(saved_f.at[s], fine.at[s], sems.at[s]) for s in range(steps)]
    for copy in copies:
        copy.start()
    for s in range(steps):
        copies[s].wait()
        total = shares[0] * fine[s, 0]
        for v in range(1, fields):
            total = total + shares[v] * fine[s, v]
        pay[s] = total
        pay[steps + s] = fine[s, 0]


def mix_coarse(saved_c, seed_c, shares, after, payc):
    fields, blocks = saved_c.shape[1], saved_c.shape[2]
    for c in range(saved_c.shape[0]):
        total = shares[0] * saved_c[c, 0]
        for v in range(1, fields):
            total = total + shares[v] * saved_c[c, v]
        payc[0, pl.ds(c * blocks, blocks), :] = total
        payc[1, pl.ds(c * blocks, blocks), :] = saved_c[c, 0]
    for v in range(fields):
        payc[2 + v, pl.ds(0, blocks), :] = seed_c[v]
        payc[2 + v, pl.ds(blocks, blocks), :] = seed_c[v]


def substeps(counts):
    step = HEAT / counts.astype(F32)
    return [jnp.where(n < counts, step, 0.0) for n in range(NSUB)]


def reaction_tables(mix, start, steps):
    state = start
    history = []
    for step in steps:
        inverse = 1.0 / state
        decay = jnp.exp(-ENERGY * inverse)
        rise = step * mix * decay
        history.append((step * decay, rise * (inverse * inverse)))
        state = state + rise
    passed = jnp.ones_like(start)
    weight = jnp.zeros_like(start)
    for grown, slope in reversed(history):
        weight = weight + grown * passed
        passed = passed + passed * (ENERGY * slope)
    return passed - 1.0, weight


def chem_kernel(which, pay, pay_o, fine_counts, pack, after, gain, weight, edges, planes):
    core = lax.axis_index("fld")
    every = pay.shape[0] // 2
    shape = (8, CHEM * LANES)
    rows = lax.broadcasted_iota(jnp.int32, shape, 0)
    counts = jnp.ones(shape, jnp.int32)
    for b in range(fine_counts.shape[0]):
        counts = jnp.where(rows == b, fine_counts[b], counts)
    lengths = substeps(counts)

    def body(t, carry):
        at = pl.ds(pl.multiple_of(t * CHEM * LANES, CHEM * LANES), CHEM * LANES)
        for n, s in enumerate(which):
            start = pick(core, pay[every + s, :, at], pay_o[every + s, :, at])
            a, w = reaction_tables(pay[s, :, at] + pay_o[s, :, at], start, lengths)
            gain[n, :, at] = a
            weight[n, :, at] = w
        return carry

    lax.fori_loop(0, TILES // CHEM, body, 0)
    later = [n for n, s in enumerate(which) if s < every - 1]
    for m, table in enumerate((gain, weight)):
        for order, n in enumerate(later):
            for i in range(0, B, 2):
                for jh in range(2):
                    put_split(
                        planes,
                        rows_of((m * len(later) + order) * HG + i % HG, 2),
                        (i // HG,),
                        jnp.concatenate(
                            [table[n, :, cols(i, jh)], table[n, :, cols(i + 1, jh)]], axis=0
                        ),
                        half(jh),
                        half(2 + jh),
                    )
    edges[...] = pack_faces(planes, pack, edges.shape[0])


def chem_coarse(payc, payc_o, coarse_counts, gain, weight):
    core = lax.axis_index("fld")
    blocks = coarse_counts.shape[0]
    entries = gain.shape[0]
    shape = (entries, 4 * LANES)
    counts = jnp.ones(shape, jnp.int32)
    rows = lax.broadcasted_iota(jnp.int32, shape, 0)
    for r in range(entries):
        counts = jnp.where(rows == r, coarse_counts[r % blocks], counts)
    lengths = substeps(counts)

    def body(t, carry):
        at = pl.ds(pl.multiple_of(t * 4 * LANES, 4 * LANES), 4 * LANES)
        start = pick(core, payc[1, :, at], payc_o[1, :, at])
        gain[:, at], weight[:, at] = reaction_tables(
            payc[0, :, at] + payc_o[0, :, at], start, lengths
        )
        return carry

    lax.fori_loop(0, TILES // 4, body, 0)


def octant_finder(children, count_f):
    me = lax.axis_index("blk")
    devices = lax.axis_size("blk")
    found = []
    for p in range(children.shape[0]):
        for o in range(8):
            child = children[p, o]
            distance = jnp.where(child >= 0, (child // count_f - me) % devices, FAR)
            found.append((distance, child, p * 8 + o))

    def find(want):
        slot = jnp.int32(0)
        label = jnp.int32(-1)
        for distance, child, place in found:
            hit = distance == want
            slot = jnp.where(hit, place, slot)
            label = jnp.where(hit, child % count_f, label)
        return slot, label

    return find


def write_octant(state, first_slab, found, wanted_fields, out, at):
    slot, label = found
    p, a, b, c = slot // 8, slot // 4 % 2, slot // 2 % 2, slot % 2
    kept = lane_ids() % B // H == c
    for n, f in enumerate(wanted_fields):
        layers = state[first_slab + p, b, pl.ds(a * (H * 8) + f, H, stride=8), :]
        out[at + n] = jnp.where(kept, layers, 0.0)
    out[at + len(wanted_fields)] = jnp.full((H, LANES), label.astype(F32))


def slot_fields(core, fields):
    return [core * fields + v for v in range(fields)] + [0]


def keep_coarse(state, first_slab, children):
    upper = lane_ids() % B // H
    for p in range(children.shape[0]):
        for a in range(2):
            for b in range(2):
                low = jnp.where(children[p, 4 * a + 2 * b] < 0, 1.0, 0.0)
                high = jnp.where(children[p, 4 * a + 2 * b + 1] < 0, 1.0, 0.0)
                kept = jnp.where(upper == 0, low, high)
                for i in range(a * H, a * H + H):
                    at = (first_slab + p, b, rows_of(i))
                    state[at] = state[at] * kept


def fill_pack(table):
    cell = lax.broadcasted_iota(jnp.int32, (PLANE, 2 * LANES), 0)
    place = lax.broadcasted_iota(jnp.int32, (PLANE, 2 * LANES), 1)
    depth = place // B % 2
    layer = jnp.where(place < LANES, B - 1 - depth, depth)
    match = jnp.where(cell == place % B * B + layer, 1.0, 0.0)
    group = place % LANES // PACK
    for g in range(G):
        table[g] = jnp.where(group == g, match, 0.0).astype(BF16)


def start_kernel(
    sends, count_f, fields, payc, payc_o, children, coarse_counts, dif, shr, dif_o, shr_o,
    fine_nbr, coarse_nbr, coarse, gain_c, weight_c, local, *rest
):
    core = lax.axis_index("fld")
    count_c = children.shape[0]
    outs, (planes, packed, table, stage) = rest[:-4], rest[-4:]
    fill_pack(table)
    up, down = outs[-2:]
    for p in range(count_c):
        for v in range(fields):
            mine = payc[2 + v, pl.ds(p, 1), :]
            theirs = payc_o[2 + v, pl.ds(p, 1), :]
            stage[p, pl.ds(v, 1), :] = pick(core, mine, theirs)
            stage[p, pl.ds(fields + v, 1), :] = pick(core, theirs, mine)
        for i in range(B):
            for jh in range(2):
                coarse[p, jh, rows_of(i), :] = stage[p, :, cols(i, jh)]
    find = octant_finder(children, count_f)
    for out, distances in zip(outs, sends):
        write_octant(coarse, 0, find(pick(core, *distances)), list(range(2 * fields)), out, 0)
    write_octant(coarse, 0, find(0), slot_fields(core, fields), local, 0)
    chem_coarse(payc, payc_o, coarse_counts, gain_c, weight_c)
    keep_coarse(coarse, 0, children)
    react_coarse(
        coarse,
        0,
        count_c,
        spread_vector(core, (dif, shr), (dif_o, shr_o), 1, fields),
        gain_c,
        weight_c,
        gain_c.shape[0] - count_c,
    )
    build_planes(coarse, count_c, planes)
    packed[...] = pack_faces(planes, table, count_c * HG * 8)
    rows = row_ids()
    lane = lane_ids()
    faces = jnp.zeros((8, LANES), F32)
    for f in range(6):
        column = fine_nbr[:, pl.ds(f, 1)].astype(F32)
        faces = jnp.where(lane == f, jnp.broadcast_to(column, (8, LANES)), faces)
        for p in range(count_c):
            column = coarse_nbr[pl.ds(p, 1), pl.ds(f, 1)].astype(F32)
            faces = jnp.where(
                (lane == 8 + f) & (rows == p), jnp.broadcast_to(column, (8, LANES)), faces
            )
    base = 2 * fields + 1
    for n in range(count_c * HG):
        up[base + n] = packed[rows_of(n), half(0)]
        down[base + n] = packed[rows_of(n), half(1)]
    up[base + count_c * HG] = faces
    down[base + count_c * HG] = faces


def add_octants(entries, state, stage, fields):
    slots = fields + 1
    rows = row_ids()
    lane = lane_ids()
    source = jnp.zeros((8, LANES), jnp.int32)
    for d, tile in enumerate(entries):
        source = jnp.where(tile(None).astype(jnp.int32) == rows, d, source)
        for s in range(slots):
            stage[d // 8, s, pl.ds(d % 8, H, stride=8), :] = tile(s)
    lanes_of = [((H // 2 * jh + lane // B // 2) * B + lane % B // 2) for jh in range(2)]
    groups = (len(entries) + 7) // 8
    indices = []
    for g in range(groups):
        index = source - 8 * g
        indices.append((jnp.clip(index, 0, 7), (index >= 0) & (index < 8)))
    for s in range(slots):
        for i in range(H):
            got = None
            for g in range(groups):
                part = jnp.take_along_axis(
                    stage[g, s, rows_of(i), :], indices[g][0], axis=0, mode="promise_in_bounds"
                )
                part = jnp.where(indices[g][1], part, 0.0)
                got = part if got is None else got + part
            got = 0.125 * (got + roll(got, -H))
            for jh in range(2):
                wide = jnp.take_along_axis(got, lanes_of[jh], axis=1, mode="promise_in_bounds")
                for ii in range(2):
                    at = (s, jh, rows_of(2 * i + ii))
                    state[at] = state[at] + wide


def all_fields(core, fields, ref):
    def tile(s):
        if s is None:
            return ref[2 * fields]
        return ref[0] if s == fields else ref[pl.ds(core * fields + s, 1)][0]

    return tile


def own_slots(fields, ref, at=0):
    return lambda s: ref[at + (fields + 1 if s is None else s)]


def react_fine(state, fields, par, par_o, gain, weight):
    core = lax.axis_index("fld")
    share = [par[1][s] for s in range(fields)] + [pick(core, par[1][0], par_o[1][0])]
    extra = jnp.where(core == 0, 1.0, 0.0)
    for i in range(B):
        for jh in range(2):
            at = cols(i, jh)
            here = (jh, rows_of(i))
            driver = state[(fields,) + here]
            heat = weight[:, at] * driver
            grown = gain[:, at] * driver
            for s in range(fields + 1):
                value = state[(s,) + here] + share[s] * heat
                if s == 0:
                    value = value + extra * grown
                if s == fields:
                    value = value + grown
                state[(s,) + here] = value


def react_coarse(state, first_slab, count_c, shares, gain, weight, first_row):
    own = jnp.where(row_ids() == 0, 1.0, 0.0)
    for p in range(count_c):
        for i in range(B):
            for jh in range(2):
                at = cols(i, jh)
                here = (first_slab + p, jh, rows_of(i))
                value = state[here]
                driver = jnp.broadcast_to(value[0:1], (8, LANES))
                heat = weight[pl.ds(first_row + p, 1), at] * driver
                grown = gain[pl.ds(first_row + p, 1), at] * driver
                state[here] = value + shares * heat + own * grown


def links_maker(plan, faces, shift, fine_slabs):
    me = lax.axis_index("blk") + shift
    count_f, count_c = plan.count_f, plan.count_c

    def column(slab, face):
        return faces[:, face : face + 1].astype(jnp.int32)

    def column_c(slab, face):
        return faces[slab : slab + 1, 8 + face : 9 + face].astype(jnp.int32)

    fine = Links(column, me * count_f, count_f, True, 0)
    coarse = Links(column_c, me * count_c, count_c, False, fine_slabs)
    return lambda s: fine if s < fine_slabs else coarse


def strips_out(plan, r, out, faces, up_octant):
    going = plan.slabs_out
    even = lax.axis_index("blk") % 2 == 0
    build_planes(out, going, r.planes)
    r.packed[pl.ds(0, going * HG * 8), :] = pack_faces(
        r.planes, r.pack, going * HG * 8
    )

    def send(up, down):
        for n in range(going * HG):
            up[n] = r.packed[rows_of(n), half(0)]
            down[n] = r.packed[rows_of(n), half(1)]
        at = going * HG
        up[at] = faces
        down[at] = faces
        if up_octant is not None:
            up_octant(up, at + 1)
            for n in range(plan.fields + 2):
                down[at + 1 + n] = zero_tile()

    pl.when(even)(lambda: send(r.send_e, r.send_o))
    pl.when(jnp.logical_not(even))(lambda: send(r.send_o, r.send_e))


def zero_tile():
    return jnp.zeros((8, LANES), F32)


def open_kernel(plan, names, *refs):
    r = SimpleNamespace(**dict(zip(names, refs)))
    core = lax.axis_index("fld")
    fields = plan.fields
    slots = fields + 1
    count_f, count_c = plan.count_f, plan.count_c
    par, par_o = (r.dif, r.shr), (r.dif_o, r.shr_o)
    out = r.state_out
    base = 2 * fields + 1
    strip = count_c * HG

    def far(ref, ref_o, n):
        return pick(core, ref[base + n], ref_o[base + n])

    last = len(plan.sends) - 1
    below = [far(getattr(r, numbered("landed", last - 1)), getattr(r, numbered("shared", last - 1)), n) for n in range(strip + 1)]
    above = [far(getattr(r, numbered("landed", last)), getattr(r, numbered("shared", last)), n) for n in range(strip + 1)]
    own_up, own_down = r.own_up, r.own_down
    faces = own_up[base + strip]
    rates = 0.5 * spread_vector(core, par, par_o, 0, fields)

    def finish(p, i, jh, value):
        out[slots + p, jh, rows_of(i), :] = value

    diffuse(
        r.coarse,
        count_c,
        links_maker(plan, faces, 0, 0),
        links_maker(plan, below[strip], -1, 0),
        links_maker(plan, above[strip], 1, 0),
        lambda s: rates,
        lambda s, h: own_up[base + s * HG + h],
        lambda s, h: own_down[base + s * HG + h],
        lambda s, h: below[s * HG + h],
        lambda s, h: above[s * HG + h],
        r,
        r,
        finish,
    )
    find = octant_finder(r.children, count_f)
    for n, distances in enumerate(plan.later):
        write_octant(
            out, slots, find(pick(core, *distances)), list(range(2 * fields)), getattr(r, numbered("octant", n)), 0
        )
    mine = slot_fields(core, fields)
    write_octant(out, slots, find(0), mine, r.local_out, 0)
    near_octant = r.near_octant
    write_octant(out, slots, find(1), mine, near_octant, 0)
    keep_coarse(out, slots, r.children)
    react_coarse(
        out, slots, count_c, spread_vector(core, par, par_o, 1, fields), r.gain_c, r.weight_c, 0
    )
    for i in range(B):
        for jh in range(2):
            at = cols(i, jh)
            for s in range(fields):
                out[s, jh, rows_of(i), :] = r.seed_f[s, :, at]
            out[fields, jh, rows_of(i), :] = pick(core, r.seed_f[0, :, at], r.seed_other[0, :, at])
    entries = [own_slots(fields, r.local)]
    for n in range(last):
        entries.append(all_fields(core, fields, getattr(r, numbered("landed", n))))
        entries.append(all_fields(core, fields, getattr(r, numbered("shared", n))))
    one, two = (all_fields(core, fields, getattr(r, numbered(word, last))) for word in ("landed", "shared"))
    entries.append(lambda s: pick(core, two(s), one(s)))
    add_octants(entries, out, r.stage, fields)
    react_fine(out, fields, par, par_o, r.gain.at[plan.step], r.weight.at[plan.step])

    def up_octant(up, at):
        for n in range(slots + 1):
            up[at + n] = near_octant[n]

    strips_out(plan, r, out, faces, up_octant)


def rates_of(plan, r):
    core = lax.axis_index("fld")
    par, par_o = (r.dif, r.shr), (r.dif_o, r.shr_o)
    fields = plan.fields
    rates = [par[0][s] for s in range(fields)] + [pick(core, par[0][0], par_o[0][0])]
    return rates + [0.5 * spread_vector(core, par, par_o, 0, fields)] * plan.count_c


def by_parity(action, r):
    even = lax.axis_index("blk") % 2 == 0
    pl.when(even)(lambda: action(r.sent_e, r.sent_o, r.got_o, r.got_e))
    pl.when(jnp.logical_not(even))(lambda: action(r.sent_o, r.sent_e, r.got_e, r.got_o))


def react_bulk(plan, r, out):
    slots = plan.fields + 1
    par, par_o = (r.dif, r.shr), (r.dif_o, r.shr_o)
    react_fine(out, plan.fields, par, par_o, r.gain.at[plan.step], r.weight.at[plan.step])
    build_planes(out, slots, r.planes)
    r.faces_out[...] = pack_faces(r.planes, r.pack, slots * HG * 8)


def bulk_kernel(plan, names, *refs):
    r = SimpleNamespace(**dict(zip(names, refs)))
    core = lax.axis_index("fld")
    fields = plan.fields
    slots = fields + 1
    count_c = plan.count_c
    par, par_o = (r.dif, r.shr), (r.dif_o, r.shr_o)
    slabs, arrived = plan.slabs, plan.slabs_in
    own_up, own_down = r.own_up, r.own_down

    def sort_strips(up, down, below, above):
        for n in range(arrived * HG + 1):
            own_up[n] = up[n]
            own_down[n] = down[n]

    even = lax.axis_index("blk") % 2 == 0
    pl.when(even)(lambda: sort_strips(r.sent_e, r.sent_o, None, None))
    pl.when(jnp.logical_not(even))(lambda: sort_strips(r.sent_o, r.sent_e, None, None))
    faces = own_up[arrived * HG]
    source, out = r.state, r.state_out
    if plan.late:
        late = plan.late * HG * 8
        high, low = split(r.late[pl.ds(0, late), :])
        r.ends[pl.ds(0, late), pl.ds(0, 2 * LANES)] = high
        r.ends[pl.ds(0, late), pl.ds(2 * LANES, 2 * LANES)] = low
        place_ends(r.ends, r.placed, late, r)
        source = r.whole
        for i in range(B):
            for jh in range(2):
                for s in range(slabs):
                    source[s, jh, rows_of(i), :] = r.state[s, jh, rows_of(i), :] + placed_tile(
                        r.placed, s, i, jh
                    )
                for p in range(plan.late - slots):
                    r.coarse_stage[p, :, cols(i, jh)] = r.coarse[p, jh, rows_of(i), :] + placed_tile(
                        r.placed, slots + p, i, jh
                    )
        for p in range(plan.late - slots):
            for v in range(fields):
                r.coarse_final[v, pl.ds(p, 1), :] = pick(
                    core,
                    r.coarse_stage[p, pl.ds(v, 1), :],
                    r.coarse_stage[p, pl.ds(fields + v, 1), :],
                )

    def finish(s, i, jh, value):
        if s >= slots:
            r.coarse_out[s - slots, jh, rows_of(i), :] = value
        else:
            out[s, jh, rows_of(i), :] = value

    rates = rates_of(plan, r)
    diffuse(
        source,
        slabs,
        links_maker(plan, faces, 0, slots),
        None,
        None,
        lambda s: rates[s],
        lambda s, h: own_up[s * HG + h],
        lambda s, h: own_down[s * HG + h],
        None,
        None,
        r,
        r,
        finish,
    )
    if not plan.final and not plan.pause:
        react_bulk(plan, r, out)


def resume_kernel(plan, names, *refs):
    r = SimpleNamespace(**dict(zip(names, refs)))
    core = lax.axis_index("fld")
    even = lax.axis_index("blk") % 2 == 0
    fields = plan.fields
    slots = fields + 1
    out = r.state_out
    out[...] = r.state[...]
    near = r.near_octant

    def take(ref):
        for n in range(slots + 1):
            near[n] = ref[plan.near_at + n]

    pl.when(even)(lambda: take(r.near_o))
    pl.when(jnp.logical_not(even))(lambda: take(r.near_e))
    entries = [own_slots(fields, r.local), own_slots(fields, near)]
    for n in range(len(plan.later)):
        entries.append(all_fields(core, fields, getattr(r, numbered("landed", n))))
        entries.append(own_slots(fields, r.shared, n * (slots + 1)))
    add_octants(entries, out, r.stage, fields)
    react_bulk(plan, r, out)


def edge_kernel(plan, names, *refs):
    sems = refs[-1]
    r = SimpleNamespace(**dict(zip(names, refs)))
    core = lax.axis_index("fld")
    fields = plan.fields
    slots = fields + 1
    par, par_o = (r.dif, r.shr), (r.dif_o, r.shr_o)
    slabs, arrived = plan.slabs, plan.slabs_in
    own_up, own_down, far_b, far_a = r.own_up, r.own_down, r.far_b, r.far_a

    def sort_strips(up, down, below, above):
        for n in range(arrived * HG + 1):
            own_up[n] = up[n]
            own_down[n] = down[n]
            far_b[n] = below[n]
            far_a[n] = above[n]

    by_parity(sort_strips, r)
    if plan.share:
        for n in range(len(plan.later)):
            tile = all_fields(1 - core, fields, getattr(r, numbered("landed", n)))
            for s in range(slots):
                r.shared[n * (slots + 1) + s] = tile(s)
            r.shared[n * (slots + 1) + slots] = tile(None)
    faces = own_up[arrived * HG]
    rates = rates_of(plan, r)
    near = links_maker(plan, faces, 0, slots)
    from_below = links_maker(plan, far_b[arrived * HG], -1, slots)
    from_above = links_maker(plan, far_a[arrived * HG], 1, slots)
    outer = outer_lanes()
    delta, far_first, lateral, late = r.delta, r.far_first, r.lateral, r.late

    def at_tile(ref):
        return lambda s, h: ref[s * HG + h]

    for s in range(slabs):
        for h in range(HG):
            for n, (name, ref) in enumerate((((5, 1), far_a), ((4, -1), far_b))):
                ghost = near(s).read(name, s, lambda q, ref=ref: ref[q * HG + h])
                delta[n, s * HG + h] = jnp.where(outer, rates[s] * ghost, 0.0)

    def keep_far(n, s, h, lap):
        far_first[n, s * HG + h] = rates[s] * lap

    def keep_lateral(n, s, h, lap):
        lateral[n, s * HG + h] = lap

    laplace_far(
        slabs,
        (
            (from_below, at_tile(far_b), at_tile(own_down), (5, 1)),
            (from_above, at_tile(far_a), at_tile(own_up), (4, -1)),
        ),
        r,
        r,
        keep_far,
    )
    laplace_far(
        slabs,
        ((near, at_tile(delta.at[0]), None, None), (near, at_tile(delta.at[1]), None, None)),
        r,
        SimpleNamespace(far_lhs=r.far_lhs2, far_out=r.far_out2),
        keep_lateral,
    )
    share = [par[1][s] for s in range(fields)] + [pick(core, par[1][0], par_o[1][0])]
    extra = jnp.where(core == 0, 1.0, 0.0)
    for n, (name, other) in enumerate((((5, 1), 1), ((4, -1), 0))):
        for h in range(HG):
            added = []
            for s in range(slabs):
                at = s * HG + h
                ghost = near(s).read(name, s, lambda q: far_first[other, q * HG + h])
                value = delta[n, at]
                more = 0.5 * rates[s]
                inner = more * roll(value, B)
                value = value + more * (lateral[n, at] + ghost)
                added.append(jnp.where(outer, value, inner))
            if not plan.final:
                gain = r.edges[rows_of(plan.step * HG + h), half(n)]
                weight = r.edges[rows_of((plan.packed + plan.step) * HG + h), half(n)]
                driver = added[fields]
                heat, grown = weight * driver, gain * driver
                for s in range(slots):
                    added[s] = added[s] + share[s] * heat
                added[0] = added[0] + extra * grown
                added[fields] = added[fields] + grown
            for s in range(slabs):
                late[rows_of(s * HG + h), half(n)] = added[s]
    if plan.final:
        high, low = split(late[...])
        r.ends[:, pl.ds(0, 2 * LANES)] = high
        r.ends[:, pl.ds(2 * LANES, 2 * LANES)] = low
        place_ends(r.ends, r.placed, slabs * HG * 8, r)
        copies = []
        for s in range(slabs):
            for i in range(B):
                for jh in range(2):
                    r.result[s, :, cols(i, jh)] = r.state[s, jh, rows_of(i), :] + placed_tile(
                        r.placed, s, i, jh
                    )
            copies.append(pltpu.make_async_copy(r.result.at[s], r.state_out.at[s], sems.at[s]))
            copies[s].start()
        for copy in copies:
            copy.wait()
        return

    def send(up, down):
        for n in range(slots * HG):
            up[n] = r.faces_in[rows_of(n), half(0)] + late[rows_of(n), half(0)]
            down[n] = r.faces_in[rows_of(n), half(1)] + late[rows_of(n), half(1)]
        up[slots * HG] = faces
        down[slots * HG] = faces

    even = lax.axis_index("blk") % 2 == 0
    pl.when(even)(lambda: send(r.send_e, r.send_o))
    pl.when(jnp.logical_not(even))(lambda: send(r.send_o, r.send_e))


SCALARS = ("dif", "shr", "dif_o", "shr_o", "children", "fine_counts", "coarse_counts")
MATS = ("plane", "side", "place", "pack", "far")
MIB = 1024 * 1024
LIMIT = 51


def call(kernel, inputs, outputs, scratch, hbm=(), sems=(), limit=None, cost=1000):
    names = list(inputs) + list(outputs) + list(scratch)
    scratch = {
        name: value if value[-1] is BF16 else value + (F32,) for name, value in scratch.items()
    }
    size = sum(4 * np.prod(v.shape) for name, v in inputs.items() if name not in hbm)
    size += sum(4 * np.prod(v) for v in outputs.values())
    size += sum(4 * np.prod(v[:-1]) for v in scratch.values())

    def spec(name):
        if name in hbm:
            return HBM
        return SMEM if name in SCALARS else VMEM

    result = pl.pallas_call(
        functools.partial(kernel, names),
        out_shape=[jax.ShapeDtypeStruct(shape, F32) for shape in outputs.values()],
        in_specs=[spec(name) for name in inputs],
        out_specs=[spec(name) for name in outputs],
        scratch_shapes=[pltpu.VMEM(value[:-1], value[-1]) for value in scratch.values()]
        + [pltpu.SemaphoreType.DMA(shape) for shape in sems],
        compiler_params=pltpu.CompilerParams(vmem_limit_bytes=limit or int(size) + 12 * MIB),
        cost_estimate=pl.CostEstimate(flops=cost, bytes_accessed=cost, transcendentals=0),
    )(*inputs.values())
    return SimpleNamespace(**dict(zip(outputs, result)))


def shards(
    seed_fine,
    seed_coarse,
    saved_fine,
    saved_coarse,
    diffusion,
    species_shares,
    fine_nbr,
    coarse_nbr,
    children,
    fine_counts,
    coarse_counts,
):
    fields, count_f, cells = seed_fine.shape
    count_c = seed_coarse.shape[1]
    steps = saved_fine.shape[0]
    cycles = saved_coarse.shape[0]
    slots = fields + 1
    every = slots + count_c
    sends, later = first_sends(count_f), later_sends(count_f)
    mats = tables()
    octant_shape = (2 * fields + 1, H, LANES)
    slots_shape = (slots + 1, H, LANES)
    loaded_shape = (2 * fields + 1 + count_c * HG + 1, 8, LANES)

    def plain(kernel, *fixed):
        return lambda names, *refs: kernel(*fixed, *refs)

    def strip(slabs, more=0):
        return (slabs * HG + 1 + more, 8, LANES)

    def state_shape(slabs):
        return (slabs, 2, 8 * B, LANES)

    def work(slabs):
        rows = slabs * HG * 8
        return dict(
            first=state_shape(slabs),
            far_first=(2, slabs * HG, 8, LANES),
            sums=(G, rows, PLANE),
            ends=(rows, 4 * LANES, BF16),
            placed=(rows, G * PLANE),
            far_lhs=(2 * rows, 4 * LANES, BF16),
            far_out=(2 * rows, LANES),
        )

    def strip_work(slabs):
        return {name: strip(slabs) for name in ("far_b", "far_a", "own_up", "own_down")}

    def pack_work(slabs):
        rows = slabs * HG * 8
        return dict(
            planes=(G, rows, 2 * PLANE + 2 * LANES, BF16),
            packed=(rows, 2 * LANES),
        )

    def after(value, *before):
        return lax.optimization_barrier((value, before))[0]

    stage_work = dict(stage=(1, slots, 8 * H, LANES))
    dif_o, shr_o = core_swap(diffusion), core_swap(species_shares)
    pay = call(
        plain(mix_fine),
        dict(saved_f=saved_fine, shr=species_shares),
        dict(pay=(2 * steps, count_f, cells)),
        dict(fine=saved_fine.shape),
        hbm=("saved_f",),
        sems=((steps,),),
        limit=LIMIT * MIB,
    ).pay
    payc = call(
        plain(mix_coarse),
        dict(saved_c=saved_coarse, seed_c=seed_coarse, shr=species_shares, after=pay),
        dict(payc=(2 + fields, cycles * count_c, cells)),
        {},
        hbm=("after",),
    ).payc
    payc_o = core_swap(payc)
    pay, sown, payc_o, dif_o, shr_o = lax.optimization_barrier(
        (pay, seed_fine, payc_o, dif_o, shr_o)
    )
    par = dict(dif=diffusion, shr=species_shares, dif_o=dif_o, shr_o=shr_o)
    pay_o, seed_o = core_swap(pay), core_swap(sown)

    loaded = [numbered("octant", n) for n in range(len(sends) - 2)] + ["up", "down"]
    started = call(
        plain(start_kernel, sends, count_f, fields),
        dict(
            payc=payc,
            payc_o=payc_o,
            children=children,
            coarse_counts=coarse_counts,
            **par,
            fine_nbr=fine_nbr,
            coarse_nbr=coarse_nbr,
        ),
        dict(
            coarse=state_shape(count_c),
            gain_c=(cycles * count_c, cells),
            weight_c=(cycles * count_c, cells),
            local=slots_shape,
            **{name: loaded_shape if name in ("up", "down") else octant_shape for name in loaded},
        ),
        dict(
            pack_work(count_c),
            table=(G, PLANE, 2 * LANES, BF16),
            coarse_stage=(count_c, 2 * fields, cells),
        ),
    )
    landed = [octant_move(getattr(started, name), d) for name, d in zip(loaded, sends)]
    def chem_of(which, before):
        packed = 2 * sum(step < steps - 1 for step in which)
        return call(
            plain(chem_kernel, which),
            dict(pay=pay, pay_o=pay_o, fine_counts=fine_counts, pack=mats.pack, after=before),
            dict(
                gain=(len(which), count_f, cells),
                weight=(len(which), count_f, cells),
                edges=(packed * HG * 8, 2 * LANES),
            ),
            dict(planes=pack_work(packed)["planes"]),
            hbm=("after",),
        )

    chem = chem_of(tuple(range(steps)), payc)
    landed, (chem.gain, chem.weight, chem.edges) = lax.optimization_barrier(
        (landed, (chem.gain, chem.weight, chem.edges))
    )
    shared = [core_swap(value) for value in landed]

    def named(word, values):
        return {numbered(word, n): value for n, value in enumerate(values)}

    plan = dict(
        fields=fields,
        count_f=count_f,
        count_c=count_c,
        sends=sends,
        later=later,
        slabs_in=every,
        slabs=every,
        slabs_out=slots,
        final=False,
        add=False,
        near_at=every * HG + 1,
        late=0,
        share=False,
        pause=False,
        packed=0,
    )

    def run(kernel, changes, inputs, outputs, scratch, **more):
        return call(
            functools.partial(kernel, SimpleNamespace(**{**plan, **changes})),
            dict(par, **vars(mats), **inputs),
            outputs,
            scratch,
            **more,
        )

    def halo(made, ring=False):
        got_o = pair_swap(made.send_o, 1, ring)
        got_e = pair_swap(made.send_e, 0, ring)
        return dict(sent_o=made.send_o, got_o=got_o, sent_e=made.send_e, got_e=got_e)

    def sending(slabs, more=0):
        return dict(
            state_out=state_shape(slabs), send_e=strip(slabs, more), send_o=strip(slabs, more)
        )

    made = run(
        open_kernel,
        dict(slabs_out=every, step=steps - 1),
        dict(
            gain=chem.gain,
            weight=chem.weight,
            gain_c=started.gain_c,
            weight_c=started.weight_c,
            children=children,
            coarse=started.coarse,
            own_up=started.up,
            own_down=started.down,
            seed_f=seed_fine,
            seed_other=seed_o,
            local=started.local,
            **named("landed", landed),
            **named("shared", shared),
        ),
        dict(
            sending(every, slots + 1),
            local_out=slots_shape,
            **named("octant", [octant_shape] * len(later)),
        ),
        dict(work(count_c), **pack_work(every), **stage_work, near_octant=slots_shape),
    )
    first_halo = halo(made, True)
    landed = [octant_move(getattr(made, numbered("octant", n)), d) for n, d in enumerate(later)]
    landed, arrived_halo = lax.optimization_barrier((landed, first_halo))

    def edge_work(slabs):
        rows = slabs * HG * 8
        packed = (2, slabs * HG, 8, LANES)
        return dict(
            delta=packed,
            far_first=packed,
            lateral=packed,
            far_lhs=(2 * rows, 4 * LANES, BF16),
            far_out=(2 * rows, LANES),
            far_lhs2=(2 * rows, 4 * LANES, BF16),
            far_out2=(2 * rows, LANES),
        )

    def place_work(slabs):
        rows = slabs * HG * 8
        return dict(ends=(rows, 4 * LANES, BF16), placed=(rows, G * PLANE))

    def own_strips(slabs):
        return dict(own_up=strip(slabs), own_down=strip(slabs))

    state, flown, held = made.state_out, arrived_halo, every
    local = made.local_out
    sent = dict(sent_e=made.send_e, sent_o=made.send_o)
    late, coarse, coarse_final = None, None, None
    for step in reversed(range(-1, steps - 1)):
        final = step < 0
        slabs = fields if final else held
        changes = dict(step=step, packed=steps - 1)
        changes.update(slabs_in=held, slabs=slabs, final=final)
        inputs = dict(state=state, **sent)
        outputs = dict(state_out=state_shape(min(slabs, slots)))
        scratch = dict(work(slabs), **own_strips(held), **pack_work(slabs))
        if not final:
            inputs.update(gain=chem.gain, weight=chem.weight)
            outputs.update(faces_out=(slots * HG * 8, 2 * LANES))
        if held > slots:
            outputs.update(coarse_out=state_shape(count_c))
        if late is not None:
            before = every if coarse is not None else slabs
            inputs.update(late=late)
            scratch.update(whole=state_shape(slabs), **place_work(max(before, slabs)))
            changes.update(late=before)
            if coarse is not None:
                inputs.update(coarse=coarse)
                outputs.update(coarse_final=seed_coarse.shape)
                scratch.update(coarse_stage=(count_c, 2 * fields, cells))
        paused = step == steps - 3
        if paused:
            for name in ("gain", "weight"):
                inputs.pop(name)
            outputs.pop("faces_out")
            changes.update(pause=True)
        bulk = run(bulk_kernel, changes, inputs, outputs, scratch)
        if paused:
            whole = run(
                resume_kernel,
                changes,
                dict(
                    state=bulk.state_out,
                    gain=chem.gain,
                    weight=chem.weight,
                    near_e=arrived_halo["got_e"],
                    near_o=arrived_halo["got_o"],
                    local=local,
                    shared=shared,
                    **named("landed", landed),
                ),
                dict(state_out=state_shape(slots), faces_out=(slots * HG * 8, 2 * LANES)),
                dict(pack_work(slots), **stage_work, near_octant=slots_shape),
            )
            bulk.state_out, bulk.faces_out = whole.state_out, whole.faces_out
        if coarse is not None:
            coarse_final = bulk.coarse_final
        coarse = bulk.coarse_out if held > slots else None
        inputs = dict(flown)
        scratch = dict(edge_work(slabs), **strip_work(held))
        if final:
            inputs.update(state=bulk.state_out)
            outputs = dict(state_out=seed_fine.shape)
            scratch.update(
                late=(slabs * HG * 8, 2 * LANES), result=seed_fine.shape, **place_work(slabs)
            )
        else:
            inputs.update(edges=chem.edges, faces_in=bulk.faces_out)
            outputs = dict(
                late=(slabs * HG * 8, 2 * LANES), send_e=strip(slots), send_o=strip(slots)
            )
        if step == steps - 2:
            inputs.update(named("landed", landed))
            outputs.update(shared=(len(later) * (slots + 1), 8, LANES))
            changes.update(share=True)
        more = dict(hbm=("state_out",), sems=((fields,),)) if final else {}
        made = run(edge_kernel, changes, inputs, outputs, scratch, **more)
        if step == steps - 2:
            shared = core_swap(made.shared)
        if final:
            break
        state, late, held = bulk.state_out, made.late, slots
        flown = halo(made)
        sent = dict(sent_e=made.send_e, sent_o=made.send_o)
    return made.state_out, coarse_final


def solution(mesh):
    return jax.shard_map(
        shards,
        mesh=mesh,
        in_specs=(
            P("fld", "blk", None),
            P("fld", "blk", None),
            P(None, "fld", "blk", None),
            P(None, "fld", "blk", None),
            P("fld"),
            P("fld"),
            P("blk", None),
            P("blk", None),
            P("blk", None),
            P("blk"),
            P("blk"),
        ),
        out_specs=(P("fld", "blk", None), P("fld", "blk", None)),
        check_vma=False,
    )
```

```python
import functools
from types import SimpleNamespace
import jax
import numpy as np
import jax.numpy as jnp
from jax import lax
from jax.experimental import pallas as pl
from jax.experimental.pallas import tpu as pltpu
from jax.sharding import PartitionSpec as P

B = 16
H = B // 2
NSUB = 4
G = 4
HG = B // G
PLANE = B * B
CYCLES = 2
LANES = 128
TILES = B**3 // LANES
PACK = LANES // G
CHEM = 4
HEAT = 0.5
ENERGY = 2.0
FAR = -(1 << 20)
VMEM = pl.BlockSpec(memory_space=pltpu.VMEM)
SMEM = pl.BlockSpec(memory_space=pltpu.SMEM)
HBM = pl.BlockSpec(memory_space=pltpu.HBM)
F32 = jnp.float32
BF16 = jnp.bfloat16


def core_swap(value):
    return lax.ppermute(value, "fld", [(0, 1), (1, 0)])


def pair_swap(value, first, ring):
    n = lax.axis_size("blk")
    pairs = []
    for i in range(n):
        other = i + 1 if (i - first) % 2 == 0 else i - 1
        for core in range(2):
            if ring or 0 <= other < n:
                pairs.append((2 * i + core, 2 * (other % n) + core))
            else:
                pairs.append((2 * i + core, 2 * i + 1 - core))
    return lax.ppermute(value, ("blk", "fld"), pairs)


def first_sends(count):
    middle = count // 2
    return list(zip(list(range(2, middle)) + [1, -1], range(middle, count)))


def later_sends(count):
    middle = count // 2 + 1
    return list(zip(range(2, middle), range(middle, count)))


def octant_move(value, distances):
    n = lax.axis_size("blk")
    pairs = []
    for i in range(n):
        for core in range(2):
            pairs.append((2 * i + core, 2 * ((i + distances[core]) % n) + core))
    return lax.ppermute(value, ("blk", "fld"), pairs)


def tables():
    cell = np.arange(PLANE)
    j, k = cell // B, cell % B
    near = np.abs(j[:, None] - j[None, :]) + np.abs(k[:, None] - k[None, :])
    plane = (near == 1).astype(np.float32)
    side = np.zeros((LANES, PLANE), np.float32)
    line = np.arange(B)
    side[line, (B - 1) * B + line] = 1
    side[LANES - B + line, line] = 1
    pack = np.zeros((G, PLANE, 2 * LANES), np.float32)
    far = np.zeros((2 * LANES, LANES), np.float32)
    for g in range(G):
        at = g * PACK + line
        for depth in range(2):
            pack[g, line * B + B - 1 - depth, at + depth * B] = 1
            pack[g, line * B + depth, LANES + at + depth * B] = 1
        far[at[:-1], at[1:]] = 1
        far[at[1:], at[:-1]] = 1
        far[at + B, at] = 1
        far[LANES + at[B - 1], at[0]] = 1
        far[LANES + at[0], at[B - 1]] = 1
    place = np.concatenate([pack[g].T for g in range(G)], axis=1)
    return SimpleNamespace(
        plane=jnp.asarray(plane, BF16),
        side=jnp.asarray(side, BF16),
        place=jnp.asarray(place, BF16),
        pack=jnp.asarray(pack, BF16),
        far=jnp.asarray(far, BF16),
    )


def lane_ids():
    return lax.broadcasted_iota(jnp.int32, (8, LANES), 1)


def row_ids():
    return lax.broadcasted_iota(jnp.int32, (8, LANES), 0)


def roll(x, steps):
    steps = steps % LANES
    return x if steps == 0 else pltpu.roll(x, steps, 1)


def cols(i, jh, width=1):
    return pl.ds((2 * i + jh) * LANES, width * LANES)


def half(jh):
    return pl.ds(jh * LANES, LANES)


def rows_of(i, count=1):
    return pl.ds(8 * i, 8 * count)


def split(x):
    high = x.astype(BF16)
    return high, (x - high.astype(F32)).astype(BF16)


def product(pairs):
    total = None
    for a, b in pairs:
        term = jnp.dot(a, b, preferred_element_type=F32)
        total = term if total is None else total + term
    return total


class Links:
    def __init__(self, column, base, count, by_rows, first_slab):
        self.count = count
        self.by_rows = by_rows
        self.column = column
        self.base = base
        self.first_slab = first_slab
        self.cache = {}

    def place(self, slab, face, shift=0):
        raw = jnp.broadcast_to(self.column(slab, face), (8, LANES))
        return jnp.where(raw >= 0, raw - (self.base + shift), FAR)

    def make(self, name, slab):
        lane = lane_ids()
        if name == "j":
            return jnp.where(lane < LANES // 2, self.place(slab, 3), self.place(slab, 2))
        if name == "j_packed":
            return jnp.where(lane % B == B - 1, self.place(slab, 2), self.place(slab, 3))
        face, step = name
        return self.place(slab, face, step * self.count)

    def index(self, name, slab):
        key = (name, None if self.by_rows else slab)
        if key not in self.cache:
            where = self.make(name, slab - self.first_slab)
            if self.by_rows:
                there = (where >= 0) & (where < self.count)
                self.cache[key] = (jnp.clip(where, 0, self.count - 1), there)
            else:
                self.cache[key] = [where == q for q in range(self.count)]
        return self.cache[key]

    def read(self, name, slab, tile):
        where = self.index(name, slab)
        if self.by_rows:
            got = jnp.take_along_axis(tile(slab), where[0], axis=0, mode="promise_in_bounds")
            return jnp.where(where[1], got, 0.0)
        result = jnp.zeros((8, LANES), F32)
        for q in range(self.count):
            result = jnp.where(where[q], tile(self.first_slab + q), result)
        return result


def put_split(ref, at, lead, value, high_at, low_at):
    high, low = split(value)
    ref[lead + (at, high_at)] = high
    ref[lead + (at, low_at)] = low


def build_planes(source, slabs, planes):
    for s in range(slabs):
        for i in range(0, B, 2):
            g, h = i // HG, i % HG
            for jh in range(2):
                put_split(
                    planes,
                    rows_of(s * HG + h, 2),
                    (g,),
                    source[s, jh, rows_of(i, 2), :],
                    half(jh),
                    half(2 + jh),
                )


def build_sides(source, slabs, near, planes):
    lane = lane_ids()
    for s in range(slabs):
        for i in range(0, B, 2):
            g, h = i // HG, i % HG
            edge = []
            for n in (i, i + 1):

                def tile(q, n=n):
                    return jnp.where(
                        lane < LANES // 2,
                        source[q, 0, rows_of(n), :],
                        source[q, 1, rows_of(n), :],
                    )

                edge.append(near(s).read("j", s, tile))
            put_split(
                planes,
                rows_of(s * HG + h, 2),
                (g,),
                jnp.concatenate(edge, axis=0),
                pl.ds(2 * PLANE, LANES),
                pl.ds(2 * PLANE + LANES, LANES),
            )


def pack_faces(planes, table, used):
    pairs = []
    for g in range(G):
        pairs.append((planes[g, pl.ds(0, used), pl.ds(0, PLANE)], table[g]))
        pairs.append((planes[g, pl.ds(0, used), pl.ds(PLANE, PLANE)], table[g]))
    return product(pairs)


def outer_lanes():
    return lane_ids() // B % 2 == 0


def place_ends(ends, placed, used, mats):
    every = pl.ds(0, used)
    for g in range(G):
        table = mats.place[:, pl.ds(g * PLANE, PLANE)]
        placed[every, pl.ds(g * PLANE, PLANE)] = product(
            [
                (ends[every, pl.ds(0, 2 * LANES)], table),
                (ends[every, pl.ds(2 * LANES, 2 * LANES)], table),
            ]
        )


def placed_tile(placed, s, i, jh):
    return placed[rows_of(s * HG + i % HG), pl.ds(i // HG * PLANE + jh * LANES, LANES)]


def laplace(source, slabs, near, up, down, below, above, mats, work, emit):
    planes, sums, ends, placed = work.planes, work.sums, work.ends, work.placed
    used = slabs * HG * 8
    outer = outer_lanes()
    for s in range(slabs):
        for h in range(0, HG, 2):
            for side in range(2):
                pieces = []
                for n in (h, h + 1):
                    if side == 0:
                        value = near(s).read((5, 0), s, lambda q, n=n: down(q, n))
                        if above is not None:
                            value = value + near(s).read((5, 1), s, lambda q, n=n: above(q, n))
                    else:
                        value = near(s).read((4, 0), s, lambda q, n=n: up(q, n))
                        if below is not None:
                            value = value + near(s).read((4, -1), s, lambda q, n=n: below(q, n))
                    pieces.append(jnp.where(outer, value, 0.0))
                put_split(
                    ends,
                    rows_of(s * HG + h, 2),
                    (),
                    jnp.concatenate(pieces, axis=0),
                    half(side),
                    half(2 + side),
                )
    every = pl.ds(0, used)
    plane, side = mats.plane[...], mats.side[...]
    for g in range(G):
        sums[g, every, :] = product(
            [
                (planes[g, every, pl.ds(0, PLANE)], plane),
                (planes[g, every, pl.ds(PLANE, PLANE)], plane),
                (planes[g, every, pl.ds(2 * PLANE, LANES)], side),
                (planes[g, every, pl.ds(2 * PLANE + LANES, LANES)], side),
            ]
        )
    place_ends(ends, placed, used, mats)
    for s in range(slabs):
        for i in range(B):
            g, h = i // HG, i % HG
            at = rows_of(s * HG + h)
            for jh in range(2):
                c = source[s, jh, rows_of(i), :]
                if i > 0:
                    before = source[s, jh, rows_of(i - 1), :]
                else:
                    before = near(s).read(
                        (0, 0), s, lambda q, jh=jh: source[q, jh, rows_of(B - 1), :]
                    )
                if i < B - 1:
                    after = source[s, jh, rows_of(i + 1), :]
                else:
                    after = near(s).read((1, 0), s, lambda q, jh=jh: source[q, jh, rows_of(0), :])
                lap = (before + after) - 6.0 * c
                lap = lap + (
                    sums[g, at, half(jh)] + placed[at, pl.ds(g * PLANE + jh * LANES, LANES)]
                )
                emit(s, i, jh, c, lap)


def laplace_far(slabs, sides, mats, work, emit):
    lhs, out = work.far_lhs, work.far_out
    group = lane_ids() // PACK
    for n, (links, tile, _, _) in enumerate(sides):
        for s in range(slabs):
            for h in range(0, HG, 2):
                c = jnp.concatenate([tile(s, h), tile(s, h + 1)], axis=0)
                edge = jnp.concatenate(
                    [
                        links(s).read("j_packed", s, lambda q, m=m: tile(q, m))
                        for m in (h, h + 1)
                    ],
                    axis=0,
                )
                at = rows_of((n * slabs + s) * HG + h, 2)
                put_split(lhs, at, (), c, half(0), half(2))
                put_split(lhs, at, (), edge, half(1), half(3))
    every = pl.ds(0, 2 * slabs * HG * 8)
    table = mats.far[...]
    out[every, :] = product(
        [
            (lhs[every, pl.ds(0, 2 * LANES)], table),
            (lhs[every, pl.ds(2 * LANES, 2 * LANES)], table),
        ]
    )
    for n, (links, tile, own, own_name) in enumerate(sides):
        for s in range(slabs):
            for h in range(HG):
                c = tile(s, h)
                if h > 0:
                    before = tile(s, h - 1)
                else:
                    wrap = links(s).read((0, 0), s, lambda q: tile(q, HG - 1))
                    before = roll(jnp.where(group == G - 1, wrap, tile(s, HG - 1)), PACK)
                if h < HG - 1:
                    after = tile(s, h + 1)
                else:
                    wrap = links(s).read((1, 0), s, lambda q: tile(q, 0))
                    after = roll(jnp.where(group == 0, wrap, tile(s, 0)), -PACK)
                lap = (before + after) + out[rows_of((n * slabs + s) * HG + h), :] - 6.0 * c
                if own is not None:
                    lap = lap + links(s).read(own_name, s, lambda q: own(q, h))
                emit(n, s, h, lap)


def diffuse(source, slabs, near, from_below, from_above, rate, up, down, below, above, mats, work, finish):
    first, packed = work.first, work.packed
    alone = below is None
    far_first = None if alone else work.far_first
    build_planes(source, slabs, work.planes)
    build_sides(source, slabs, near, work.planes)

    def keep_first(s, i, jh, c, lap):
        first[s, jh, rows_of(i), :] = rate(s) * lap

    laplace(source, slabs, near, up, down, below, above, mats, work, keep_first)

    def keep_far(n, s, h, lap):
        far_first[n, s * HG + h] = rate(s) * lap

    if not alone:
        laplace_far(
            slabs,
            ((from_below, below, down, (5, 1)), (from_above, above, up, (4, -1))),
            mats,
            work,
            keep_far,
        )
    build_planes(first, slabs, work.planes)
    build_sides(first, slabs, near, work.planes)
    packed[pl.ds(0, slabs * HG * 8), :] = pack_faces(work.planes, mats.pack, slabs * HG * 8)

    def last(s, i, jh, c, lap):
        finish(s, i, jh, source[s, jh, rows_of(i), :] + c + 0.5 * rate(s) * lap)

    laplace(
        first,
        slabs,
        near,
        lambda s, h: packed[rows_of(s * HG + h), half(0)],
        lambda s, h: packed[rows_of(s * HG + h), half(1)],
        None if alone else lambda s, h: far_first[0, s * HG + h],
        None if alone else lambda s, h: far_first[1, s * HG + h],
        mats,
        work,
        last,
    )


def numbered(word, n):
    return word + str(n)


def pick(core, a, b):
    return jnp.where(core == 0, a, b)


def spread_vector(core, own, other, row, fields):
    rows = row_ids()
    result = jnp.zeros((8, LANES), F32)
    for f in range(2 * fields):
        value = pick(core, own[row][f], other[row][f]) if f < fields else pick(
            core, other[row][f - fields], own[row][f - fields]
        )
        result = jnp.where(rows == f, value, result)
    return result


def mix_fine(saved_f, shares, pay, fine, sems):
    steps, fields = saved_f.shape[0], saved_f.shape[1]
    copies = [pltpu.make_async_copy(saved_f.at[s], fine.at[s], sems.at[s]) for s in range(steps)]
    for copy in copies:
        copy.start()
    for s in range(steps):
        copies[s].wait()
        total = shares[0] * fine[s, 0]
        for v in range(1, fields):
            total = total + shares[v] * fine[s, v]
        pay[s] = total
        pay[steps + s] = fine[s, 0]


def mix_coarse(saved_c, seed_c, shares, after, payc):
    fields, blocks = saved_c.shape[1], saved_c.shape[2]
    for c in range(saved_c.shape[0]):
        total = shares[0] * saved_c[c, 0]
        for v in range(1, fields):
            total = total + shares[v] * saved_c[c, v]
        payc[0, pl.ds(c * blocks, blocks), :] = total
        payc[1, pl.ds(c * blocks, blocks), :] = saved_c[c, 0]
    for v in range(fields):
        payc[2 + v, pl.ds(0, blocks), :] = seed_c[v]
        payc[2 + v, pl.ds(blocks, blocks), :] = seed_c[v]


def substeps(counts):
    step = HEAT / counts.astype(F32)
    return [jnp.where(n < counts, step, 0.0) for n in range(NSUB)]


def reaction_tables(mix, start, steps):
    state = start
    history = []
    for step in steps:
        inverse = 1.0 / state
        decay = jnp.exp(-ENERGY * inverse)
        rise = step * mix * decay
        history.append((step * decay, rise * (inverse * inverse)))
        state = state + rise
    passed = jnp.ones_like(start)
    weight = jnp.zeros_like(start)
    for grown, slope in reversed(history):
        weight = weight + grown * passed
        passed = passed + passed * (ENERGY * slope)
    return passed - 1.0, weight


def chem_kernel(which, pay, pay_o, fine_counts, pack, after, gain, weight, edges, planes):
    core = lax.axis_index("fld")
    every = pay.shape[0] // 2
    shape = (8, CHEM * LANES)
    rows = lax.broadcasted_iota(jnp.int32, shape, 0)
    counts = jnp.ones(shape, jnp.int32)
    for b in range(fine_counts.shape[0]):
        counts = jnp.where(rows == b, fine_counts[b], counts)
    lengths = substeps(counts)

    def body(t, carry):
        at = pl.ds(pl.multiple_of(t * CHEM * LANES, CHEM * LANES), CHEM * LANES)
        for n, s in enumerate(which):
            start = pick(core, pay[every + s, :, at], pay_o[every + s, :, at])
            a, w = reaction_tables(pay[s, :, at] + pay_o[s, :, at], start, lengths)
            gain[n, :, at] = a
            weight[n, :, at] = w
        return carry

    lax.fori_loop(0, TILES // CHEM, body, 0)
    later = [n for n, s in enumerate(which) if s < every - 1]
    for m, table in enumerate((gain, weight)):
        for order, n in enumerate(later):
            for i in range(0, B, 2):
                for jh in range(2):
                    put_split(
                        planes,
                        rows_of((m * len(later) + order) * HG + i % HG, 2),
                        (i // HG,),
                        jnp.concatenate(
                            [table[n, :, cols(i, jh)], table[n, :, cols(i + 1, jh)]], axis=0
                        ),
                        half(jh),
                        half(2 + jh),
                    )
    edges[...] = pack_faces(planes, pack, edges.shape[0])


def chem_coarse(payc, payc_o, coarse_counts, gain, weight):
    core = lax.axis_index("fld")
    blocks = coarse_counts.shape[0]
    entries = gain.shape[0]
    shape = (entries, 8 * LANES)
    counts = jnp.ones(shape, jnp.int32)
    rows = lax.broadcasted_iota(jnp.int32, shape, 0)
    for r in range(entries):
        counts = jnp.where(rows == r, coarse_counts[r % blocks], counts)
    lengths = substeps(counts)

    def body(t, carry):
        at = pl.ds(pl.multiple_of(t * 8 * LANES, 8 * LANES), 8 * LANES)
        start = pick(core, payc[1, :, at], payc_o[1, :, at])
        gain[:, at], weight[:, at] = reaction_tables(
            payc[0, :, at] + payc_o[0, :, at], start, lengths
        )
        return carry

    lax.fori_loop(0, TILES // 8, body, 0)


def octant_finder(children, count_f):
    me = lax.axis_index("blk")
    devices = lax.axis_size("blk")
    found = []
    for p in range(children.shape[0]):
        for o in range(8):
            child = children[p, o]
            distance = jnp.where(child >= 0, (child // count_f - me) % devices, FAR)
            found.append((distance, child, p * 8 + o))

    def find(want):
        slot = jnp.int32(0)
        label = jnp.int32(-1)
        for distance, child, place in found:
            hit = distance == want
            slot = jnp.where(hit, place, slot)
            label = jnp.where(hit, child % count_f, label)
        return slot, label

    return find


def write_octant(state, first_slab, found, wanted_fields, out, at):
    slot, label = found
    p, a, b, c = slot // 8, slot // 4 % 2, slot // 2 % 2, slot % 2
    kept = lane_ids() % B // H == c
    for n, f in enumerate(wanted_fields):
        layers = state[first_slab + p, b, pl.ds(a * (H * 8) + f, H, stride=8), :]
        out[at + n] = jnp.where(kept, layers, 0.0)
    out[at + len(wanted_fields)] = jnp.full((H, LANES), label.astype(F32))


def slot_fields(core, fields):
    return [core * fields + v for v in range(fields)] + [0]


def keep_coarse(state, first_slab, children):
    upper = lane_ids() % B // H
    for p in range(children.shape[0]):
        for a in range(2):
            for b in range(2):
                low = jnp.where(children[p, 4 * a + 2 * b] < 0, 1.0, 0.0)
                high = jnp.where(children[p, 4 * a + 2 * b + 1] < 0, 1.0, 0.0)
                kept = jnp.where(upper == 0, low, high)
                for i in range(a * H, a * H + H):
                    at = (first_slab + p, b, rows_of(i))
                    state[at] = state[at] * kept


def fill_pack(table):
    cell = lax.broadcasted_iota(jnp.int32, (PLANE, 2 * LANES), 0)
    place = lax.broadcasted_iota(jnp.int32, (PLANE, 2 * LANES), 1)
    depth = place // B % 2
    layer = jnp.where(place < LANES, B - 1 - depth, depth)
    match = jnp.where(cell == place % B * B + layer, 1.0, 0.0)
    group = place % LANES // PACK
    for g in range(G):
        table[g] = jnp.where(group == g, match, 0.0).astype(BF16)


def start_kernel(
    sends, count_f, fields, payc, payc_o, children, coarse_counts, dif, shr, dif_o, shr_o,
    fine_nbr, coarse_nbr, coarse, gain_c, weight_c, local, *rest
):
    core = lax.axis_index("fld")
    count_c = children.shape[0]
    outs, (planes, packed, table, stage) = rest[:-4], rest[-4:]
    fill_pack(table)
    up, down = outs[-2:]
    for p in range(count_c):
        for v in range(fields):
            mine = payc[2 + v, pl.ds(p, 1), :]
            theirs = payc_o[2 + v, pl.ds(p, 1), :]
            stage[p, pl.ds(v, 1), :] = pick(core, mine, theirs)
            stage[p, pl.ds(fields + v, 1), :] = pick(core, theirs, mine)
        for i in range(B):
            for jh in range(2):
                coarse[p, jh, rows_of(i), :] = stage[p, :, cols(i, jh)]
    find = octant_finder(children, count_f)
    for out, distances in zip(outs, sends):
        write_octant(coarse, 0, find(pick(core, *distances)), list(range(2 * fields)), out, 0)
    write_octant(coarse, 0, find(0), slot_fields(core, fields), local, 0)
    chem_coarse(payc, payc_o, coarse_counts, gain_c, weight_c)
    keep_coarse(coarse, 0, children)
    react_coarse(
        coarse,
        0,
        count_c,
        spread_vector(core, (dif, shr), (dif_o, shr_o), 1, fields),
        gain_c,
        weight_c,
        gain_c.shape[0] - count_c,
    )
    build_planes(coarse, count_c, planes)
    packed[...] = pack_faces(planes, table, count_c * HG * 8)
    rows = row_ids()
    lane = lane_ids()
    faces = jnp.zeros((8, LANES), F32)
    for f in range(6):
        column = fine_nbr[:, pl.ds(f, 1)].astype(F32)
        faces = jnp.where(lane == f, jnp.broadcast_to(column, (8, LANES)), faces)
        for p in range(count_c):
            column = coarse_nbr[pl.ds(p, 1), pl.ds(f, 1)].astype(F32)
            faces = jnp.where(
                (lane == 8 + f) & (rows == p), jnp.broadcast_to(column, (8, LANES)), faces
            )
    base = 2 * fields + 1
    for n in range(count_c * HG):
        up[base + n] = packed[rows_of(n), half(0)]
        down[base + n] = packed[rows_of(n), half(1)]
    up[base + count_c * HG] = faces
    down[base + count_c * HG] = faces


def add_octants(entries, state, stage, fields):
    slots = fields + 1
    rows = row_ids()
    lane = lane_ids()
    source = jnp.zeros((8, LANES), jnp.int32)
    for d, tile in enumerate(entries):
        source = jnp.where(tile(None).astype(jnp.int32) == rows, d, source)
        for s in range(slots):
            stage[d // 8, s, pl.ds(d % 8, H, stride=8), :] = tile(s)
    lanes_of = [((H // 2 * jh + lane // B // 2) * B + lane % B // 2) for jh in range(2)]
    groups = (len(entries) + 7) // 8
    indices = []
    for g in range(groups):
        index = source - 8 * g
        indices.append((jnp.clip(index, 0, 7), (index >= 0) & (index < 8)))
    for s in range(slots):
        for i in range(H):
            got = None
            for g in range(groups):
                part = jnp.take_along_axis(
                    stage[g, s, rows_of(i), :], indices[g][0], axis=0, mode="promise_in_bounds"
                )
                part = jnp.where(indices[g][1], part, 0.0)
                got = part if got is None else got + part
            got = 0.125 * (got + roll(got, -H))
            for jh in range(2):
                wide = jnp.take_along_axis(got, lanes_of[jh], axis=1, mode="promise_in_bounds")
                for ii in range(2):
                    at = (s, jh, rows_of(2 * i + ii))
                    state[at] = state[at] + wide


def all_fields(core, fields, ref):
    def tile(s):
        if s is None:
            return ref[2 * fields]
        return ref[0] if s == fields else ref[pl.ds(core * fields + s, 1)][0]

    return tile


def own_slots(fields, ref, at=0):
    return lambda s: ref[at + (fields + 1 if s is None else s)]


def react_fine(state, fields, par, par_o, gain, weight):
    core = lax.axis_index("fld")
    share = [par[1][s] for s in range(fields)] + [pick(core, par[1][0], par_o[1][0])]
    extra = jnp.where(core == 0, 1.0, 0.0)
    for i in range(B):
        for jh in range(2):
            at = cols(i, jh)
            here = (jh, rows_of(i))
            driver = state[(fields,) + here]
            heat = weight[:, at] * driver
            grown = gain[:, at] * driver
            for s in range(fields + 1):
                value = state[(s,) + here] + share[s] * heat
                if s == 0:
                    value = value + extra * grown
                if s == fields:
                    value = value + grown
                state[(s,) + here] = value


def react_coarse(state, first_slab, count_c, shares, gain, weight, first_row):
    own = jnp.where(row_ids() == 0, 1.0, 0.0)
    for p in range(count_c):
        for i in range(B):
            for jh in range(2):
                at = cols(i, jh)
                here = (first_slab + p, jh, rows_of(i))
                value = state[here]
                driver = jnp.broadcast_to(value[0:1], (8, LANES))
                heat = weight[pl.ds(first_row + p, 1), at] * driver
                grown = gain[pl.ds(first_row + p, 1), at] * driver
                state[here] = value + shares * heat + own * grown


def links_maker(plan, faces, shift, fine_slabs):
    me = lax.axis_index("blk") + shift
    count_f, count_c = plan.count_f, plan.count_c

    def column(slab, face):
        return faces[:, face : face + 1].astype(jnp.int32)

    def column_c(slab, face):
        return faces[slab : slab + 1, 8 + face : 9 + face].astype(jnp.int32)

    fine = Links(column, me * count_f, count_f, True, 0)
    coarse = Links(column_c, me * count_c, count_c, False, fine_slabs)
    return lambda s: fine if s < fine_slabs else coarse


def strips_out(plan, r, out, faces, up_octant):
    going = plan.slabs_out
    even = lax.axis_index("blk") % 2 == 0
    build_planes(out, going, r.planes)
    r.packed[pl.ds(0, going * HG * 8), :] = pack_faces(
        r.planes, r.pack, going * HG * 8
    )

    def send(up, down):
        for n in range(going * HG):
            up[n] = r.packed[rows_of(n), half(0)]
            down[n] = r.packed[rows_of(n), half(1)]
        at = going * HG
        up[at] = faces
        down[at] = faces
        if up_octant is not None:
            up_octant(up, at + 1)
            for n in range(plan.fields + 2):
                down[at + 1 + n] = zero_tile()

    pl.when(even)(lambda: send(r.send_e, r.send_o))
    pl.when(jnp.logical_not(even))(lambda: send(r.send_o, r.send_e))


def zero_tile():
    return jnp.zeros((8, LANES), F32)


def open_kernel(plan, names, *refs):
    r = SimpleNamespace(**dict(zip(names, refs)))
    core = lax.axis_index("fld")
    fields = plan.fields
    slots = fields + 1
    count_f, count_c = plan.count_f, plan.count_c
    par, par_o = (r.dif, r.shr), (r.dif_o, r.shr_o)
    out = r.state_out
    base = 2 * fields + 1
    strip = count_c * HG

    def far(ref, ref_o, n):
        return pick(core, ref[base + n], ref_o[base + n])

    last = len(plan.sends) - 1
    below = [far(getattr(r, numbered("landed", last - 1)), getattr(r, numbered("shared", last - 1)), n) for n in range(strip + 1)]
    above = [far(getattr(r, numbered("landed", last)), getattr(r, numbered("shared", last)), n) for n in range(strip + 1)]
    own_up, own_down = r.own_up, r.own_down
    faces = own_up[base + strip]
    rates = 0.5 * spread_vector(core, par, par_o, 0, fields)

    def finish(p, i, jh, value):
        out[slots + p, jh, rows_of(i), :] = value

    diffuse(
        r.coarse,
        count_c,
        links_maker(plan, faces, 0, 0),
        links_maker(plan, below[strip], -1, 0),
        links_maker(plan, above[strip], 1, 0),
        lambda s: rates,
        lambda s, h: own_up[base + s * HG + h],
        lambda s, h: own_down[base + s * HG + h],
        lambda s, h: below[s * HG + h],
        lambda s, h: above[s * HG + h],
        r,
        r,
        finish,
    )
    find = octant_finder(r.children, count_f)
    for n, distances in enumerate(plan.later):
        write_octant(
            out, slots, find(pick(core, *distances)), list(range(2 * fields)), getattr(r, numbered("octant", n)), 0
        )
    mine = slot_fields(core, fields)
    write_octant(out, slots, find(0), mine, r.local_out, 0)
    near_octant = r.near_octant
    write_octant(out, slots, find(1), mine, near_octant, 0)
    keep_coarse(out, slots, r.children)
    react_coarse(
        out, slots, count_c, spread_vector(core, par, par_o, 1, fields), r.gain_c, r.weight_c, 0
    )
    for i in range(B):
        for jh in range(2):
            at = cols(i, jh)
            for s in range(fields):
                out[s, jh, rows_of(i), :] = r.seed_f[s, :, at]
            out[fields, jh, rows_of(i), :] = pick(core, r.seed_f[0, :, at], r.seed_other[0, :, at])
    entries = [own_slots(fields, r.local)]
    for n in range(last):
        entries.append(all_fields(core, fields, getattr(r, numbered("landed", n))))
        entries.append(all_fields(core, fields, getattr(r, numbered("shared", n))))
    one, two = (all_fields(core, fields, getattr(r, numbered(word, last))) for word in ("landed", "shared"))
    entries.append(lambda s: pick(core, two(s), one(s)))
    add_octants(entries, out, r.stage, fields)
    react_fine(out, fields, par, par_o, r.gain.at[plan.step], r.weight.at[plan.step])

    def up_octant(up, at):
        for n in range(slots + 1):
            up[at + n] = near_octant[n]

    strips_out(plan, r, out, faces, up_octant)


def rates_of(plan, r):
    core = lax.axis_index("fld")
    par, par_o = (r.dif, r.shr), (r.dif_o, r.shr_o)
    fields = plan.fields
    rates = [par[0][s] for s in range(fields)] + [pick(core, par[0][0], par_o[0][0])]
    return rates + [0.5 * spread_vector(core, par, par_o, 0, fields)] * plan.count_c


def by_parity(action, r):
    even = lax.axis_index("blk") % 2 == 0
    pl.when(even)(lambda: action(r.sent_e, r.sent_o, r.got_o, r.got_e))
    pl.when(jnp.logical_not(even))(lambda: action(r.sent_o, r.sent_e, r.got_e, r.got_o))


def react_bulk(plan, r, out):
    slots = plan.fields + 1
    par, par_o = (r.dif, r.shr), (r.dif_o, r.shr_o)
    react_fine(out, plan.fields, par, par_o, r.gain.at[plan.step], r.weight.at[plan.step])
    build_planes(out, slots, r.planes)
    r.faces_out[...] = pack_faces(r.planes, r.pack, slots * HG * 8)


def bulk_kernel(plan, names, *refs):
    r = SimpleNamespace(**dict(zip(names, refs)))
    core = lax.axis_index("fld")
    fields = plan.fields
    slots = fields + 1
    count_c = plan.count_c
    par, par_o = (r.dif, r.shr), (r.dif_o, r.shr_o)
    slabs, arrived = plan.slabs, plan.slabs_in
    own_up, own_down = r.own_up, r.own_down

    def sort_strips(up, down, below, above):
        for n in range(arrived * HG + 1):
            own_up[n] = up[n]
            own_down[n] = down[n]

    even = lax.axis_index("blk") % 2 == 0
    pl.when(even)(lambda: sort_strips(r.sent_e, r.sent_o, None, None))
    pl.when(jnp.logical_not(even))(lambda: sort_strips(r.sent_o, r.sent_e, None, None))
    faces = own_up[arrived * HG]
    source, out = r.state, r.state_out
    if plan.late:
        late = plan.late * HG * 8
        high, low = split(r.late[pl.ds(0, late), :])
        r.ends[pl.ds(0, late), pl.ds(0, 2 * LANES)] = high
        r.ends[pl.ds(0, late), pl.ds(2 * LANES, 2 * LANES)] = low
        place_ends(r.ends, r.placed, late, r)
        source = r.whole
        for i in range(B):
            for jh in range(2):
                for s in range(slabs):
                    source[s, jh, rows_of(i), :] = r.state[s, jh, rows_of(i), :] + placed_tile(
                        r.placed, s, i, jh
                    )

    def finish(s, i, jh, value):
        if s >= slots:
            r.coarse_out[s - slots, jh, rows_of(i), :] = value
        else:
            out[s, jh, rows_of(i), :] = value

    rates = rates_of(plan, r)
    diffuse(
        source,
        slabs,
        links_maker(plan, faces, 0, slots),
        None,
        None,
        lambda s: rates[s],
        lambda s, h: own_up[s * HG + h],
        lambda s, h: own_down[s * HG + h],
        None,
        None,
        r,
        r,
        finish,
    )
    if not plan.final and not plan.pause:
        react_bulk(plan, r, out)


def coarse_kernel(plan, names, *refs):
    r = SimpleNamespace(**dict(zip(names, refs)))
    core = lax.axis_index("fld")
    fields, count_c = plan.fields, plan.count_c
    high, low = split(r.late[pl.ds((fields + 1) * HG * 8, count_c * HG * 8), :])
    r.ends[:, pl.ds(0, 2 * LANES)] = high
    r.ends[:, pl.ds(2 * LANES, 2 * LANES)] = low
    place_ends(r.ends, r.placed, count_c * HG * 8, r)
    for p in range(count_c):
        for i in range(B):
            for jh in range(2):
                r.coarse_stage[p, :, cols(i, jh)] = r.coarse[p, jh, rows_of(i), :] + placed_tile(
                    r.placed, p, i, jh
                )
        for v in range(fields):
            r.coarse_final[v, pl.ds(p, 1), :] = pick(
                core,
                r.coarse_stage[p, pl.ds(v, 1), :],
                r.coarse_stage[p, pl.ds(fields + v, 1), :],
            )


def share_kernel(plan, names, *refs):
    r = SimpleNamespace(**dict(zip(names, refs)))
    slots = plan.fields + 1
    for n in range(len(plan.later)):
        ref = getattr(r, numbered("landed", n))
        tile = all_fields(1 - lax.axis_index("fld"), plan.fields, ref)
        for s in range(slots):
            r.shared[n * (slots + 1) + s] = tile(s)
        r.shared[n * (slots + 1) + slots] = tile(None)


def resume_kernel(plan, names, *refs):
    r = SimpleNamespace(**dict(zip(names, refs)))
    core = lax.axis_index("fld")
    even = lax.axis_index("blk") % 2 == 0
    fields = plan.fields
    slots = fields + 1
    out = r.state_out
    out[...] = r.state[...]
    near = r.near_octant

    def take(ref):
        for n in range(slots + 1):
            near[n] = ref[plan.near_at + n]

    pl.when(even)(lambda: take(r.near_o))
    pl.when(jnp.logical_not(even))(lambda: take(r.near_e))
    entries = [own_slots(fields, r.local), own_slots(fields, near)]
    for n in range(len(plan.later)):
        entries.append(all_fields(core, fields, getattr(r, numbered("landed", n))))
        entries.append(own_slots(fields, r.shared, n * (slots + 1)))
    add_octants(entries, out, r.stage, fields)
    react_bulk(plan, r, out)


def edge_kernel(plan, names, *refs):
    sems = refs[-1]
    r = SimpleNamespace(**dict(zip(names, refs)))
    core = lax.axis_index("fld")
    fields = plan.fields
    slots = fields + 1
    par, par_o = (r.dif, r.shr), (r.dif_o, r.shr_o)
    slabs, arrived = plan.slabs, plan.slabs_in
    own_up, own_down, far_b, far_a = r.own_up, r.own_down, r.far_b, r.far_a

    def sort_strips(up, down, below, above):
        for n in range(arrived * HG + 1):
            own_up[n] = up[n]
            own_down[n] = down[n]
            far_b[n] = below[n]
            far_a[n] = above[n]

    by_parity(sort_strips, r)
    faces = own_up[arrived * HG]
    rates = rates_of(plan, r)
    near = links_maker(plan, faces, 0, slots)
    from_below = links_maker(plan, far_b[arrived * HG], -1, slots)
    from_above = links_maker(plan, far_a[arrived * HG], 1, slots)
    outer = outer_lanes()
    delta, far_first, lateral, late = r.delta, r.far_first, r.lateral, r.late

    def at_tile(ref):
        return lambda s, h: ref[s * HG + h]

    for s in range(slabs):
        for h in range(HG):
            for n, (name, ref) in enumerate((((5, 1), far_a), ((4, -1), far_b))):
                ghost = near(s).read(name, s, lambda q, ref=ref: ref[q * HG + h])
                delta[n, s * HG + h] = jnp.where(outer, rates[s] * ghost, 0.0)

    def keep_far(n, s, h, lap):
        far_first[n, s * HG + h] = rates[s] * lap

    def keep_lateral(n, s, h, lap):
        lateral[n, s * HG + h] = lap

    laplace_far(
        slabs,
        (
            (from_below, at_tile(far_b), at_tile(own_down), (5, 1)),
            (from_above, at_tile(far_a), at_tile(own_up), (4, -1)),
        ),
        r,
        r,
        keep_far,
    )
    laplace_far(
        slabs,
        ((near, at_tile(delta.at[0]), None, None), (near, at_tile(delta.at[1]), None, None)),
        r,
        SimpleNamespace(far_lhs=r.far_lhs2, far_out=r.far_out2),
        keep_lateral,
    )
    share = [par[1][s] for s in range(fields)] + [pick(core, par[1][0], par_o[1][0])]
    extra = jnp.where(core == 0, 1.0, 0.0)
    for n, (name, other) in enumerate((((5, 1), 1), ((4, -1), 0))):
        for h in range(HG):
            added = []
            for s in range(slabs):
                at = s * HG + h
                ghost = near(s).read(name, s, lambda q: far_first[other, q * HG + h])
                value = delta[n, at]
                more = 0.5 * rates[s]
                inner = more * roll(value, B)
                value = value + more * (lateral[n, at] + ghost)
                added.append(jnp.where(outer, value, inner))
            if not plan.final:
                gain = r.edges[rows_of(plan.step * HG + h), half(n)]
                weight = r.edges[rows_of((plan.packed + plan.step) * HG + h), half(n)]
                driver = added[fields]
                heat, grown = weight * driver, gain * driver
                for s in range(slots):
                    added[s] = added[s] + share[s] * heat
                added[0] = added[0] + extra * grown
                added[fields] = added[fields] + grown
            for s in range(slabs):
                late[rows_of(s * HG + h), half(n)] = added[s]
    if plan.final:
        high, low = split(late[...])
        r.ends[:, pl.ds(0, 2 * LANES)] = high
        r.ends[:, pl.ds(2 * LANES, 2 * LANES)] = low
        place_ends(r.ends, r.placed, slabs * HG * 8, r)
        copies = []
        for s in range(slabs):
            for i in range(B):
                for jh in range(2):
                    r.result[s, :, cols(i, jh)] = r.state[s, jh, rows_of(i), :] + placed_tile(
                        r.placed, s, i, jh
                    )
            copies.append(pltpu.make_async_copy(r.result.at[s], r.state_out.at[s], sems.at[s]))
            copies[s].start()
        for copy in copies:
            copy.wait()
        return

    def send(up, down):
        for n in range(slots * HG):
            up[n] = r.faces_in[rows_of(n), half(0)] + late[rows_of(n), half(0)]
            down[n] = r.faces_in[rows_of(n), half(1)] + late[rows_of(n), half(1)]
        up[slots * HG] = faces
        down[slots * HG] = faces

    even = lax.axis_index("blk") % 2 == 0
    pl.when(even)(lambda: send(r.send_e, r.send_o))
    pl.when(jnp.logical_not(even))(lambda: send(r.send_o, r.send_e))


SCALARS = ("dif", "shr", "dif_o", "shr_o", "children", "fine_counts", "coarse_counts")
MATS = ("plane", "side", "place", "pack", "far")
MIB = 1024 * 1024
LIMIT = 51


def call(kernel, inputs, outputs, scratch, hbm=(), sems=(), limit=None, cost=1000):
    names = list(inputs) + list(outputs) + list(scratch)
    scratch = {
        name: value if value[-1] is BF16 else value + (F32,) for name, value in scratch.items()
    }
    size = sum(4 * np.prod(v.shape) for name, v in inputs.items() if name not in hbm)
    size += sum(4 * np.prod(v) for v in outputs.values())
    size += sum(4 * np.prod(v[:-1]) for v in scratch.values())

    def spec(name):
        if name in hbm:
            return HBM
        return SMEM if name in SCALARS else VMEM

    result = pl.pallas_call(
        functools.partial(kernel, names),
        out_shape=[jax.ShapeDtypeStruct(shape, F32) for shape in outputs.values()],
        in_specs=[spec(name) for name in inputs],
        out_specs=[spec(name) for name in outputs],
        scratch_shapes=[pltpu.VMEM(value[:-1], value[-1]) for value in scratch.values()]
        + [pltpu.SemaphoreType.DMA(shape) for shape in sems],
        compiler_params=pltpu.CompilerParams(vmem_limit_bytes=limit or int(size) + 12 * MIB),
        cost_estimate=pl.CostEstimate(flops=cost, bytes_accessed=cost, transcendentals=0),
    )(*inputs.values())
    return SimpleNamespace(**dict(zip(outputs, result)))


def shards(
    seed_fine,
    seed_coarse,
    saved_fine,
    saved_coarse,
    diffusion,
    species_shares,
    fine_nbr,
    coarse_nbr,
    children,
    fine_counts,
    coarse_counts,
):
    fields, count_f, cells = seed_fine.shape
    count_c = seed_coarse.shape[1]
    steps = saved_fine.shape[0]
    cycles = saved_coarse.shape[0]
    slots = fields + 1
    every = slots + count_c
    sends, later = first_sends(count_f), later_sends(count_f)
    mats = tables()
    octant_shape = (2 * fields + 1, H, LANES)
    slots_shape = (slots + 1, H, LANES)
    loaded_shape = (2 * fields + 1 + count_c * HG + 1, 8, LANES)

    def plain(kernel, *fixed):
        return lambda names, *refs: kernel(*fixed, *refs)

    def strip(slabs, more=0):
        return (slabs * HG + 1 + more, 8, LANES)

    def state_shape(slabs):
        return (slabs, 2, 8 * B, LANES)

    def work(slabs):
        rows = slabs * HG * 8
        return dict(
            first=state_shape(slabs),
            far_first=(2, slabs * HG, 8, LANES),
            sums=(G, rows, PLANE),
            ends=(rows, 4 * LANES, BF16),
            placed=(rows, G * PLANE),
            far_lhs=(2 * rows, 4 * LANES, BF16),
            far_out=(2 * rows, LANES),
        )

    def strip_work(slabs):
        return {name: strip(slabs) for name in ("far_b", "far_a", "own_up", "own_down")}

    def pack_work(slabs):
        rows = slabs * HG * 8
        return dict(
            planes=(G, rows, 2 * PLANE + 2 * LANES, BF16),
            packed=(rows, 2 * LANES),
        )

    def after(value, *before):
        return lax.optimization_barrier((value, before))[0]

    stage_work = dict(stage=(1, slots, 8 * H, LANES))
    dif_o, shr_o = core_swap(diffusion), core_swap(species_shares)
    pay = call(
        plain(mix_fine),
        dict(saved_f=saved_fine, shr=species_shares),
        dict(pay=(2 * steps, count_f, cells)),
        dict(fine=saved_fine.shape),
        hbm=("saved_f",),
        sems=((steps,),),
        limit=LIMIT * MIB,
    ).pay
    payc = call(
        plain(mix_coarse),
        dict(saved_c=saved_coarse, seed_c=seed_coarse, shr=species_shares, after=pay),
        dict(payc=(2 + fields, cycles * count_c, cells)),
        {},
        hbm=("after",),
    ).payc
    payc_o = core_swap(payc)
    pay, sown, payc_o, dif_o, shr_o = lax.optimization_barrier(
        (pay, seed_fine, payc_o, dif_o, shr_o)
    )
    par = dict(dif=diffusion, shr=species_shares, dif_o=dif_o, shr_o=shr_o)
    pay_o, seed_o = core_swap(pay), core_swap(sown)

    loaded = [numbered("octant", n) for n in range(len(sends) - 2)] + ["up", "down"]
    started = call(
        plain(start_kernel, sends, count_f, fields),
        dict(
            payc=payc,
            payc_o=payc_o,
            children=children,
            coarse_counts=coarse_counts,
            **par,
            fine_nbr=fine_nbr,
            coarse_nbr=coarse_nbr,
        ),
        dict(
            coarse=state_shape(count_c),
            gain_c=(cycles * count_c, cells),
            weight_c=(cycles * count_c, cells),
            local=slots_shape,
            **{name: loaded_shape if name in ("up", "down") else octant_shape for name in loaded},
        ),
        dict(
            pack_work(count_c),
            table=(G, PLANE, 2 * LANES, BF16),
            coarse_stage=(count_c, 2 * fields, cells),
        ),
    )
    landed = [octant_move(getattr(started, name), d) for name, d in zip(loaded, sends)]
    def chem_of(which, before):
        packed = 2 * sum(step < steps - 1 for step in which)
        return call(
            plain(chem_kernel, which),
            dict(pay=pay, pay_o=pay_o, fine_counts=fine_counts, pack=mats.pack, after=before),
            dict(
                gain=(len(which), count_f, cells),
                weight=(len(which), count_f, cells),
                edges=(packed * HG * 8, 2 * LANES),
            ),
            dict(planes=pack_work(packed)["planes"]),
            hbm=("after",),
        )

    chem = chem_of(tuple(range(steps)), payc)
    landed, (chem.gain, chem.weight, chem.edges) = lax.optimization_barrier(
        (landed, (chem.gain, chem.weight, chem.edges))
    )
    shared = [core_swap(value) for value in landed]

    def named(word, values):
        return {numbered(word, n): value for n, value in enumerate(values)}

    plan = dict(
        fields=fields,
        count_f=count_f,
        count_c=count_c,
        sends=sends,
        later=later,
        slabs_in=every,
        slabs=every,
        slabs_out=slots,
        final=False,
        add=False,
        near_at=every * HG + 1,
        late=0,
        pause=False,
        packed=0,
    )

    def run(kernel, changes, inputs, outputs, scratch, **more):
        return call(
            functools.partial(kernel, SimpleNamespace(**{**plan, **changes})),
            dict(par, **vars(mats), **inputs),
            outputs,
            scratch,
            **more,
        )

    def halo(made, ring=False):
        got_o = pair_swap(made.send_o, 1, ring)
        got_e = pair_swap(made.send_e, 0, ring)
        return dict(sent_o=made.send_o, got_o=got_o, sent_e=made.send_e, got_e=got_e)

    def sending(slabs, more=0):
        return dict(
            state_out=state_shape(slabs), send_e=strip(slabs, more), send_o=strip(slabs, more)
        )

    made = run(
        open_kernel,
        dict(slabs_out=every, step=steps - 1),
        dict(
            gain=chem.gain,
            weight=chem.weight,
            gain_c=started.gain_c,
            weight_c=started.weight_c,
            children=children,
            coarse=started.coarse,
            own_up=started.up,
            own_down=started.down,
            seed_f=seed_fine,
            seed_other=seed_o,
            local=started.local,
            **named("landed", landed),
            **named("shared", shared),
        ),
        dict(
            sending(every, slots + 1),
            local_out=slots_shape,
            **named("octant", [octant_shape] * len(later)),
        ),
        dict(work(count_c), **pack_work(every), **stage_work, near_octant=slots_shape),
    )
    first_halo = halo(made, True)
    landed = [octant_move(getattr(made, numbered("octant", n)), d) for n, d in enumerate(later)]
    arrived_halo = first_halo

    def edge_work(slabs):
        rows = slabs * HG * 8
        packed = (2, slabs * HG, 8, LANES)
        return dict(
            delta=packed,
            far_first=packed,
            lateral=packed,
            far_lhs=(2 * rows, 4 * LANES, BF16),
            far_out=(2 * rows, LANES),
            far_lhs2=(2 * rows, 4 * LANES, BF16),
            far_out2=(2 * rows, LANES),
        )

    def place_work(slabs):
        rows = slabs * HG * 8
        return dict(ends=(rows, 4 * LANES, BF16), placed=(rows, G * PLANE))

    def own_strips(slabs):
        return dict(own_up=strip(slabs), own_down=strip(slabs))

    state, flown, held = made.state_out, arrived_halo, every
    local = made.local_out
    sent = dict(sent_e=made.send_e, sent_o=made.send_o)
    late, coarse, coarse_final = None, None, None
    for step in reversed(range(-1, steps - 1)):
        final = step < 0
        slabs = fields if final else held
        changes = dict(step=step, packed=steps - 1)
        changes.update(slabs_in=held, slabs=slabs, final=final)
        inputs = dict(state=state, **sent)
        outputs = dict(state_out=state_shape(min(slabs, slots)))
        scratch = dict(work(slabs), **own_strips(held), **pack_work(slabs))
        if not final:
            inputs.update(gain=chem.gain, weight=chem.weight)
            outputs.update(faces_out=(slots * HG * 8, 2 * LANES))
        if held > slots:
            outputs.update(coarse_out=state_shape(count_c))
        if late is not None:
            inputs.update(late=late)
            scratch.update(whole=state_shape(slabs), **place_work(slabs))
            changes.update(late=slabs)
        paused = step == steps - 3
        if paused:
            for name in ("gain", "weight"):
                inputs.pop(name)
            outputs.pop("faces_out")
            changes.update(pause=True)
        bulk = run(bulk_kernel, changes, inputs, outputs, scratch)
        if paused:
            whole = run(
                resume_kernel,
                changes,
                dict(
                    state=bulk.state_out,
                    gain=chem.gain,
                    weight=chem.weight,
                    near_e=arrived_halo["got_e"],
                    near_o=arrived_halo["got_o"],
                    local=local,
                    shared=shared,
                    **named("landed", landed),
                ),
                dict(state_out=state_shape(slots), faces_out=(slots * HG * 8, 2 * LANES)),
                dict(pack_work(slots), **stage_work, near_octant=slots_shape),
            )
            bulk.state_out, bulk.faces_out = whole.state_out, whole.faces_out
        if held > slots:
            coarse = bulk.coarse_out
        inputs = dict(flown)
        scratch = dict(edge_work(slabs), **strip_work(held))
        if final:
            inputs.update(state=bulk.state_out)
            outputs = dict(state_out=seed_fine.shape)
            scratch.update(
                late=(slabs * HG * 8, 2 * LANES), result=seed_fine.shape, **place_work(slabs)
            )
        else:
            inputs.update(edges=chem.edges, faces_in=bulk.faces_out)
            outputs = dict(
                late=(slabs * HG * 8, 2 * LANES), send_e=strip(slots), send_o=strip(slots)
            )
        more = dict(hbm=("state_out",), sems=((fields,),)) if final else {}
        made = run(edge_kernel, changes, inputs, outputs, scratch, **more)
        if step == steps - 2:
            first_late = made.late
            part = run(
                share_kernel,
                dict(),
                dict(named("landed", landed), after=first_late),
                dict(shared=(len(later) * (slots + 1), 8, LANES)),
                {},
                hbm=("after",),
            )
            shared = core_swap(part.shared)
        if final:
            break
        state, late, held = bulk.state_out, made.late, slots
        if step == 0:
            coarse_final = run(
                coarse_kernel,
                dict(),
                dict(coarse=coarse, late=first_late, after=late),
                dict(coarse_final=seed_coarse.shape),
                dict(place_work(count_c), coarse_stage=(count_c, 2 * fields, cells)),
                hbm=("after",),
            ).coarse_final
        flown = halo(made)
        sent = dict(sent_e=made.send_e, sent_o=made.send_o)
    return made.state_out, coarse_final


def solution(mesh):
    return jax.shard_map(
        shards,
        mesh=mesh,
        in_specs=(
            P("fld", "blk", None),
            P("fld", "blk", None),
            P(None, "fld", "blk", None),
            P(None, "fld", "blk", None),
            P("fld"),
            P("fld"),
            P("blk", None),
            P("blk", None),
            P("blk", None),
            P("blk"),
            P("blk"),
        ),
        out_specs=(P("fld", "blk", None), P("fld", "blk", None)),
        check_vma=False,
    )
```

```python
import functools
from types import SimpleNamespace
import jax
import numpy as np
import jax.numpy as jnp
from jax import lax
from jax.experimental import pallas as pl
from jax.experimental.pallas import tpu as pltpu
from jax.sharding import PartitionSpec as P

B = 16
H = B // 2
NSUB = 4
G = 4
HG = B // G
PLANE = B * B
CYCLES = 2
LANES = 128
TILES = B**3 // LANES
PACK = LANES // G
CHEM = 4
HEAT = 0.5
ENERGY = 2.0
FAR = -(1 << 20)
VMEM = pl.BlockSpec(memory_space=pltpu.VMEM)
SMEM = pl.BlockSpec(memory_space=pltpu.SMEM)
HBM = pl.BlockSpec(memory_space=pltpu.HBM)
F32 = jnp.float32
BF16 = jnp.bfloat16


def core_swap(value):
    return lax.ppermute(value, "fld", [(0, 1), (1, 0)])


def pair_swap(value, first, ring):
    n = lax.axis_size("blk")
    pairs = []
    for i in range(n):
        other = i + 1 if (i - first) % 2 == 0 else i - 1
        for core in range(2):
            if ring or 0 <= other < n:
                pairs.append((2 * i + core, 2 * (other % n) + core))
            else:
                pairs.append((2 * i + core, 2 * i + 1 - core))
    return lax.ppermute(value, ("blk", "fld"), pairs)


def first_sends(count):
    middle = count // 2
    return list(zip(list(range(2, middle)) + [1, -1], range(middle, count)))


def later_sends(count):
    middle = count // 2 + 1
    return list(zip(range(2, middle), range(middle, count)))


def octant_move(value, distances):
    n = lax.axis_size("blk")
    pairs = []
    for i in range(n):
        for core in range(2):
            pairs.append((2 * i + core, 2 * ((i + distances[core]) % n) + core))
    return lax.ppermute(value, ("blk", "fld"), pairs)


def tables():
    cell = np.arange(PLANE)
    j, k = cell // B, cell % B
    near = np.abs(j[:, None] - j[None, :]) + np.abs(k[:, None] - k[None, :])
    plane = (near == 1).astype(np.float32)
    side = np.zeros((LANES, PLANE), np.float32)
    line = np.arange(B)
    side[line, (B - 1) * B + line] = 1
    side[LANES - B + line, line] = 1
    pack = np.zeros((G, PLANE, 2 * LANES), np.float32)
    far = np.zeros((2 * LANES, LANES), np.float32)
    for g in range(G):
        at = g * PACK + line
        for depth in range(2):
            pack[g, line * B + B - 1 - depth, at + depth * B] = 1
            pack[g, line * B + depth, LANES + at + depth * B] = 1
        far[at[:-1], at[1:]] = 1
        far[at[1:], at[:-1]] = 1
        far[at + B, at] = 1
        far[LANES + at[B - 1], at[0]] = 1
        far[LANES + at[0], at[B - 1]] = 1
    place = np.concatenate([pack[g].T for g in range(G)], axis=1)
    return SimpleNamespace(
        plane=jnp.asarray(plane, BF16),
        side=jnp.asarray(side, BF16),
        place=jnp.asarray(place, BF16),
        pack=jnp.asarray(pack, BF16),
        far=jnp.asarray(far, BF16),
    )


def lane_ids():
    return lax.broadcasted_iota(jnp.int32, (8, LANES), 1)


def row_ids():
    return lax.broadcasted_iota(jnp.int32, (8, LANES), 0)


def roll(x, steps):
    steps = steps % LANES
    return x if steps == 0 else pltpu.roll(x, steps, 1)


def cols(i, jh, width=1):
    return pl.ds((2 * i + jh) * LANES, width * LANES)


def half(jh):
    return pl.ds(jh * LANES, LANES)


def rows_of(i, count=1):
    return pl.ds(8 * i, 8 * count)


def split(x):
    high = x.astype(BF16)
    return high, (x - high.astype(F32)).astype(BF16)


def product(pairs):
    total = None
    for a, b in pairs:
        term = jnp.dot(a, b, preferred_element_type=F32)
        total = term if total is None else total + term
    return total


class Links:
    def __init__(self, column, base, count, by_rows, first_slab):
        self.count = count
        self.by_rows = by_rows
        self.column = column
        self.base = base
        self.first_slab = first_slab
        self.cache = {}

    def place(self, slab, face, shift=0):
        raw = jnp.broadcast_to(self.column(slab, face), (8, LANES))
        return jnp.where(raw >= 0, raw - (self.base + shift), FAR)

    def make(self, name, slab):
        lane = lane_ids()
        if name == "j":
            return jnp.where(lane < LANES // 2, self.place(slab, 3), self.place(slab, 2))
        if name == "j_packed":
            return jnp.where(lane % B == B - 1, self.place(slab, 2), self.place(slab, 3))
        face, step = name
        return self.place(slab, face, step * self.count)

    def index(self, name, slab):
        key = (name, None if self.by_rows else slab)
        if key not in self.cache:
            where = self.make(name, slab - self.first_slab)
            if self.by_rows:
                there = (where >= 0) & (where < self.count)
                self.cache[key] = (jnp.clip(where, 0, self.count - 1), there)
            else:
                self.cache[key] = [where == q for q in range(self.count)]
        return self.cache[key]

    def read(self, name, slab, tile):
        where = self.index(name, slab)
        if self.by_rows:
            got = jnp.take_along_axis(tile(slab), where[0], axis=0, mode="promise_in_bounds")
            return jnp.where(where[1], got, 0.0)
        result = jnp.zeros((8, LANES), F32)
        for q in range(self.count):
            result = jnp.where(where[q], tile(self.first_slab + q), result)
        return result


def put_split(ref, at, lead, value, high_at, low_at):
    high, low = split(value)
    ref[lead + (at, high_at)] = high
    ref[lead + (at, low_at)] = low


def build_planes(source, slabs, planes):
    for s in range(slabs):
        for i in range(0, B, 2):
            g, h = i // HG, i % HG
            for jh in range(2):
                put_split(
                    planes,
                    rows_of(s * HG + h, 2),
                    (g,),
                    source[s, jh, rows_of(i, 2), :],
                    half(jh),
                    half(2 + jh),
                )


def build_sides(source, slabs, near, planes):
    lane = lane_ids()
    for s in range(slabs):
        for i in range(0, B, 2):
            g, h = i // HG, i % HG
            edge = []
            for n in (i, i + 1):

                def tile(q, n=n):
                    return jnp.where(
                        lane < LANES // 2,
                        source[q, 0, rows_of(n), :],
                        source[q, 1, rows_of(n), :],
                    )

                edge.append(near(s).read("j", s, tile))
            put_split(
                planes,
                rows_of(s * HG + h, 2),
                (g,),
                jnp.concatenate(edge, axis=0),
                pl.ds(2 * PLANE, LANES),
                pl.ds(2 * PLANE + LANES, LANES),
            )


def pack_faces(planes, table, used):
    pairs = []
    for g in range(G):
        pairs.append((planes[g, pl.ds(0, used), pl.ds(0, PLANE)], table[g]))
        pairs.append((planes[g, pl.ds(0, used), pl.ds(PLANE, PLANE)], table[g]))
    return product(pairs)


def outer_lanes():
    return lane_ids() // B % 2 == 0


def place_ends(ends, placed, used, mats):
    every = pl.ds(0, used)
    for g in range(G):
        table = mats.place[:, pl.ds(g * PLANE, PLANE)]
        placed[every, pl.ds(g * PLANE, PLANE)] = product(
            [
                (ends[every, pl.ds(0, 2 * LANES)], table),
                (ends[every, pl.ds(2 * LANES, 2 * LANES)], table),
            ]
        )


def placed_tile(placed, s, i, jh):
    return placed[rows_of(s * HG + i % HG), pl.ds(i // HG * PLANE + jh * LANES, LANES)]


def laplace(source, slabs, near, up, down, below, above, mats, work, emit):
    planes, sums, ends, placed = work.planes, work.sums, work.ends, work.placed
    used = slabs * HG * 8
    outer = outer_lanes()
    for s in range(slabs):
        for h in range(0, HG, 2):
            for side in range(2):
                pieces = []
                for n in (h, h + 1):
                    if side == 0:
                        value = near(s).read((5, 0), s, lambda q, n=n: down(q, n))
                        if above is not None:
                            value = value + near(s).read((5, 1), s, lambda q, n=n: above(q, n))
                    else:
                        value = near(s).read((4, 0), s, lambda q, n=n: up(q, n))
                        if below is not None:
                            value = value + near(s).read((4, -1), s, lambda q, n=n: below(q, n))
                    pieces.append(jnp.where(outer, value, 0.0))
                put_split(
                    ends,
                    rows_of(s * HG + h, 2),
                    (),
                    jnp.concatenate(pieces, axis=0),
                    half(side),
                    half(2 + side),
                )
    every = pl.ds(0, used)
    plane, side = mats.plane[...], mats.side[...]
    for g in range(G):
        sums[g, every, :] = product(
            [
                (planes[g, every, pl.ds(0, PLANE)], plane),
                (planes[g, every, pl.ds(PLANE, PLANE)], plane),
                (planes[g, every, pl.ds(2 * PLANE, LANES)], side),
                (planes[g, every, pl.ds(2 * PLANE + LANES, LANES)], side),
            ]
        )
    place_ends(ends, placed, used, mats)
    for s in range(slabs):
        for i in range(B):
            g, h = i // HG, i % HG
            at = rows_of(s * HG + h)
            for jh in range(2):
                c = source[s, jh, rows_of(i), :]
                if i > 0:
                    before = source[s, jh, rows_of(i - 1), :]
                else:
                    before = near(s).read(
                        (0, 0), s, lambda q, jh=jh: source[q, jh, rows_of(B - 1), :]
                    )
                if i < B - 1:
                    after = source[s, jh, rows_of(i + 1), :]
                else:
                    after = near(s).read((1, 0), s, lambda q, jh=jh: source[q, jh, rows_of(0), :])
                lap = (before + after) - 6.0 * c
                lap = lap + (
                    sums[g, at, half(jh)] + placed[at, pl.ds(g * PLANE + jh * LANES, LANES)]
                )
                emit(s, i, jh, c, lap)


def laplace_far(slabs, sides, mats, work, emit):
    lhs, out = work.far_lhs, work.far_out
    group = lane_ids() // PACK
    for n, (links, tile, _, _) in enumerate(sides):
        for s in range(slabs):
            for h in range(0, HG, 2):
                c = jnp.concatenate([tile(s, h), tile(s, h + 1)], axis=0)
                edge = jnp.concatenate(
                    [
                        links(s).read("j_packed", s, lambda q, m=m: tile(q, m))
                        for m in (h, h + 1)
                    ],
                    axis=0,
                )
                at = rows_of((n * slabs + s) * HG + h, 2)
                put_split(lhs, at, (), c, half(0), half(2))
                put_split(lhs, at, (), edge, half(1), half(3))
    every = pl.ds(0, 2 * slabs * HG * 8)
    table = mats.far[...]
    out[every, :] = product(
        [
            (lhs[every, pl.ds(0, 2 * LANES)], table),
            (lhs[every, pl.ds(2 * LANES, 2 * LANES)], table),
        ]
    )
    for n, (links, tile, own, own_name) in enumerate(sides):
        for s in range(slabs):
            for h in range(HG):
                c = tile(s, h)
                if h > 0:
                    before = tile(s, h - 1)
                else:
                    wrap = links(s).read((0, 0), s, lambda q: tile(q, HG - 1))
                    before = roll(jnp.where(group == G - 1, wrap, tile(s, HG - 1)), PACK)
                if h < HG - 1:
                    after = tile(s, h + 1)
                else:
                    wrap = links(s).read((1, 0), s, lambda q: tile(q, 0))
                    after = roll(jnp.where(group == 0, wrap, tile(s, 0)), -PACK)
                lap = (before + after) + out[rows_of((n * slabs + s) * HG + h), :] - 6.0 * c
                if own is not None:
                    lap = lap + links(s).read(own_name, s, lambda q: own(q, h))
                emit(n, s, h, lap)


def diffuse(source, slabs, near, from_below, from_above, rate, up, down, below, above, mats, work, finish):
    first, packed = work.first, work.packed
    alone = below is None
    far_first = None if alone else work.far_first
    build_planes(source, slabs, work.planes)
    build_sides(source, slabs, near, work.planes)

    def keep_first(s, i, jh, c, lap):
        first[s, jh, rows_of(i), :] = rate(s) * lap

    laplace(source, slabs, near, up, down, below, above, mats, work, keep_first)

    def keep_far(n, s, h, lap):
        far_first[n, s * HG + h] = rate(s) * lap

    if not alone:
        laplace_far(
            slabs,
            ((from_below, below, down, (5, 1)), (from_above, above, up, (4, -1))),
            mats,
            work,
            keep_far,
        )
    build_planes(first, slabs, work.planes)
    build_sides(first, slabs, near, work.planes)
    packed[pl.ds(0, slabs * HG * 8), :] = pack_faces(work.planes, mats.pack, slabs * HG * 8)

    def last(s, i, jh, c, lap):
        finish(s, i, jh, source[s, jh, rows_of(i), :] + c + 0.5 * rate(s) * lap)

    laplace(
        first,
        slabs,
        near,
        lambda s, h: packed[rows_of(s * HG + h), half(0)],
        lambda s, h: packed[rows_of(s * HG + h), half(1)],
        None if alone else lambda s, h: far_first[0, s * HG + h],
        None if alone else lambda s, h: far_first[1, s * HG + h],
        mats,
        work,
        last,
    )


def numbered(word, n):
    return word + str(n)


def pick(core, a, b):
    return jnp.where(core == 0, a, b)


def spread_vector(core, own, other, row, fields):
    rows = row_ids()
    result = jnp.zeros((8, LANES), F32)
    for f in range(2 * fields):
        value = pick(core, own[row][f], other[row][f]) if f < fields else pick(
            core, other[row][f - fields], own[row][f - fields]
        )
        result = jnp.where(rows == f, value, result)
    return result


def mix_fine(saved_f, shares, pay, fine, sems):
    steps, fields = saved_f.shape[0], saved_f.shape[1]
    copies = [pltpu.make_async_copy(saved_f.at[s], fine.at[s], sems.at[s]) for s in range(steps)]
    for copy in copies:
        copy.start()
    for s in range(steps):
        copies[s].wait()
        total = shares[0] * fine[s, 0]
        for v in range(1, fields):
            total = total + shares[v] * fine[s, v]
        pay[s] = total
        pay[steps + s] = fine[s, 0]


def mix_coarse(saved_c, seed_c, shares, after, payc):
    fields, blocks = saved_c.shape[1], saved_c.shape[2]
    for c in range(saved_c.shape[0]):
        total = shares[0] * saved_c[c, 0]
        for v in range(1, fields):
            total = total + shares[v] * saved_c[c, v]
        payc[0, pl.ds(c * blocks, blocks), :] = total
        payc[1, pl.ds(c * blocks, blocks), :] = saved_c[c, 0]
    for v in range(fields):
        payc[2 + v, pl.ds(0, blocks), :] = seed_c[v]
        payc[2 + v, pl.ds(blocks, blocks), :] = seed_c[v]


def substeps(counts):
    step = HEAT / counts.astype(F32)
    return [jnp.where(n < counts, step, 0.0) for n in range(NSUB)]


def reaction_tables(mix, start, steps):
    state = start
    history = []
    for step in steps:
        inverse = 1.0 / state
        decay = jnp.exp(-ENERGY * inverse)
        rise = step * mix * decay
        history.append((step * decay, rise * (inverse * inverse)))
        state = state + rise
    passed = jnp.ones_like(start)
    weight = jnp.zeros_like(start)
    for grown, slope in reversed(history):
        weight = weight + grown * passed
        passed = passed + passed * (ENERGY * slope)
    return passed - 1.0, weight


def chem_kernel(which, pay, pay_o, fine_counts, pack, after, gain, weight, edges, planes):
    core = lax.axis_index("fld")
    every = pay.shape[0] // 2
    shape = (8, CHEM * LANES)
    rows = lax.broadcasted_iota(jnp.int32, shape, 0)
    counts = jnp.ones(shape, jnp.int32)
    for b in range(fine_counts.shape[0]):
        counts = jnp.where(rows == b, fine_counts[b], counts)
    lengths = substeps(counts)

    def body(t, carry):
        at = pl.ds(pl.multiple_of(t * CHEM * LANES, CHEM * LANES), CHEM * LANES)
        for n, s in enumerate(which):
            start = pick(core, pay[every + s, :, at], pay_o[every + s, :, at])
            a, w = reaction_tables(pay[s, :, at] + pay_o[s, :, at], start, lengths)
            gain[n, :, at] = a
            weight[n, :, at] = w
        return carry

    lax.fori_loop(0, TILES // CHEM, body, 0)
    later = [n for n, s in enumerate(which) if s < every - 1]
    for m, table in enumerate((gain, weight)):
        for order, n in enumerate(later):
            for i in range(0, B, 2):
                for jh in range(2):
                    put_split(
                        planes,
                        rows_of((m * len(later) + order) * HG + i % HG, 2),
                        (i // HG,),
                        jnp.concatenate(
                            [table[n, :, cols(i, jh)], table[n, :, cols(i + 1, jh)]], axis=0
                        ),
                        half(jh),
                        half(2 + jh),
                    )
    edges[...] = pack_faces(planes, pack, edges.shape[0])


def chem_coarse(payc, payc_o, coarse_counts, gain, weight):
    core = lax.axis_index("fld")
    blocks = coarse_counts.shape[0]
    entries = gain.shape[0]
    shape = (entries, 8 * LANES)
    counts = jnp.ones(shape, jnp.int32)
    rows = lax.broadcasted_iota(jnp.int32, shape, 0)
    for r in range(entries):
        counts = jnp.where(rows == r, coarse_counts[r % blocks], counts)
    lengths = substeps(counts)

    def body(t, carry):
        at = pl.ds(pl.multiple_of(t * 8 * LANES, 8 * LANES), 8 * LANES)
        start = pick(core, payc[1, :, at], payc_o[1, :, at])
        gain[:, at], weight[:, at] = reaction_tables(
            payc[0, :, at] + payc_o[0, :, at], start, lengths
        )
        return carry

    lax.fori_loop(0, TILES // 8, body, 0)


def octant_finder(children, count_f):
    me = lax.axis_index("blk")
    devices = lax.axis_size("blk")
    found = []
    for p in range(children.shape[0]):
        for o in range(8):
            child = children[p, o]
            distance = jnp.where(child >= 0, (child // count_f - me) % devices, FAR)
            found.append((distance, child, p * 8 + o))

    def find(want):
        slot = jnp.int32(0)
        label = jnp.int32(-1)
        for distance, child, place in found:
            hit = distance == want
            slot = jnp.where(hit, place, slot)
            label = jnp.where(hit, child % count_f, label)
        return slot, label

    return find


def write_octant(state, first_slab, found, wanted_fields, out, at):
    slot, label = found
    p, a, b, c = slot // 8, slot // 4 % 2, slot // 2 % 2, slot % 2
    kept = lane_ids() % B // H == c
    for n, f in enumerate(wanted_fields):
        layers = state[first_slab + p, b, pl.ds(a * (H * 8) + f, H, stride=8), :]
        out[at + n] = jnp.where(kept, layers, 0.0)
    out[at + len(wanted_fields)] = jnp.full((H, LANES), label.astype(F32))


def slot_fields(core, fields):
    return [core * fields + v for v in range(fields)] + [0]


def keep_coarse(state, first_slab, children):
    upper = lane_ids() % B // H
    for p in range(children.shape[0]):
        for a in range(2):
            for b in range(2):
                low = jnp.where(children[p, 4 * a + 2 * b] < 0, 1.0, 0.0)
                high = jnp.where(children[p, 4 * a + 2 * b + 1] < 0, 1.0, 0.0)
                kept = jnp.where(upper == 0, low, high)
                for i in range(a * H, a * H + H):
                    at = (first_slab + p, b, rows_of(i))
                    state[at] = state[at] * kept


def fill_pack(table):
    cell = lax.broadcasted_iota(jnp.int32, (PLANE, 2 * LANES), 0)
    place = lax.broadcasted_iota(jnp.int32, (PLANE, 2 * LANES), 1)
    depth = place // B % 2
    layer = jnp.where(place < LANES, B - 1 - depth, depth)
    match = jnp.where(cell == place % B * B + layer, 1.0, 0.0)
    group = place % LANES // PACK
    for g in range(G):
        table[g] = jnp.where(group == g, match, 0.0).astype(BF16)


def start_kernel(
    sends, count_f, fields, payc, payc_o, children, coarse_counts, dif, shr, dif_o, shr_o,
    fine_nbr, coarse_nbr, coarse, gain_c, weight_c, local, *rest
):
    core = lax.axis_index("fld")
    count_c = children.shape[0]
    outs, (planes, packed, table, stage) = rest[:-4], rest[-4:]
    fill_pack(table)
    up, down = outs[-2:]
    for p in range(count_c):
        for v in range(fields):
            mine = payc[2 + v, pl.ds(p, 1), :]
            theirs = payc_o[2 + v, pl.ds(p, 1), :]
            stage[p, pl.ds(v, 1), :] = pick(core, mine, theirs)
            stage[p, pl.ds(fields + v, 1), :] = pick(core, theirs, mine)
        for i in range(B):
            for jh in range(2):
                coarse[p, jh, rows_of(i), :] = stage[p, :, cols(i, jh)]
    find = octant_finder(children, count_f)
    for out, distances in zip(outs, sends):
        write_octant(coarse, 0, find(pick(core, *distances)), list(range(2 * fields)), out, 0)
    write_octant(coarse, 0, find(0), slot_fields(core, fields), local, 0)
    chem_coarse(payc, payc_o, coarse_counts, gain_c, weight_c)
    keep_coarse(coarse, 0, children)
    react_coarse(
        coarse,
        0,
        count_c,
        spread_vector(core, (dif, shr), (dif_o, shr_o), 1, fields),
        gain_c,
        weight_c,
        gain_c.shape[0] - count_c,
    )
    build_planes(coarse, count_c, planes)
    packed[...] = pack_faces(planes, table, count_c * HG * 8)
    rows = row_ids()
    lane = lane_ids()
    faces = jnp.zeros((8, LANES), F32)
    for f in range(6):
        column = fine_nbr[:, pl.ds(f, 1)].astype(F32)
        faces = jnp.where(lane == f, jnp.broadcast_to(column, (8, LANES)), faces)
        for p in range(count_c):
            column = coarse_nbr[pl.ds(p, 1), pl.ds(f, 1)].astype(F32)
            faces = jnp.where(
                (lane == 8 + f) & (rows == p), jnp.broadcast_to(column, (8, LANES)), faces
            )
    base = 2 * fields + 1
    for n in range(count_c * HG):
        up[base + n] = packed[rows_of(n), half(0)]
        down[base + n] = packed[rows_of(n), half(1)]
    up[base + count_c * HG] = faces
    down[base + count_c * HG] = faces


def add_octants(entries, state, stage, fields):
    slots = fields + 1
    rows = row_ids()
    lane = lane_ids()
    source = jnp.zeros((8, LANES), jnp.int32)
    for d, tile in enumerate(entries):
        source = jnp.where(tile(None).astype(jnp.int32) == rows, d, source)
        for s in range(slots):
            stage[d // 8, s, pl.ds(d % 8, H, stride=8), :] = tile(s)
    lanes_of = [((H // 2 * jh + lane // B // 2) * B + lane % B // 2) for jh in range(2)]
    groups = (len(entries) + 7) // 8
    indices = []
    for g in range(groups):
        index = source - 8 * g
        indices.append((jnp.clip(index, 0, 7), (index >= 0) & (index < 8)))
    for s in range(slots):
        for i in range(H):
            got = None
            for g in range(groups):
                part = jnp.take_along_axis(
                    stage[g, s, rows_of(i), :], indices[g][0], axis=0, mode="promise_in_bounds"
                )
                part = jnp.where(indices[g][1], part, 0.0)
                got = part if got is None else got + part
            got = 0.125 * (got + roll(got, -H))
            for jh in range(2):
                wide = jnp.take_along_axis(got, lanes_of[jh], axis=1, mode="promise_in_bounds")
                for ii in range(2):
                    at = (s, jh, rows_of(2 * i + ii))
                    state[at] = state[at] + wide


def all_fields(core, fields, ref):
    def tile(s):
        if s is None:
            return ref[2 * fields]
        return ref[0] if s == fields else ref[pl.ds(core * fields + s, 1)][0]

    return tile


def own_slots(fields, ref, at=0):
    return lambda s: ref[at + (fields + 1 if s is None else s)]


def react_fine(state, fields, par, par_o, gain, weight):
    core = lax.axis_index("fld")
    share = [par[1][s] for s in range(fields)] + [pick(core, par[1][0], par_o[1][0])]
    extra = jnp.where(core == 0, 1.0, 0.0)
    for i in range(B):
        for jh in range(2):
            at = cols(i, jh)
            here = (jh, rows_of(i))
            driver = state[(fields,) + here]
            heat = weight[:, at] * driver
            grown = gain[:, at] * driver
            for s in range(fields + 1):
                value = state[(s,) + here] + share[s] * heat
                if s == 0:
                    value = value + extra * grown
                if s == fields:
                    value = value + grown
                state[(s,) + here] = value


def react_coarse(state, first_slab, count_c, shares, gain, weight, first_row):
    own = jnp.where(row_ids() == 0, 1.0, 0.0)
    for p in range(count_c):
        for i in range(B):
            for jh in range(2):
                at = cols(i, jh)
                here = (first_slab + p, jh, rows_of(i))
                value = state[here]
                driver = jnp.broadcast_to(value[0:1], (8, LANES))
                heat = weight[pl.ds(first_row + p, 1), at] * driver
                grown = gain[pl.ds(first_row + p, 1), at] * driver
                state[here] = value + shares * heat + own * grown


def links_maker(plan, faces, shift, fine_slabs):
    me = lax.axis_index("blk") + shift
    count_f, count_c = plan.count_f, plan.count_c

    def column(slab, face):
        return faces[:, face : face + 1].astype(jnp.int32)

    def column_c(slab, face):
        return faces[slab : slab + 1, 8 + face : 9 + face].astype(jnp.int32)

    fine = Links(column, me * count_f, count_f, True, 0)
    coarse = Links(column_c, me * count_c, count_c, False, fine_slabs)
    return lambda s: fine if s < fine_slabs else coarse


def strips_out(plan, r, out, faces, up_octant):
    going = plan.slabs_out
    even = lax.axis_index("blk") % 2 == 0
    build_planes(out, going, r.planes)
    r.packed[pl.ds(0, going * HG * 8), :] = pack_faces(
        r.planes, r.pack, going * HG * 8
    )

    def send(up, down):
        for n in range(going * HG):
            up[n] = r.packed[rows_of(n), half(0)]
            down[n] = r.packed[rows_of(n), half(1)]
        at = going * HG
        up[at] = faces
        down[at] = faces
        if up_octant is not None:
            up_octant(up, at + 1)
            for n in range(plan.fields + 2):
                down[at + 1 + n] = zero_tile()

    pl.when(even)(lambda: send(r.send_e, r.send_o))
    pl.when(jnp.logical_not(even))(lambda: send(r.send_o, r.send_e))


def zero_tile():
    return jnp.zeros((8, LANES), F32)


def open_kernel(plan, names, *refs):
    r = SimpleNamespace(**dict(zip(names, refs)))
    core = lax.axis_index("fld")
    fields = plan.fields
    slots = fields + 1
    count_f, count_c = plan.count_f, plan.count_c
    par, par_o = (r.dif, r.shr), (r.dif_o, r.shr_o)
    out = r.state_out
    base = 2 * fields + 1
    strip = count_c * HG

    last = len(plan.sends) - 1
    strips_at = (last + 1) * (slots + 1)

    def far(ref, order, n):
        return pick(core, ref[base + n], r.shared[strips_at + order * (strip + 1) + n])

    below = [far(getattr(r, numbered("landed", last - 1)), 0, n) for n in range(strip + 1)]
    above = [far(getattr(r, numbered("landed", last)), 1, n) for n in range(strip + 1)]
    own_up, own_down = r.own_up, r.own_down
    faces = own_up[base + strip]
    rates = 0.5 * spread_vector(core, par, par_o, 0, fields)

    def finish(p, i, jh, value):
        out[slots + p, jh, rows_of(i), :] = value

    diffuse(
        r.coarse,
        count_c,
        links_maker(plan, faces, 0, 0),
        links_maker(plan, below[strip], -1, 0),
        links_maker(plan, above[strip], 1, 0),
        lambda s: rates,
        lambda s, h: own_up[base + s * HG + h],
        lambda s, h: own_down[base + s * HG + h],
        lambda s, h: below[s * HG + h],
        lambda s, h: above[s * HG + h],
        r,
        r,
        finish,
    )
    find = octant_finder(r.children, count_f)
    for n, distances in enumerate(plan.later):
        write_octant(
            out, slots, find(pick(core, *distances)), list(range(2 * fields)), getattr(r, numbered("octant", n)), 0
        )
    mine = slot_fields(core, fields)
    write_octant(out, slots, find(0), mine, r.local_out, 0)
    near_octant = r.near_octant
    write_octant(out, slots, find(1), mine, near_octant, 0)
    keep_coarse(out, slots, r.children)
    react_coarse(
        out, slots, count_c, spread_vector(core, par, par_o, 1, fields), r.gain_c, r.weight_c, 0
    )
    for i in range(B):
        for jh in range(2):
            at = cols(i, jh)
            for s in range(fields):
                out[s, jh, rows_of(i), :] = r.seed_f[s, :, at]
            out[fields, jh, rows_of(i), :] = pick(core, r.seed_f[0, :, at], r.seed_other[0, :, at])
    entries = [own_slots(fields, r.local)]
    for n in range(last):
        entries.append(all_fields(core, fields, getattr(r, numbered("landed", n))))
        entries.append(own_slots(fields, r.shared, n * (slots + 1)))
    one = all_fields(core, fields, getattr(r, numbered("landed", last)))
    two = own_slots(fields, r.shared, last * (slots + 1))
    entries.append(lambda s: pick(core, two(s), one(s)))
    add_octants(entries, out, r.stage, fields)
    react_fine(out, fields, par, par_o, r.gain.at[plan.step], r.weight.at[plan.step])

    def up_octant(up, at):
        for n in range(slots + 1):
            up[at + n] = near_octant[n]

    strips_out(plan, r, out, faces, up_octant)


def rates_of(plan, r):
    core = lax.axis_index("fld")
    par, par_o = (r.dif, r.shr), (r.dif_o, r.shr_o)
    fields = plan.fields
    rates = [par[0][s] for s in range(fields)] + [pick(core, par[0][0], par_o[0][0])]
    return rates + [0.5 * spread_vector(core, par, par_o, 0, fields)] * plan.count_c


def by_parity(action, r):
    even = lax.axis_index("blk") % 2 == 0
    pl.when(even)(lambda: action(r.sent_e, r.sent_o, r.got_o, r.got_e))
    pl.when(jnp.logical_not(even))(lambda: action(r.sent_o, r.sent_e, r.got_e, r.got_o))


def react_bulk(plan, r, out):
    slots = plan.fields + 1
    par, par_o = (r.dif, r.shr), (r.dif_o, r.shr_o)
    react_fine(out, plan.fields, par, par_o, r.gain.at[plan.step], r.weight.at[plan.step])
    build_planes(out, slots, r.planes)
    r.faces_out[...] = pack_faces(r.planes, r.pack, slots * HG * 8)


def bulk_kernel(plan, names, *refs):
    r = SimpleNamespace(**dict(zip(names, refs)))
    core = lax.axis_index("fld")
    fields = plan.fields
    slots = fields + 1
    count_c = plan.count_c
    par, par_o = (r.dif, r.shr), (r.dif_o, r.shr_o)
    slabs, arrived = plan.slabs, plan.slabs_in
    own_up, own_down = r.own_up, r.own_down

    def sort_strips(up, down, below, above):
        for n in range(arrived * HG + 1):
            own_up[n] = up[n]
            own_down[n] = down[n]

    even = lax.axis_index("blk") % 2 == 0
    pl.when(even)(lambda: sort_strips(r.sent_e, r.sent_o, None, None))
    pl.when(jnp.logical_not(even))(lambda: sort_strips(r.sent_o, r.sent_e, None, None))
    faces = own_up[arrived * HG]
    source, out = r.state, r.state_out
    if plan.late:
        late = plan.late * HG * 8
        high, low = split(r.late[pl.ds(0, late), :])
        r.ends[pl.ds(0, late), pl.ds(0, 2 * LANES)] = high
        r.ends[pl.ds(0, late), pl.ds(2 * LANES, 2 * LANES)] = low
        place_ends(r.ends, r.placed, late, r)
        source = r.whole
        for i in range(B):
            for jh in range(2):
                for s in range(slabs):
                    source[s, jh, rows_of(i), :] = r.state[s, jh, rows_of(i), :] + placed_tile(
                        r.placed, s, i, jh
                    )

    def finish(s, i, jh, value):
        if s >= slots:
            r.coarse_out[s - slots, jh, rows_of(i), :] = value
        else:
            out[s, jh, rows_of(i), :] = value

    rates = rates_of(plan, r)
    diffuse(
        source,
        slabs,
        links_maker(plan, faces, 0, slots),
        None,
        None,
        lambda s: rates[s],
        lambda s, h: own_up[s * HG + h],
        lambda s, h: own_down[s * HG + h],
        None,
        None,
        r,
        r,
        finish,
    )
    if not plan.final and not plan.pause:
        react_bulk(plan, r, out)


def coarse_kernel(plan, names, *refs):
    r = SimpleNamespace(**dict(zip(names, refs)))
    core = lax.axis_index("fld")
    fields, count_c = plan.fields, plan.count_c
    high, low = split(r.late[pl.ds((fields + 1) * HG * 8, count_c * HG * 8), :])
    r.ends[:, pl.ds(0, 2 * LANES)] = high
    r.ends[:, pl.ds(2 * LANES, 2 * LANES)] = low
    place_ends(r.ends, r.placed, count_c * HG * 8, r)
    for p in range(count_c):
        for i in range(B):
            for jh in range(2):
                r.coarse_stage[p, :, cols(i, jh)] = r.coarse[p, jh, rows_of(i), :] + placed_tile(
                    r.placed, p, i, jh
                )
        for v in range(fields):
            r.coarse_final[v, pl.ds(p, 1), :] = pick(
                core,
                r.coarse_stage[p, pl.ds(v, 1), :],
                r.coarse_stage[p, pl.ds(fields + v, 1), :],
            )


def share_kernel(plan, names, *refs):
    r = SimpleNamespace(**dict(zip(names, refs)))
    slots = plan.fields + 1
    for n in range(plan.pieces):
        ref = getattr(r, numbered("landed", n))
        tile = all_fields(1 - lax.axis_index("fld"), plan.fields, ref)
        for s in range(slots):
            r.shared[n * (slots + 1) + s] = tile(s)
        r.shared[n * (slots + 1) + slots] = tile(None)
    at = plan.pieces * (slots + 1)
    for n in range(plan.pieces - 2, plan.pieces) if plan.strips else ():
        ref = getattr(r, numbered("landed", n))
        for m in range(plan.strips):
            r.shared[at + m] = ref[2 * plan.fields + 1 + m]
        at += plan.strips


def resume_kernel(plan, names, *refs):
    r = SimpleNamespace(**dict(zip(names, refs)))
    core = lax.axis_index("fld")
    even = lax.axis_index("blk") % 2 == 0
    fields = plan.fields
    slots = fields + 1
    out = r.state_out
    out[...] = r.state[...]
    near = r.near_octant

    def take(ref):
        for n in range(slots + 1):
            near[n] = ref[plan.near_at + n]

    pl.when(even)(lambda: take(r.near_o))
    pl.when(jnp.logical_not(even))(lambda: take(r.near_e))
    entries = [own_slots(fields, r.local), own_slots(fields, near)]
    for n in range(len(plan.later)):
        entries.append(all_fields(core, fields, getattr(r, numbered("landed", n))))
        entries.append(own_slots(fields, r.shared, n * (slots + 1)))
    add_octants(entries, out, r.stage, fields)
    react_bulk(plan, r, out)


def edge_kernel(plan, names, *refs):
    sems = refs[-1]
    r = SimpleNamespace(**dict(zip(names, refs)))
    core = lax.axis_index("fld")
    fields = plan.fields
    slots = fields + 1
    par, par_o = (r.dif, r.shr), (r.dif_o, r.shr_o)
    slabs, arrived = plan.slabs, plan.slabs_in
    own_up, own_down, far_b, far_a = r.own_up, r.own_down, r.far_b, r.far_a

    def sort_strips(up, down, below, above):
        for n in range(arrived * HG + 1):
            own_up[n] = up[n]
            own_down[n] = down[n]
            far_b[n] = below[n]
            far_a[n] = above[n]

    by_parity(sort_strips, r)
    faces = own_up[arrived * HG]
    rates = rates_of(plan, r)
    near = links_maker(plan, faces, 0, slots)
    from_below = links_maker(plan, far_b[arrived * HG], -1, slots)
    from_above = links_maker(plan, far_a[arrived * HG], 1, slots)
    outer = outer_lanes()
    delta, far_first, lateral, late = r.delta, r.far_first, r.lateral, r.late

    def at_tile(ref):
        return lambda s, h: ref[s * HG + h]

    for s in range(slabs):
        for h in range(HG):
            for n, (name, ref) in enumerate((((5, 1), far_a), ((4, -1), far_b))):
                ghost = near(s).read(name, s, lambda q, ref=ref: ref[q * HG + h])
                delta[n, s * HG + h] = jnp.where(outer, rates[s] * ghost, 0.0)

    def keep_far(n, s, h, lap):
        far_first[n, s * HG + h] = rates[s] * lap

    def keep_lateral(n, s, h, lap):
        lateral[n, s * HG + h] = lap

    laplace_far(
        slabs,
        (
            (from_below, at_tile(far_b), at_tile(own_down), (5, 1)),
            (from_above, at_tile(far_a), at_tile(own_up), (4, -1)),
        ),
        r,
        r,
        keep_far,
    )
    laplace_far(
        slabs,
        ((near, at_tile(delta.at[0]), None, None), (near, at_tile(delta.at[1]), None, None)),
        r,
        SimpleNamespace(far_lhs=r.far_lhs2, far_out=r.far_out2),
        keep_lateral,
    )
    share = [par[1][s] for s in range(fields)] + [pick(core, par[1][0], par_o[1][0])]
    extra = jnp.where(core == 0, 1.0, 0.0)
    for n, (name, other) in enumerate((((5, 1), 1), ((4, -1), 0))):
        for h in range(HG):
            added = []
            for s in range(slabs):
                at = s * HG + h
                ghost = near(s).read(name, s, lambda q: far_first[other, q * HG + h])
                value = delta[n, at]
                more = 0.5 * rates[s]
                inner = more * roll(value, B)
                value = value + more * (lateral[n, at] + ghost)
                added.append(jnp.where(outer, value, inner))
            if not plan.final:
                gain = r.edges[rows_of(plan.step * HG + h), half(n)]
                weight = r.edges[rows_of((plan.packed + plan.step) * HG + h), half(n)]
                driver = added[fields]
                heat, grown = weight * driver, gain * driver
                for s in range(slots):
                    added[s] = added[s] + share[s] * heat
                added[0] = added[0] + extra * grown
                added[fields] = added[fields] + grown
            for s in range(slabs):
                late[rows_of(s * HG + h), half(n)] = added[s]
    if plan.final:
        high, low = split(late[...])
        r.ends[:, pl.ds(0, 2 * LANES)] = high
        r.ends[:, pl.ds(2 * LANES, 2 * LANES)] = low
        place_ends(r.ends, r.placed, slabs * HG * 8, r)
        copies = []
        for s in range(slabs):
            for i in range(B):
                for jh in range(2):
                    r.result[s, :, cols(i, jh)] = r.state[s, jh, rows_of(i), :] + placed_tile(
                        r.placed, s, i, jh
                    )
            copies.append(pltpu.make_async_copy(r.result.at[s], r.state_out.at[s], sems.at[s]))
            copies[s].start()
        for copy in copies:
            copy.wait()
        return

    def send(up, down):
        for n in range(slots * HG):
            up[n] = r.faces_in[rows_of(n), half(0)] + late[rows_of(n), half(0)]
            down[n] = r.faces_in[rows_of(n), half(1)] + late[rows_of(n), half(1)]
        up[slots * HG] = faces
        down[slots * HG] = faces

    even = lax.axis_index("blk") % 2 == 0
    pl.when(even)(lambda: send(r.send_e, r.send_o))
    pl.when(jnp.logical_not(even))(lambda: send(r.send_o, r.send_e))


SCALARS = ("dif", "shr", "dif_o", "shr_o", "children", "fine_counts", "coarse_counts")
MATS = ("plane", "side", "place", "pack", "far")
MIB = 1024 * 1024
LIMIT = 52


def call(kernel, inputs, outputs, scratch, hbm=(), sems=(), limit=None, cost=1000):
    names = list(inputs) + list(outputs) + list(scratch)
    scratch = {
        name: value if value[-1] is BF16 else value + (F32,) for name, value in scratch.items()
    }
    size = sum(4 * np.prod(v.shape) for name, v in inputs.items() if name not in hbm)
    size += sum(4 * np.prod(v) for v in outputs.values())
    size += sum(4 * np.prod(v[:-1]) for v in scratch.values())

    def spec(name):
        if name in hbm:
            return HBM
        return SMEM if name in SCALARS else VMEM

    result = pl.pallas_call(
        functools.partial(kernel, names),
        out_shape=[jax.ShapeDtypeStruct(shape, F32) for shape in outputs.values()],
        in_specs=[spec(name) for name in inputs],
        out_specs=[spec(name) for name in outputs],
        scratch_shapes=[pltpu.VMEM(value[:-1], value[-1]) for value in scratch.values()]
        + [pltpu.SemaphoreType.DMA(shape) for shape in sems],
        compiler_params=pltpu.CompilerParams(vmem_limit_bytes=limit or int(size) + 12 * MIB),
        cost_estimate=pl.CostEstimate(flops=cost, bytes_accessed=cost, transcendentals=0),
    )(*inputs.values())
    return SimpleNamespace(**dict(zip(outputs, result)))


def shards(
    seed_fine,
    seed_coarse,
    saved_fine,
    saved_coarse,
    diffusion,
    species_shares,
    fine_nbr,
    coarse_nbr,
    children,
    fine_counts,
    coarse_counts,
):
    fields, count_f, cells = seed_fine.shape
    count_c = seed_coarse.shape[1]
    steps = saved_fine.shape[0]
    cycles = saved_coarse.shape[0]
    slots = fields + 1
    every = slots + count_c
    sends, later = first_sends(count_f), later_sends(count_f)
    mats = tables()
    octant_shape = (2 * fields + 1, H, LANES)
    slots_shape = (slots + 1, H, LANES)
    loaded_shape = (2 * fields + 1 + count_c * HG + 1, 8, LANES)

    def plain(kernel, *fixed):
        return lambda names, *refs: kernel(*fixed, *refs)

    def strip(slabs, more=0):
        return (slabs * HG + 1 + more, 8, LANES)

    def state_shape(slabs):
        return (slabs, 2, 8 * B, LANES)

    def work(slabs):
        rows = slabs * HG * 8
        return dict(
            first=state_shape(slabs),
            far_first=(2, slabs * HG, 8, LANES),
            sums=(G, rows, PLANE),
            ends=(rows, 4 * LANES, BF16),
            placed=(rows, G * PLANE),
            far_lhs=(2 * rows, 4 * LANES, BF16),
            far_out=(2 * rows, LANES),
        )

    def strip_work(slabs):
        return {name: strip(slabs) for name in ("far_b", "far_a", "own_up", "own_down")}

    def pack_work(slabs):
        rows = slabs * HG * 8
        return dict(
            planes=(G, rows, 2 * PLANE + 2 * LANES, BF16),
            packed=(rows, 2 * LANES),
        )

    def after(value, *before):
        return lax.optimization_barrier((value, before))[0]

    stage_work = dict(stage=(1, slots, 8 * H, LANES))
    dif_o, shr_o = core_swap(diffusion), core_swap(species_shares)
    pay = call(
        plain(mix_fine),
        dict(saved_f=saved_fine, shr=species_shares),
        dict(pay=(2 * steps, count_f, cells)),
        dict(fine=saved_fine.shape),
        hbm=("saved_f",),
        sems=((steps,),),
        limit=LIMIT * MIB,
    ).pay
    payc = call(
        plain(mix_coarse),
        dict(saved_c=saved_coarse, seed_c=seed_coarse, shr=species_shares, after=pay),
        dict(payc=(2 + fields, cycles * count_c, cells)),
        {},
        hbm=("after",),
    ).payc
    payc_o = core_swap(payc)
    pay, sown, payc_o, dif_o, shr_o = lax.optimization_barrier(
        (pay, seed_fine, payc_o, dif_o, shr_o)
    )
    par = dict(dif=diffusion, shr=species_shares, dif_o=dif_o, shr_o=shr_o)
    pay_o, seed_o = core_swap(pay), core_swap(sown)

    loaded = [numbered("octant", n) for n in range(len(sends) - 2)] + ["up", "down"]
    started = call(
        plain(start_kernel, sends, count_f, fields),
        dict(
            payc=payc,
            payc_o=payc_o,
            children=children,
            coarse_counts=coarse_counts,
            **par,
            fine_nbr=fine_nbr,
            coarse_nbr=coarse_nbr,
        ),
        dict(
            coarse=state_shape(count_c),
            gain_c=(cycles * count_c, cells),
            weight_c=(cycles * count_c, cells),
            local=slots_shape,
            **{name: loaded_shape if name in ("up", "down") else octant_shape for name in loaded},
        ),
        dict(
            pack_work(count_c),
            table=(G, PLANE, 2 * LANES, BF16),
            coarse_stage=(count_c, 2 * fields, cells),
        ),
    )
    landed = [octant_move(getattr(started, name), d) for name, d in zip(loaded, sends)]
    def chem_of(which, before):
        packed = 2 * sum(step < steps - 1 for step in which)
        return call(
            plain(chem_kernel, which),
            dict(pay=pay, pay_o=pay_o, fine_counts=fine_counts, pack=mats.pack, after=before),
            dict(
                gain=(len(which), count_f, cells),
                weight=(len(which), count_f, cells),
                edges=(packed * HG * 8, 2 * LANES),
            ),
            dict(planes=pack_work(packed)["planes"]),
            hbm=("after",),
        )

    chem = chem_of(tuple(range(steps)), payc)
    landed, (chem.gain, chem.weight, chem.edges) = lax.optimization_barrier(
        (landed, (chem.gain, chem.weight, chem.edges))
    )

    def named(word, values):
        return {numbered(word, n): value for n, value in enumerate(values)}

    plan = dict(
        fields=fields,
        count_f=count_f,
        count_c=count_c,
        sends=sends,
        later=later,
        slabs_in=every,
        slabs=every,
        slabs_out=slots,
        final=False,
        add=False,
        near_at=every * HG + 1,
        late=0,
        pause=False,
        packed=0,
    )

    def run(kernel, changes, inputs, outputs, scratch, **more):
        return call(
            functools.partial(kernel, SimpleNamespace(**{**plan, **changes})),
            dict(par, **vars(mats), **inputs),
            outputs,
            scratch,
            **more,
        )

    def halo(made, ring=False):
        got_o = pair_swap(made.send_o, 1, ring)
        got_e = pair_swap(made.send_e, 0, ring)
        return dict(sent_o=made.send_o, got_o=got_o, sent_e=made.send_e, got_e=got_e)

    def sending(slabs, more=0):
        return dict(
            state_out=state_shape(slabs), send_e=strip(slabs, more), send_o=strip(slabs, more)
        )

    def share(landed, before, strips):
        tiles = len(landed) * (slots + 1) + 2 * strips
        part = run(
            share_kernel,
            dict(pieces=len(landed), strips=strips),
            dict(named("landed", landed), after=before),
            dict(shared=(tiles, 8, LANES)),
            {},
            hbm=("after",),
        )
        return core_swap(part.shared)

    made = run(
        open_kernel,
        dict(slabs_out=every, step=steps - 1),
        dict(
            gain=chem.gain,
            weight=chem.weight,
            gain_c=started.gain_c,
            weight_c=started.weight_c,
            children=children,
            coarse=started.coarse,
            own_up=started.up,
            own_down=started.down,
            seed_f=seed_fine,
            seed_other=seed_o,
            local=started.local,
            **named("landed", landed),
            shared=share(landed, chem.edges, count_c * HG + 1),
        ),
        dict(
            sending(every, slots + 1),
            local_out=slots_shape,
            **named("octant", [octant_shape] * len(later)),
        ),
        dict(work(count_c), **pack_work(every), **stage_work, near_octant=slots_shape),
    )
    first_halo = halo(made, True)
    landed = [octant_move(getattr(made, numbered("octant", n)), d) for n, d in enumerate(later)]
    arrived_halo = first_halo

    def edge_work(slabs):
        rows = slabs * HG * 8
        packed = (2, slabs * HG, 8, LANES)
        return dict(
            delta=packed,
            far_first=packed,
            lateral=packed,
            far_lhs=(2 * rows, 4 * LANES, BF16),
            far_out=(2 * rows, LANES),
            far_lhs2=(2 * rows, 4 * LANES, BF16),
            far_out2=(2 * rows, LANES),
        )

    def place_work(slabs):
        rows = slabs * HG * 8
        return dict(ends=(rows, 4 * LANES, BF16), placed=(rows, G * PLANE))

    def own_strips(slabs):
        return dict(own_up=strip(slabs), own_down=strip(slabs))

    state, flown, held = made.state_out, arrived_halo, every
    local = made.local_out
    sent = dict(sent_e=made.send_e, sent_o=made.send_o)
    late, coarse, coarse_final = None, None, None
    for step in reversed(range(-1, steps - 1)):
        final = step < 0
        slabs = fields if final else held
        changes = dict(step=step, packed=steps - 1)
        changes.update(slabs_in=held, slabs=slabs, final=final)
        inputs = dict(state=state, **sent)
        outputs = dict(state_out=state_shape(min(slabs, slots)))
        scratch = dict(work(slabs), **own_strips(held), **pack_work(slabs))
        if not final:
            inputs.update(gain=chem.gain, weight=chem.weight)
            outputs.update(faces_out=(slots * HG * 8, 2 * LANES))
        if held > slots:
            outputs.update(coarse_out=state_shape(count_c))
        if late is not None:
            inputs.update(late=late)
            scratch.update(whole=state_shape(slabs), **place_work(slabs))
            changes.update(late=slabs)
        paused = step == steps - 3
        if paused:
            for name in ("gain", "weight"):
                inputs.pop(name)
            outputs.pop("faces_out")
            changes.update(pause=True)
        bulk = run(bulk_kernel, changes, inputs, outputs, scratch)
        if paused:
            whole = run(
                resume_kernel,
                changes,
                dict(
                    state=bulk.state_out,
                    gain=chem.gain,
                    weight=chem.weight,
                    near_e=arrived_halo["got_e"],
                    near_o=arrived_halo["got_o"],
                    local=local,
                    shared=shared,
                    **named("landed", landed),
                ),
                dict(state_out=state_shape(slots), faces_out=(slots * HG * 8, 2 * LANES)),
                dict(pack_work(slots), **stage_work, near_octant=slots_shape),
            )
            bulk.state_out, bulk.faces_out = whole.state_out, whole.faces_out
        if held > slots:
            coarse = bulk.coarse_out
        inputs = dict(flown)
        scratch = dict(edge_work(slabs), **strip_work(held))
        if final:
            inputs.update(state=bulk.state_out)
            outputs = dict(state_out=seed_fine.shape)
            scratch.update(
                late=(slabs * HG * 8, 2 * LANES), result=seed_fine.shape, **place_work(slabs)
            )
        else:
            inputs.update(edges=chem.edges, faces_in=bulk.faces_out)
            outputs = dict(
                late=(slabs * HG * 8, 2 * LANES), send_e=strip(slots), send_o=strip(slots)
            )
        more = dict(hbm=("state_out",), sems=((fields,),)) if final else {}
        made = run(edge_kernel, changes, inputs, outputs, scratch, **more)
        if step == steps - 2:
            first_late = made.late
            shared = share(landed, first_late, 0)
        if final:
            break
        state, late, held = bulk.state_out, made.late, slots
        if step == 0:
            coarse_final = run(
                coarse_kernel,
                dict(),
                dict(coarse=coarse, late=first_late, after=late),
                dict(coarse_final=seed_coarse.shape),
                dict(place_work(count_c), coarse_stage=(count_c, 2 * fields, cells)),
                hbm=("after",),
            ).coarse_final
        flown = halo(made)
        sent = dict(sent_e=made.send_e, sent_o=made.send_o)
    return made.state_out, coarse_final


def solution(mesh):
    return jax.shard_map(
        shards,
        mesh=mesh,
        in_specs=(
            P("fld", "blk", None),
            P("fld", "blk", None),
            P(None, "fld", "blk", None),
            P(None, "fld", "blk", None),
            P("fld"),
            P("fld"),
            P("blk", None),
            P("blk", None),
            P("blk", None),
            P("blk"),
            P("blk"),
        ),
        out_specs=(P("fld", "blk", None), P("fld", "blk", None)),
        check_vma=False,
    )
```
